512 devices in a mesh: cap: 4 (over z_lo), clip: 32 (over z_hi, y, core), frame: 4 (over x).
Axes of the slice: x: 4, y: 8, z: 8 (z_hi: 2, z_lo: 4; z = z_hi * 4 + z_lo), core: 2. Of those that a mesh axis runs over, the one named last changes fastest.
Arguments:
- cap_tokens: float32 [32, 32, 512], P('cap', 'clip')
- clip_tokens: float32 [32, 16, 50, 512], P('clip', 'frame')
- win_frame: int32 [32, 32, 32], P('cap', None, 'clip'), may hold values from 0 to 15
- win_patch: int32 [32, 32, 32], P('cap', None, 'clip'), may hold values from 0 to 49
- cap_lengths: int32 [32], P('cap'), may hold values from 8 to 32
Outputs:
- loss: float32 [], replicated
- cap_grad: float32 [32, 32, 512], P('cap', 'clip')
- clip_grad: float32 [32, 16, 50, 512], P('clip', 'frame', None, 'cap')
The draws below stay inside these ranges and needn't reach their ends.
All inputs are finite; a program needn't handle non-finite values.
Results may differ from the reference program's by a relative error of at most 0.00009.
Values sent between devices are 32-bit elements; how exact they have to be, the bound alone decides.
A program may use at most 64 MiB of HBM per device.

```python
import jax
import jax.numpy as jnp
from jax import lax

E = 512
PATCH = 50
FRAMES = 16
LT = 32
CLIPS = 32
CAPTIONS = 32


def spread_scale(key, shape):
    return 10.0 ** jax.random.uniform(key, shape, jnp.float32, 0.0, 1.0)


def draw_cap_tokens(key, part):
    key = jax.random.fold_in(key, 11)
    first, second, third = jax.random.split(key, 3)
    shape = (CAPTIONS, LT, E)
    values = jax.random.normal(first, shape, jnp.float32)
    return values * spread_scale(second, (CAPTIONS, LT, 1)) * spread_scale(third, (E,)) * 0.0003


def draw_clip_tokens(key, part):
    key = jax.random.fold_in(key, 17)
    first, second, third = jax.random.split(key, 3)
    shape = (CLIPS, FRAMES, PATCH, E)
    values = jax.random.normal(first, shape, jnp.float32)
    return values * spread_scale(second, (CLIPS, FRAMES, PATCH, 1)) * spread_scale(third, (E,)) * 0.0003


def draw_cap_lengths(key, part):
    key = jax.random.fold_in(key, 23)
    first, second = jax.random.split(key, 2)
    lowest = max(2, LT // 4)
    values = jax.random.randint(first, (CAPTIONS,), lowest, LT + 1, jnp.int32)
    shuffled = jax.random.permutation(second, CAPTIONS)
    values = values.at[shuffled[0]].set(LT)
    values = values.at[shuffled[1]].set(lowest)
    return values


def touch_ends(entries, rng, smallest, top_value):
    shape = entries.shape
    place = [jax.random.randint(jax.random.fold_in(rng, axis), (), 0, shape[axis]) for axis in range(len(shape))]
    entries = entries.at[tuple(place)].set(smallest)
    longest = shape.index(max(shape))
    place[longest] = (place[longest] + 1) % shape[longest]
    return entries.at[tuple(place)].set(top_value)


def setup_inputs(seed: int = 0) -> dict:
    key_of = jax.random.split(jax.random.key(seed), 6)
    return {
        "cap_tokens": draw_cap_tokens(jax.random.fold_in(key_of[5], 71), 0),
        "clip_tokens": draw_clip_tokens(jax.random.fold_in(key_of[5], 71), 0),
        "win_frame": touch_ends(jax.random.randint(key_of[2], (CAPTIONS, LT, CLIPS), 0, FRAMES), jax.random.fold_in(key_of[2], 1), 0, FRAMES - 1).astype(jnp.int32),
        "win_patch": touch_ends(jax.random.randint(key_of[3], (CAPTIONS, LT, CLIPS), 0, PATCH), jax.random.fold_in(key_of[3], 1), 0, PATCH - 1).astype(jnp.int32),
        "cap_lengths": draw_cap_lengths(jax.random.fold_in(key_of[5], 71), 0),
    }


logit_scale = 1.0 / 0.07
norm_eps = 1e-06

def unit_rows(values):
    inverse = lax.rsqrt(lax.optimization_barrier(jnp.sum(values * values, axis=-1, keepdims=True)) + norm_eps)
    return values * inverse

def total_loss(cap_tokens, clip_tokens, win_frame, win_patch, cap_lengths):
    cap_unit = unit_rows(cap_tokens)
    key_rows = unit_rows(clip_tokens).reshape(CLIPS, FRAMES * PATCH, E)
    winner = (win_frame * PATCH + win_patch).astype(jnp.int32)
    clip_ids = jnp.arange(CLIPS, dtype=jnp.int32)[None, :]

    def one_caption(caption_item):
        queries, chosen = caption_item
        picked_keys = key_rows[clip_ids, chosen]
        return jnp.einsum('te,tve->tv', queries, picked_keys, precision=lax.Precision.HIGHEST)
    picked = lax.map(one_caption, (cap_unit, winner))
    live_mask = (jnp.arange(LT, dtype=jnp.int32)[None, :] < cap_lengths[:, None]).astype(jnp.float32)
    scores = lax.optimization_barrier(jnp.sum(live_mask[:, :, None] * picked, axis=1)) / cap_lengths[:, None].astype(jnp.float32)
    logits = logit_scale * scores
    row_lse = jnp.log(lax.optimization_barrier(jnp.sum(jnp.exp(logits), axis=1)))
    col_lse = jnp.log(lax.optimization_barrier(jnp.sum(jnp.exp(logits), axis=0)))
    return 0.5 * (jnp.sum(row_lse) + jnp.sum(col_lse) - 2.0 * jnp.trace(logits))

def reference(cap_tokens, clip_tokens, win_frame, win_patch, cap_lengths):

    def wrapped(first, second):
        return total_loss(first, second, win_frame, win_patch, cap_lengths)
    total, backward = jax.vjp(wrapped, cap_tokens, clip_tokens)
    cap_grad, clip_grad = backward(jnp.ones_like(total))
    return (total / CAPTIONS, cap_grad, clip_grad)
```

```python
import functools

import jax
import jax.numpy as jnp
from jax import lax
from jax.experimental import pallas as pl
from jax.experimental.pallas import tpu as pltpu
from jax.sharding import PartitionSpec as P

MESH = pl.DeviceIdType.MESH
logit_scale = 1.0 / 0.07
norm_eps = 1e-06
f32 = jnp.float32
bf16 = jnp.bfloat16
LANES = 128
SUB = 8


def iota(shape, dim):
    return lax.broadcasted_iota(jnp.int32, shape, dim)


def two_terms(x):
    high = x.astype(bf16)
    return high, (x - high.astype(f32)).astype(bf16)


def three_terms(x):
    high = x.astype(bf16).astype(f32)
    rest = x - high
    middle = rest.astype(bf16).astype(f32)
    return high, middle, rest - middle


def dot(a, b):
    return jnp.dot(a, b, preferred_element_type=f32)


def times_exact(tile, table):
    high, middle, low = three_terms(tile)
    stacked = jnp.concatenate([high, middle, low, jnp.zeros_like(high)], axis=0).astype(bf16)
    out = dot(stacked, table)
    return out[0:SUB] + out[SUB : 2 * SUB] + out[2 * SUB : 3 * SUB]


def kernel(
    nc, nv, patches,
    cap_ref, clip_ref, wf_ref, wp_ref, len_ref,
    loss_ref, cap_out, clip_out,
    cap_raw, clip_raw, wf_raw, wp_raw, qn, give, trade, q_full, keys, key_inv, key_cat, column, picked_rows,
    rows_in, tiles_in, logits_in, tile_out, grads_in, grad_out, one_hot, cap_res, clip_res,
    load_sem, store_sem, trade_send, trade_recv, key_send, key_recv, gather_send, gather_recv, spread_send,
    spread_recv, rows_send, rows_recv, tile_send, tile_recv, logit_send, logit_recv, grad_send, grad_recv,
):
    nf = nc
    tok = nv
    me_c, me_v, me_f = lax.axis_index("cap"), lax.axis_index("clip"), lax.axis_index("frame")
    rows = 4 * patches
    all_rows = nf * rows
    per_block = tok * SUB
    all_tokens = nf * per_block

    loads = [
        pltpu.make_async_copy(clip_ref, clip_raw, load_sem.at[0]),
        pltpu.make_async_copy(cap_ref, cap_raw, load_sem.at[1]),
        pltpu.make_async_copy(wf_ref, wf_raw, load_sem.at[2]),
        pltpu.make_async_copy(wp_ref, wp_raw, load_sem.at[3]),
    ]
    for load in loads:
        load.start()

    barrier = pltpu.get_barrier_semaphore()

    def device(dc, dv, df):
        return {
            "cap": lax.rem(me_c + dc, nc),
            "clip": lax.rem(me_v + dv, nv),
            "frame": lax.rem(me_f + df, nf),
        }

    def signal(dc, dv, df):
        pl.semaphore_signal(barrier, inc=1, device_id=device(dc, dv, df), device_id_type=MESH)

    @pl.loop(1, nc * nf)
    def _(step):
        signal(step // nf, 0, lax.rem(step, nf))

    @pl.loop(1, nv)
    def _(step):
        signal(0, step, 0)

    lane = iota((SUB, LANES), 1)
    sub = iota((SUB, LANES), 0)
    group = lane // tok
    slot_in_group = lax.rem(lane, tok)

    loads[1].wait()
    raw = [cap_raw[pl.ds(j, SUB, stride=nc), :] for j in range(nc)]
    total = raw[0] * raw[0]
    for j in range(1, nc):
        total = total + raw[j] * raw[j]
    cap_inv = lax.rsqrt(jnp.sum(total, axis=1, keepdims=True) + norm_eps)
    loads[2].wait()
    loads[3].wait()
    lengths = jnp.zeros((SUB, LANES), f32)
    for c in range(SUB):
        lengths = jnp.where(sub == c, len_ref[c].astype(f32), lengths)
    frame_own = wf_raw[...].astype(f32)
    patch_own = wp_raw[...].astype(f32)
    give[:, 2 * SUB : 3 * SUB, :] = jnp.zeros((nc, SUB, LANES), f32)
    give[:, SUB : 2 * SUB, :] = jnp.zeros((nc, SUB, LANES), f32)
    for j in range(nc):
        unit = raw[j] * cap_inv
        qn[j] = unit
        give[j, 0:SUB, :] = unit
        give[j, SUB : 2 * SUB, 0:tok] = frame_own
        give[j, 2 * SUB : 3 * SUB, 0:tok] = patch_own
        give[j, 3 * SUB : 4 * SUB, :] = lengths

    loads[0].wait()
    whole = clip_raw[...].reshape(patches, nc // 2, SUB, LANES)
    square = whole * whole
    summed = square[:, 0]
    for j in range(1, nc // 2):
        summed = summed + square[:, j]
    summed = summed + pltpu.roll(summed, 4, 1)
    inverse = lax.rsqrt(jnp.sum(summed, axis=2, keepdims=True) + norm_eps)
    half = clip_raw[:, pl.ds(pl.multiple_of((me_c // 2) * SUB, SUB), SUB), :]
    unit = (half * inverse).reshape(patches // 2, 2, SUB, LANES)
    first, second = unit[:, 0], unit[:, 1]
    low_half = iota((patches // 2, SUB, LANES), 1) < 4
    odd = lax.rem(me_c, 2) == 1
    even_slice = jnp.where(low_half, first, pltpu.roll(second, 4, 1))
    odd_slice = jnp.where(low_half, pltpu.roll(first, 4, 1), second)
    keys[pl.ds(pl.multiple_of(me_f * rows, SUB), rows), :] = jnp.where(odd, odd_slice, even_slice).reshape(rows, LANES)
    inverse = jnp.broadcast_to(inverse, (patches, SUB, LANES)).reshape(patches // 2, 2, SUB, LANES)
    key_inv[...] = jnp.where(low_half, inverse[:, 0], inverse[:, 1]).reshape(rows, LANES)

    pl.semaphore_wait(barrier, nc * nf - 1 + nv - 1)

    def trade_copy(d):
        to = lax.rem(me_c + d, nc)
        return pltpu.make_async_remote_copy(
            src_ref=give.at[to], dst_ref=trade.at[me_c], send_sem=trade_send.at[d], recv_sem=trade_recv.at[d],
            device_id=device(d, 0, 0), device_id_type=MESH,
        )

    def key_copy(d):
        mine = keys.at[pl.ds(pl.multiple_of(me_f * rows, SUB), rows)]
        return pltpu.make_async_remote_copy(
            src_ref=mine, dst_ref=mine, send_sem=key_send.at[d], recv_sem=key_recv.at[d],
            device_id=device(0, 0, d), device_id_type=MESH,
        )

    trades = [trade_copy(d) for d in range(1, nc)]
    key_copies = [key_copy(d) for d in range(1, nf)]
    for copy in trades:
        copy.start()
    for copy in key_copies:
        copy.start()
    trade[me_c] = give[me_c]
    for copy in trades:
        copy.wait()

    own_rows = pl.ds(pl.multiple_of(me_v * SUB, SUB), SUB)
    q_full[me_f, own_rows, :] = trade[me_f, 0:SUB, :]

    def gather_copy(step):
        return pltpu.make_async_remote_copy(
            src_ref=trade.at[me_f, pl.ds(0, SUB)], dst_ref=q_full.at[me_f, own_rows],
            send_sem=gather_send, recv_sem=gather_recv, device_id=device(0, step, 0), device_id_type=MESH,
        )

    @pl.loop(1, nv)
    def _(step):
        gather_copy(step).start()

    def row_number(frame, patch):
        return (frame // 4) * rows + patch * 4 + lax.rem(frame, 4)

    winner = row_number(
        trade[me_f, SUB : 2 * SUB, :].astype(jnp.int32), trade[me_f, 2 * SUB : 3 * SUB, :].astype(jnp.int32)
    )
    for t in range(tok):
        column[t * SUB : (t + 1) * SUB, :] = jnp.broadcast_to(winner[:, t : t + 1], (SUB, LANES))
    wide_lane = iota((per_block, LANES), 1)
    column_value = column[...]
    padded = key_cat.shape[0]
    chosen = jnp.concatenate(
        [(column_value == wide_lane + k * LANES).astype(f32).astype(bf16) for k in range(padded // LANES)], axis=1
    )

    frames = jnp.zeros((SUB, LANES), f32)
    patch_all = jnp.zeros((SUB, LANES), f32)
    length = jnp.zeros((SUB, LANES), f32)
    for j in range(nc):
        here = group == j
        frames = jnp.where(here, pltpu.roll(trade[j, SUB : 2 * SUB, :], j * tok, 1), frames)
        patch_all = jnp.where(here, pltpu.roll(trade[j, 2 * SUB : 3 * SUB, :], j * tok, 1), patch_all)
        length = jnp.where(here, trade[j, 3 * SUB : 4 * SUB, :], length)
    frames = frames.astype(jnp.int32)
    live = (slot_in_group.astype(f32) < length) & (group < nc)
    safe_length = jnp.maximum(length, 1.0)
    local = jnp.where(
        (frames // 4 == me_f) & (group < nc), patch_all.astype(jnp.int32) * 4 + lax.rem(frames, 4), 255
    )
    from_lane = iota((LANES, all_tokens), 0)
    token = iota((LANES, all_tokens), 1)
    spread = (
        (from_lane == (token // per_block) * tok + lax.rem(token, per_block) // SUB).astype(f32).astype(bf16)
    )
    mine_of = lax.rem(iota((SUB, all_tokens), 1), SUB) == iota((SUB, all_tokens), 0)

    def as_row(values):
        return jnp.sum(jnp.where(mine_of, values, 0.0), axis=0, keepdims=True)

    twice = jnp.concatenate([local.astype(f32), jnp.zeros((SUB, LANES), f32)], axis=0).astype(bf16)
    local_row = as_row(dot(twice, spread)[0:SUB]).astype(jnp.int32)
    hit = (iota((rows, all_tokens), 0) == local_row).astype(f32)
    one_hot[...] = hit.astype(bf16)
    same_group = ((iota((LANES, LANES), 0) // tok) == (iota((LANES, LANES), 1) // tok)).astype(f32).astype(bf16)

    for copy in key_copies:
        copy.wait()
    if padded > all_rows:
        key_cat[all_rows:padded, :] = jnp.zeros((padded - all_rows, 2 * LANES), bf16)
    high, low = two_terms(keys[...])
    key_cat[0:all_rows, 0:LANES] = high
    key_cat[0:all_rows, LANES:] = low
    both = dot(chosen, key_cat[...])
    picked = both[:, 0:LANES] + both[:, LANES:]
    picked_rows[...] = picked

    gathered = pltpu.make_async_copy(
        q_full.at[0, pl.ds(0, (nv - 1) * SUB)], q_full.at[0, pl.ds(0, (nv - 1) * SUB)], gather_recv
    )
    gathered.wait()
    product = picked * q_full[me_f]
    tile = jnp.zeros((SUB, LANES), f32)
    for t in range(tok):
        value = jnp.sum(product[t * SUB : (t + 1) * SUB, :], axis=1, keepdims=True)
        tile = jnp.where(lane == me_f * tok + t, value, tile)
    tile_out[0] = tile

    me_16 = me_c * nf + me_f
    tiles_in[me_16] = tile

    def tile_copy(step):
        return pltpu.make_async_remote_copy(
            src_ref=tile_out.at[0], dst_ref=tiles_in.at[me_16], send_sem=tile_send, recv_sem=tile_recv,
            device_id=device(step // nf, 0, lax.rem(step, nf)), device_id_type=MESH,
        )

    @pl.loop(1, nc * nf)
    def _(step):
        tile_copy(step).start()

    rows_in[me_v] = picked_rows[own_rows, :]

    def rows_copy(step):
        to = lax.rem(me_v + step, nv)
        return pltpu.make_async_remote_copy(
            src_ref=picked_rows.at[pl.ds(pl.multiple_of(to * SUB, SUB), SUB)], dst_ref=rows_in.at[me_v],
            send_sem=rows_send, recv_sem=rows_recv, device_id=device(0, step, 0), device_id_type=MESH,
        )

    @pl.loop(1, nv)
    def _(step):
        rows_copy(step).start()

    def spread_copy(d):
        return pltpu.make_async_remote_copy(
            src_ref=q_full.at[me_f], dst_ref=q_full.at[me_f], send_sem=spread_send.at[d], recv_sem=spread_recv.at[d],
            device_id=device(0, 0, d), device_id_type=MESH,
        )

    spreads = [spread_copy(d) for d in range(1, nf)]
    for copy in spreads:
        copy.start()

    pltpu.make_async_copy(
        tiles_in.at[pl.ds(0, nc * nf - 1)], tiles_in.at[pl.ds(0, nc * nf - 1)], tile_recv
    ).wait()
    all_picked = jnp.sum(tiles_in[...], axis=0)
    live_share = jnp.where(live, all_picked, 0.0)
    scores = times_exact(live_share, same_group) / safe_length
    own_logits = logit_scale * scores
    logit_tile = jnp.where((slot_in_group == me_v) & (group < nc), own_logits, 0.0)
    tile_out[1] = logit_tile
    logits_in[me_v] = logit_tile

    def logit_copy(step):
        return pltpu.make_async_remote_copy(
            src_ref=tile_out.at[1], dst_ref=logits_in.at[me_v], send_sem=logit_send, recv_sem=logit_recv,
            device_id=device(0, step, 0), device_id_type=MESH,
        )

    @pl.loop(1, nv)
    def _(step):
        logit_copy(step).start()

    share_row = as_row(times_exact(live_share / safe_length, spread))
    caption_of = iota((all_tokens, LANES), 0)
    caption_lane = (caption_of // per_block) * (LANES // nc) + lax.rem(caption_of, SUB)
    by_caption = (iota((all_tokens, LANES), 1) == caption_lane).astype(f32).astype(bf16)
    share_high, share_low = two_terms(hit * share_row)
    inner_table = dot(share_high, by_caption) + dot(share_low, by_caption)

    pltpu.make_async_copy(logits_in.at[pl.ds(0, nv - 1)], logits_in.at[pl.ds(0, nv - 1)], logit_recv).wait()
    logits = jnp.sum(logits_in[...], axis=0)
    used = group < nc
    exp_logits = jnp.where(used, jnp.exp(logits), 0.0)
    row_total = times_exact(exp_logits, same_group)
    col = jnp.broadcast_to(jnp.sum(exp_logits, axis=0, keepdims=True), (SUB, LANES))
    col_total = col
    for j in range(1, LANES // tok):
        col_total = col_total + pltpu.roll(col, j * tok, 1)
    positive = jnp.where(used & (slot_in_group == group * SUB + sub), 1.0, 0.0)
    grad = logit_scale * (0.5 * (exp_logits / row_total + exp_logits / col_total) - positive)
    weight = jnp.where(used, grad / safe_length, 0.0)

    block_weight = jnp.zeros((SUB, LANES), f32)
    block_length = jnp.zeros((SUB, LANES), f32)
    for j in range(nc):
        here = me_f == j
        shifted = pltpu.roll(weight, (LANES - j * tok) % LANES, 1)
        block_weight = jnp.where(here, shifted, block_weight)
        block_length = jnp.where(here, trade[j, 3 * SUB : 4 * SUB, :], block_length)
    slice_grad = jnp.zeros((SUB, LANES), f32)
    for v in range(nv):
        slice_grad = slice_grad + block_weight[:, v : v + 1] * rows_in_value(rows_in, rows_recv, nv, v)
    slice_grad = jnp.where(me_v.astype(f32) < block_length, slice_grad, 0.0)
    grad_out[...] = slice_grad
    self_last = me_c == me_f

    def grad_copy(df):
        return pltpu.make_async_remote_copy(
            src_ref=grad_out, dst_ref=grads_in.at[me_c], send_sem=grad_send.at[df], recv_sem=grad_recv.at[me_c],
            device_id={"cap": me_f, "clip": me_v, "frame": df}, device_id_type=MESH,
        )

    for df in range(nf):
        to_self = self_last & (me_f == df)

        @pl.when(jnp.logical_not(to_self))
        def _():
            grad_copy(df).start()

        @pl.when(to_self)
        def _():
            grads_in[me_c] = slice_grad

    own = jnp.where(slot_in_group == me_v, grad, 0.0)
    row_weight = jnp.zeros((SUB, LANES), f32)
    token_weight = []
    for j in range(nc):
        value = jnp.sum(jnp.where(group == j, own, 0.0), axis=1, keepdims=True)
        row_weight = jnp.where(lane == j * (LANES // nc) + sub, value, row_weight)
        token_weight.append(value / jnp.maximum(trade[j, 3 * SUB : 4 * SUB, :], 1.0))
    inner = jnp.sum(inner_table * jnp.sum(row_weight, axis=0, keepdims=True), axis=1, keepdims=True)
    for copy in spreads:
        copy.wait()
    when = iota((tok, SUB, LANES), 0).astype(f32)
    parts = []
    for j in range(nc):
        mask = when < trade[j, 3 * SUB : 4 * SUB, :][None]
        scaled = q_full[j].reshape(tok, SUB, LANES) * jnp.where(mask, token_weight[j][None], 0.0)
        parts.append(jnp.concatenate(two_terms(scaled.reshape(per_block, LANES)), axis=1))
    both = dot(one_hot[...], jnp.concatenate(parts, axis=0))
    own_keys = keys[pl.ds(pl.multiple_of(me_f * rows, SUB), rows), :]
    clip_res[...] = key_inv[...] * (both[:, 0:LANES] + both[:, LANES:] - own_keys * inner)
    clip_store = pltpu.make_async_copy(clip_res, clip_out, store_sem.at[0])
    clip_store.start()

    terms = jnp.where((slot_in_group == 0) & used, jnp.log(row_total), 0.0)
    terms = terms + jnp.where((lane < tok) & (sub == 0), jnp.log(col_total), 0.0)
    terms = 0.5 * terms - positive * logits
    loss_ref[0, 0] = jnp.sum(terms) / (nc * SUB)

    for j in range(nc):

        @pl.when(jnp.logical_not(self_last & (me_c == j)))
        def _():
            pltpu.make_async_copy(grad_out, grads_in.at[j], grad_recv.at[j]).wait()

    dot_tile = jnp.zeros((SUB, LANES), f32)
    for j in range(nc):
        dot_tile = dot_tile + qn[j] * grads_in[j]
    cap_inner = jnp.sum(dot_tile, axis=1, keepdims=True)
    for j in range(nc):
        cap_res[pl.ds(j, SUB, stride=nc), :] = cap_inv * (grads_in[j] - qn[j] * cap_inner)
    cap_store = pltpu.make_async_copy(cap_res, cap_out, store_sem.at[1])
    cap_store.start()

    pltpu.make_async_copy(
        q_full.at[0, pl.ds(0, (nv - 1) * SUB)], q_full.at[0, pl.ds(0, (nv - 1) * SUB)], gather_send
    ).wait()
    pltpu.make_async_copy(rows_in.at[pl.ds(0, nv - 1)], rows_in.at[pl.ds(0, nv - 1)], rows_send).wait()
    pltpu.make_async_copy(logits_in.at[pl.ds(0, nv - 1)], logits_in.at[pl.ds(0, nv - 1)], logit_send).wait()
    pltpu.make_async_copy(
        tiles_in.at[pl.ds(0, nc * nf - 1)], tiles_in.at[pl.ds(0, nc * nf - 1)], tile_send
    ).wait()
    for df in range(nf):

        @pl.when(jnp.logical_not(self_last & (me_f == df)))
        def _():
            pltpu.make_async_copy(grad_out, grads_in.at[0], grad_send.at[df]).wait()

    clip_store.wait()
    cap_store.wait()


def rows_in_value(rows_in, rows_recv, nv, v):
    if v == 0:
        pltpu.make_async_copy(rows_in.at[pl.ds(0, nv - 1)], rows_in.at[pl.ds(0, nv - 1)], rows_recv).wait()
    return rows_in[v]


def body(nc, nv, cap_tokens, clip_tokens, win_frame, win_patch, cap_lengths):
    block, _, width = cap_tokens.shape
    _, frames, patches, _ = clip_tokens.shape
    assert block == SUB and frames == 4 and width == nc * LANES and win_frame.shape == (SUB, nv, 1)
    rows = frames * patches
    per_block = nv * SUB
    padded = -(-nc * rows // LANES) * LANES
    caps = cap_tokens.reshape(SUB * nc, LANES)
    clips = clip_tokens.reshape(frames, patches, nc, LANES).transpose(1, 2, 0, 3).reshape(patches, nc * frames, LANES)
    vmem = pltpu.VMEM
    dma = pltpu.SemaphoreType.DMA
    scratch = [
        vmem((SUB * nc, LANES), f32),
        vmem((patches, nc * frames, LANES), f32),
        vmem((SUB, nv), jnp.int32),
        vmem((SUB, nv), jnp.int32),
        vmem((nc, SUB, LANES), f32),
        vmem((nc, 4 * SUB, LANES), f32),
        vmem((nc, 4 * SUB, LANES), f32),
        vmem((nc, per_block, LANES), f32),
        vmem((nc * rows, LANES), f32),
        vmem((rows, LANES), f32),
        vmem((padded, 2 * LANES), bf16),
        vmem((per_block, LANES), jnp.int32),
        vmem((per_block, LANES), f32),
        vmem((nv, SUB, LANES), f32),
        vmem((nc * nc, SUB, LANES), f32),
        vmem((nv, SUB, LANES), f32),
        vmem((2, SUB, LANES), f32),
        vmem((nc, SUB, LANES), f32),
        vmem((SUB, LANES), f32),
        vmem((rows, nc * per_block), bf16),
        vmem((SUB * nc, LANES), f32),
        vmem((rows, LANES), f32),
        dma((4,)), dma((2,)),
        dma((nc,)), dma((nc,)), dma((nc,)), dma((nc,)),
        dma, dma,
        dma((nc,)), dma((nc,)),
        dma, dma, dma, dma, dma, dma,
        dma((nc,)), dma((nc,)),
    ]
    hbm = pl.BlockSpec(memory_space=pl.ANY)
    smem = pl.BlockSpec(memory_space=pltpu.SMEM)
    loss, cap_grad, clip_grad = pl.pallas_call(
        functools.partial(kernel, nc, nv, patches),
        out_shape=(
            jax.ShapeDtypeStruct((1, 1), f32),
            jax.ShapeDtypeStruct((SUB * nc, LANES), f32),
            jax.ShapeDtypeStruct((rows, LANES), f32),
        ),
        in_specs=[hbm, hbm, hbm, hbm, smem],
        out_specs=(smem, hbm, hbm),
        scratch_shapes=scratch,
        compiler_params=pltpu.CompilerParams(
            collective_id=0, has_side_effects=True, vmem_limit_bytes=32 * 1024 * 1024
        ),
    )(caps, clips, win_frame.reshape(SUB, nv), win_patch.reshape(SUB, nv), cap_lengths)
    clip_grad = clip_grad.reshape(patches, frames, LANES).transpose(1, 0, 2)[None]
    return loss.reshape(()), cap_grad.reshape(SUB, 1, width), clip_grad


def solution(mesh):
    placed = (
        P("cap", "clip", None),
        P("clip", "frame", None, None),
        P("cap", None, "clip"),
        P("cap", None, "clip"),
        P("cap"),
    )
    assert mesh.shape["cap"] == mesh.shape["frame"]
    return jax.shard_map(
        functools.partial(body, mesh.shape["cap"], mesh.shape["clip"]),
        mesh=mesh,
        in_specs=placed,
        out_specs=(P(), P("cap", "clip", None), P("clip", "frame", None, "cap")),
        check_vma=False,
    )
```

```python
import functools

import jax
import jax.numpy as jnp
from jax import lax
from jax.experimental import pallas as pl
from jax.experimental.pallas import tpu as pltpu
from jax.sharding import PartitionSpec as P

MESH = pl.DeviceIdType.MESH
logit_scale = 1.0 / 0.07
norm_eps = 1e-06
f32 = jnp.float32
bf16 = jnp.bfloat16
LANES = 128
SUB = 8


def iota(shape, dim):
    return lax.broadcasted_iota(jnp.int32, shape, dim)


def two_terms(x):
    high = x.astype(bf16)
    return high, (x - high.astype(f32)).astype(bf16)


def three_terms(x):
    high = x.astype(bf16).astype(f32)
    rest = x - high
    middle = rest.astype(bf16).astype(f32)
    return high, middle, rest - middle


def dot(a, b):
    return jnp.dot(a, b, preferred_element_type=f32)


def times_exact(tile, table):
    high, middle, low = three_terms(tile)
    stacked = jnp.concatenate([high, middle, low, jnp.zeros_like(high)], axis=0).astype(bf16)
    out = dot(stacked, table)
    return out[0:SUB] + out[SUB : 2 * SUB] + out[2 * SUB : 3 * SUB]


def log2(n):
    assert n & (n - 1) == 0
    return n.bit_length() - 1


def kernel(
    nc, nv, patches,
    cap_ref, clip_ref, wf_ref, wp_ref, len_ref,
    loss_ref, cap_out, clip_out,
    cap_raw, clip_raw, wf_raw, wp_raw, qn, give, trade, q_full, q_pick, unit_keys, keys, key_inv, key_cat, column,
    picked_rows, rows_in, tiles_in, logits_in, tile_out, grads_in, grad_out, spread_table, caption_table, one_hot,
    cap_res, clip_res,
    load_sem, store_sem, trade_send, trade_recv, key_send, key_recv, pick_send, pick_recv, gather_send, gather_recv,
    spread_send, spread_recv, rows_send, rows_recv, tile_send, tile_recv, logit_send, logit_recv, grad_send, grad_recv,
):
    nf = nc
    tok = nv
    me_c, me_v, me_f = lax.axis_index("cap"), lax.axis_index("clip"), lax.axis_index("frame")
    rows = 4 * patches
    all_rows = nf * rows
    per_block = tok * SUB
    all_tokens = nf * per_block
    tok_bits, block_bits = log2(tok), log2(per_block)

    loads = [
        pltpu.make_async_copy(clip_ref, clip_raw, load_sem.at[0]),
        pltpu.make_async_copy(cap_ref, cap_raw, load_sem.at[1]),
        pltpu.make_async_copy(wf_ref, wf_raw, load_sem.at[2]),
        pltpu.make_async_copy(wp_ref, wp_raw, load_sem.at[3]),
    ]
    for load in loads:
        load.start()

    barrier = pltpu.get_barrier_semaphore()

    def device(dc, dv, df):
        return {
            "cap": lax.rem(me_c + dc, nc),
            "clip": lax.rem(me_v + dv, nv),
            "frame": lax.rem(me_f + df, nf),
        }

    def signal(dc, dv, df):
        pl.semaphore_signal(barrier, inc=1, device_id=device(dc, dv, df), device_id_type=MESH)

    @pl.loop(1, nc * nf)
    def _(step):
        signal(step // nf, 0, lax.rem(step, nf))

    @pl.loop(1, nv)
    def _(step):
        signal(0, step, 0)

    lane = iota((SUB, LANES), 1)
    sub = iota((SUB, LANES), 0)
    group = lane >> tok_bits
    slot_in_group = lane & (tok - 1)
    used = group < nc

    loads[1].wait()
    raw = [cap_raw[pl.ds(j, SUB, stride=nc), :] for j in range(nc)]
    total = raw[0] * raw[0]
    for j in range(1, nc):
        total = total + raw[j] * raw[j]
    cap_inv = lax.rsqrt(jnp.sum(total, axis=1, keepdims=True) + norm_eps)
    for j in range(nc):
        unit = raw[j] * cap_inv
        qn[j] = unit
        give[j, 0:SUB, :] = unit

    loads[0].wait()
    whole = clip_raw[...].reshape(patches, nc // 2, SUB, LANES)
    square = whole * whole
    summed = square[:, 0]
    for j in range(1, nc // 2):
        summed = summed + square[:, j]
    summed = summed + pltpu.roll(summed, 4, 1)
    inverse = lax.rsqrt(jnp.sum(summed, axis=2, keepdims=True) + norm_eps)
    low_half = iota((patches // 2, SUB, LANES), 1) < 4
    for j in range(nc // 2):
        unit = (whole[:, j] * inverse).reshape(patches // 2, 2, SUB, LANES)
        first, second = unit[:, 0], unit[:, 1]
        unit_keys[2 * j] = jnp.where(low_half, first, pltpu.roll(second, 4, 1)).reshape(rows, LANES)
        unit_keys[2 * j + 1] = jnp.where(low_half, pltpu.roll(first, 4, 1), second).reshape(rows, LANES)
    inverse = jnp.broadcast_to(inverse, (patches, SUB, LANES)).reshape(patches // 2, 2, SUB, LANES)
    key_inv[...] = jnp.where(low_half, inverse[:, 0], inverse[:, 1]).reshape(rows, LANES)

    pl.semaphore_wait(barrier, nc * nf - 1 + nv - 1)

    own_key_rows = pl.ds(pl.multiple_of(me_f * rows, SUB), rows)
    own_rows = pl.ds(pl.multiple_of(me_v * SUB, SUB), SUB)

    def key_copy(d):
        return pltpu.make_async_remote_copy(
            src_ref=unit_keys.at[lax.rem(me_f + d, nf)], dst_ref=keys.at[own_key_rows],
            send_sem=key_send.at[d], recv_sem=key_recv.at[d], device_id=device(0, 0, d), device_id_type=MESH,
        )

    key_copies = [key_copy(d) for d in range(1, nf)]
    for copy in key_copies:
        copy.start()

    @pl.loop(1, nv)
    def _(step):
        pltpu.make_async_remote_copy(
            src_ref=qn.at[me_f], dst_ref=q_pick.at[own_rows],
            send_sem=pick_send, recv_sem=pick_recv, device_id=device(0, step, 0), device_id_type=MESH,
        ).start()

    loads[2].wait()
    loads[3].wait()
    lengths = jnp.zeros((SUB, LANES), f32)
    for c in range(SUB):
        lengths = jnp.where(sub == c, len_ref[c].astype(f32), lengths)
    give[:, SUB : 3 * SUB, :] = jnp.zeros((nc, 2 * SUB, LANES), f32)
    for j in range(nc):
        give[j, SUB : 2 * SUB, 0:tok] = wf_raw[...].astype(f32)
        give[j, 2 * SUB : 3 * SUB, 0:tok] = wp_raw[...].astype(f32)
        give[j, 3 * SUB : 4 * SUB, :] = lengths

    def trade_copy(d):
        to = lax.rem(me_c + d, nc)
        return pltpu.make_async_remote_copy(
            src_ref=give.at[to], dst_ref=trade.at[me_c], send_sem=trade_send.at[d], recv_sem=trade_recv.at[d],
            device_id=device(d, 0, 0), device_id_type=MESH,
        )

    trades = [trade_copy(d) for d in range(1, nc)]
    for copy in trades:
        copy.start()
    trade[me_c] = give[me_c]
    keys[own_key_rows, :] = unit_keys[me_f]
    q_pick[own_rows, :] = qn[me_f]

    frame_own = wf_raw[...]
    winner = (frame_own >> 2) * rows + wp_raw[...] * 4 + (frame_own & 3)
    for t in range(tok):
        column[t * SUB : (t + 1) * SUB, :] = jnp.broadcast_to(winner[:, t : t + 1], (SUB, LANES))
    wide_lane = iota((per_block, LANES), 1)
    column_value = column[...]
    padded = key_cat.shape[0]
    chosen = jnp.concatenate(
        [(column_value == wide_lane + k * LANES).astype(f32).astype(bf16) for k in range(padded // LANES)], axis=1
    )
    if padded > all_rows:
        key_cat[all_rows:padded, :] = jnp.zeros((padded - all_rows, 2 * LANES), bf16)

    from_lane = iota((LANES, all_tokens), 0)
    token = iota((LANES, all_tokens), 1)
    spread_table[...] = (
        (from_lane == ((token >> block_bits) << tok_bits) + ((token & (per_block - 1)) >> 3)).astype(f32).astype(bf16)
    )
    caption_of = iota((all_tokens, LANES), 0)
    caption_lane = (caption_of >> block_bits) * (LANES // nc) + (caption_of & 7)
    caption_table[...] = (iota((all_tokens, LANES), 1) == caption_lane).astype(f32).astype(bf16)
    same_group = ((iota((LANES, LANES), 0) >> tok_bits) == (iota((LANES, LANES), 1) >> tok_bits)).astype(f32).astype(bf16)
    mine_of = (iota((SUB, all_tokens), 1) & 7) == iota((SUB, all_tokens), 0)

    def as_row(values):
        return jnp.sum(jnp.where(mine_of, values, 0.0), axis=0, keepdims=True)

    for copy in trades:
        copy.wait()
    q_full[me_f, own_rows, :] = trade[me_f, 0:SUB, :]

    @pl.loop(1, nv)
    def _(step):
        pltpu.make_async_remote_copy(
            src_ref=trade.at[me_f, pl.ds(0, SUB)], dst_ref=q_full.at[me_f, own_rows],
            send_sem=gather_send, recv_sem=gather_recv, device_id=device(0, step, 0), device_id_type=MESH,
        ).start()

    frames = jnp.zeros((SUB, LANES), f32)
    patch_all = jnp.zeros((SUB, LANES), f32)
    length = jnp.zeros((SUB, LANES), f32)
    for j in range(nc):
        here = group == j
        frames = jnp.where(here, pltpu.roll(trade[j, SUB : 2 * SUB, :], j * tok, 1), frames)
        patch_all = jnp.where(here, pltpu.roll(trade[j, 2 * SUB : 3 * SUB, :], j * tok, 1), patch_all)
        length = jnp.where(here, trade[j, 3 * SUB : 4 * SUB, :], length)
    frames = frames.astype(jnp.int32)
    live = (slot_in_group.astype(f32) < length) & used
    safe_length = jnp.maximum(length, 1.0)
    local = jnp.where(((frames >> 2) == me_f) & used, patch_all.astype(jnp.int32) * 4 + (frames & 3), 255)
    twice = jnp.concatenate([local.astype(f32), jnp.zeros((SUB, LANES), f32)], axis=0).astype(bf16)
    local_row = as_row(dot(twice, spread_table[...])[0:SUB]).astype(jnp.int32)
    one_hot[...] = (iota((rows, all_tokens), 0) == local_row).astype(f32).astype(bf16)

    for copy in key_copies:
        copy.wait()
    high, low = two_terms(keys[...])
    key_cat[0:all_rows, 0:LANES] = high
    key_cat[0:all_rows, LANES:] = low
    both = dot(chosen, key_cat[...])
    picked = both[:, 0:LANES] + both[:, LANES:]
    picked_rows[...] = picked

    all_but_one = pl.ds(0, (nv - 1) * SUB)
    pltpu.make_async_copy(q_pick.at[all_but_one], q_pick.at[all_but_one], pick_recv).wait()
    product = picked * q_pick[...]
    tile = jnp.zeros((SUB, LANES), f32)
    for t in range(tok):
        value = jnp.sum(product[t * SUB : (t + 1) * SUB, :], axis=1, keepdims=True)
        tile = jnp.where(lane == me_c * tok + t, value, tile)
    tile_out[0] = tile

    me_16 = me_c * nf + me_f
    tiles_in[me_16] = tile

    @pl.loop(1, nc * nf)
    def _(step):
        pltpu.make_async_remote_copy(
            src_ref=tile_out.at[0], dst_ref=tiles_in.at[me_16], send_sem=tile_send, recv_sem=tile_recv,
            device_id=device(step // nf, 0, lax.rem(step, nf)), device_id_type=MESH,
        ).start()

    rows_in[me_v] = picked_rows[own_rows, :]

    @pl.loop(1, nv)
    def _(step):
        to = lax.rem(me_v + step, nv)
        pltpu.make_async_remote_copy(
            src_ref=picked_rows.at[pl.ds(pl.multiple_of(to * SUB, SUB), SUB)], dst_ref=rows_in.at[me_v],
            send_sem=rows_send, recv_sem=rows_recv, device_id=device(0, step, 0), device_id_type=MESH,
        ).start()

    other_tiles = tiles_in.at[pl.ds(0, nc * nf - 1)]
    other_clips = rows_in.at[pl.ds(0, nv - 1)]
    pltpu.make_async_copy(other_tiles, other_tiles, tile_recv).wait()
    all_picked = jnp.sum(tiles_in[...], axis=0)
    live_share = jnp.where(live, all_picked, 0.0)
    own_logits = logit_scale * (times_exact(live_share, same_group) / safe_length)
    logit_tile = jnp.where((slot_in_group == me_v) & used, own_logits, 0.0)
    tile_out[1] = logit_tile
    logits_in[me_v] = logit_tile

    @pl.loop(1, nv)
    def _(step):
        pltpu.make_async_remote_copy(
            src_ref=tile_out.at[1], dst_ref=logits_in.at[me_v], send_sem=logit_send, recv_sem=logit_recv,
            device_id=device(0, step, 0), device_id_type=MESH,
        ).start()

    gathered = q_full.at[0, all_but_one]
    pltpu.make_async_copy(gathered, gathered, gather_recv).wait()

    def spread_copy(d):
        return pltpu.make_async_remote_copy(
            src_ref=q_full.at[me_f], dst_ref=q_full.at[me_f], send_sem=spread_send.at[d], recv_sem=spread_recv.at[d],
            device_id=device(0, 0, d), device_id_type=MESH,
        )

    spreads = [spread_copy(d) for d in range(1, nf)]
    for copy in spreads:
        copy.start()

    share_row = as_row(times_exact(live_share / safe_length, spread_table[...]))
    share_high, share_low = two_terms(one_hot[...].astype(f32) * share_row)
    inner_table = dot(share_high, caption_table[...]) + dot(share_low, caption_table[...])
    pltpu.make_async_copy(other_clips, other_clips, rows_recv).wait()

    pltpu.make_async_copy(other_clips, other_clips, logit_recv).wait()
    logits = jnp.sum(logits_in[...], axis=0)
    exp_logits = jnp.where(used, jnp.exp(logits), 0.0)
    row_total = times_exact(exp_logits, same_group)
    col = jnp.broadcast_to(jnp.sum(exp_logits, axis=0, keepdims=True), (SUB, LANES))
    col_total = col
    for j in range(1, LANES // tok):
        col_total = col_total + pltpu.roll(col, j * tok, 1)
    positive = jnp.where(used & (slot_in_group == group * SUB + sub), 1.0, 0.0)
    grad = logit_scale * (0.5 * (exp_logits / row_total + exp_logits / col_total) - positive)
    weight = jnp.where(used, grad / safe_length, 0.0)

    block_weight = jnp.zeros((SUB, LANES), f32)
    for j in range(nc):
        block_weight = jnp.where(me_c == j, pltpu.roll(weight, (LANES - j * tok) % LANES, 1), block_weight)
    slice_grad = jnp.zeros((SUB, LANES), f32)
    for v in range(nv):
        slice_grad = slice_grad + block_weight[:, v : v + 1] * rows_in[v]
    slice_grad = jnp.where(me_v.astype(f32) < lengths, slice_grad, 0.0)
    grad_out[...] = slice_grad
    grads_in[me_f] = slice_grad

    def grad_copy(d):
        return pltpu.make_async_remote_copy(
            src_ref=grad_out, dst_ref=grads_in.at[me_f], send_sem=grad_send.at[d], recv_sem=grad_recv.at[d],
            device_id=device(0, 0, d), device_id_type=MESH,
        )

    grad_copies = [grad_copy(d) for d in range(1, nf)]
    for copy in grad_copies:
        copy.start()

    own = jnp.where(slot_in_group == me_v, grad, 0.0)
    row_weight = jnp.zeros((SUB, LANES), f32)
    token_weight = []
    for j in range(nc):
        value = jnp.sum(jnp.where(group == j, own, 0.0), axis=1, keepdims=True)
        row_weight = jnp.where(lane == j * (LANES // nc) + sub, value, row_weight)
        token_weight.append(value / jnp.maximum(trade[j, 3 * SUB : 4 * SUB, :], 1.0))
    inner = jnp.sum(inner_table * jnp.sum(row_weight, axis=0, keepdims=True), axis=1, keepdims=True)
    for copy in spreads:
        copy.wait()
    when = iota((tok, SUB, LANES), 0).astype(f32)
    parts = []
    for j in range(nc):
        mask = when < trade[j, 3 * SUB : 4 * SUB, :][None]
        scaled = q_full[j].reshape(tok, SUB, LANES) * jnp.where(mask, token_weight[j][None], 0.0)
        parts.append(jnp.concatenate(two_terms(scaled.reshape(per_block, LANES)), axis=1))
    both = dot(one_hot[...], jnp.concatenate(parts, axis=0))
    clip_res[...] = key_inv[...] * (both[:, 0:LANES] + both[:, LANES:] - unit_keys[me_c] * inner)
    clip_store = pltpu.make_async_copy(clip_res, clip_out, store_sem.at[0])
    clip_store.start()

    terms = jnp.where((slot_in_group == 0) & used, jnp.log(row_total), 0.0)
    terms = terms + jnp.where((lane < tok) & (sub == 0), jnp.log(col_total), 0.0)
    terms = 0.5 * terms - positive * logits
    loss_ref[0, 0] = jnp.sum(terms) / (nc * SUB)

    for copy in grad_copies:
        copy.wait()
    dot_tile = jnp.zeros((SUB, LANES), f32)
    for j in range(nc):
        dot_tile = dot_tile + qn[j] * grads_in[j]
    cap_inner = jnp.sum(dot_tile, axis=1, keepdims=True)
    for j in range(nc):
        cap_res[pl.ds(j, SUB, stride=nc), :] = cap_inv * (grads_in[j] - qn[j] * cap_inner)
    cap_store = pltpu.make_async_copy(cap_res, cap_out, store_sem.at[1])
    cap_store.start()

    pltpu.make_async_copy(gathered, gathered, pick_send).wait()
    pltpu.make_async_copy(gathered, gathered, gather_send).wait()
    pltpu.make_async_copy(other_clips, other_clips, rows_send).wait()
    pltpu.make_async_copy(other_clips, other_clips, logit_send).wait()
    pltpu.make_async_copy(other_tiles, other_tiles, tile_send).wait()
    clip_store.wait()
    cap_store.wait()


def body(nc, nv, cap_tokens, clip_tokens, win_frame, win_patch, cap_lengths):
    block, _, width = cap_tokens.shape
    _, frames, patches, _ = clip_tokens.shape
    assert block == SUB and frames == 4 and width == nc * LANES and win_frame.shape == (SUB, nv, 1)
    rows = frames * patches
    per_block = nv * SUB
    padded = -(-nc * rows // LANES) * LANES
    caps = cap_tokens.reshape(SUB * nc, LANES)
    clips = clip_tokens.reshape(frames, patches, nc, LANES).transpose(1, 2, 0, 3).reshape(patches, nc * frames, LANES)
    vmem = pltpu.VMEM
    dma = pltpu.SemaphoreType.DMA
    scratch = [
        vmem((SUB * nc, LANES), f32),
        vmem((patches, nc * frames, LANES), f32),
        vmem((SUB, nv), jnp.int32),
        vmem((SUB, nv), jnp.int32),
        vmem((nc, SUB, LANES), f32),
        vmem((nc, 4 * SUB, LANES), f32),
        vmem((nc, 4 * SUB, LANES), f32),
        vmem((nc, per_block, LANES), f32),
        vmem((per_block, LANES), f32),
        vmem((nc, rows, LANES), f32),
        vmem((nc * rows, LANES), f32),
        vmem((rows, LANES), f32),
        vmem((padded, 2 * LANES), bf16),
        vmem((per_block, LANES), jnp.int32),
        vmem((per_block, LANES), f32),
        vmem((nv, SUB, LANES), f32),
        vmem((nc * nc, SUB, LANES), f32),
        vmem((nv, SUB, LANES), f32),
        vmem((2, SUB, LANES), f32),
        vmem((nc, SUB, LANES), f32),
        vmem((SUB, LANES), f32),
        vmem((LANES, nc * per_block), bf16),
        vmem((nc * per_block, LANES), bf16),
        vmem((rows, nc * per_block), bf16),
        vmem((SUB * nc, LANES), f32),
        vmem((rows, LANES), f32),
        dma((4,)), dma((2,)),
        dma((nc,)), dma((nc,)), dma((nc,)), dma((nc,)),
        dma, dma, dma, dma,
        dma((nc,)), dma((nc,)),
        dma, dma, dma, dma, dma, dma,
        dma((nc,)), dma((nc,)),
    ]
    hbm = pl.BlockSpec(memory_space=pl.ANY)
    smem = pl.BlockSpec(memory_space=pltpu.SMEM)
    loss, cap_grad, clip_grad = pl.pallas_call(
        functools.partial(kernel, nc, nv, patches),
        out_shape=(
            jax.ShapeDtypeStruct((1, 1), f32),
            jax.ShapeDtypeStruct((SUB * nc, LANES), f32),
            jax.ShapeDtypeStruct((rows, LANES), f32),
        ),
        in_specs=[hbm, hbm, hbm, hbm, smem],
        out_specs=(smem, hbm, hbm),
        scratch_shapes=scratch,
        compiler_params=pltpu.CompilerParams(
            collective_id=0, has_side_effects=True, vmem_limit_bytes=60 * 1024 * 1024
        ),
    )(caps, clips, win_frame.reshape(SUB, nv), win_patch.reshape(SUB, nv), cap_lengths)
    clip_grad = clip_grad.reshape(patches, frames, LANES).transpose(1, 0, 2)[None]
    return loss.reshape(()), cap_grad.reshape(SUB, 1, width), clip_grad


def solution(mesh):
    placed = (
        P("cap", "clip", None),
        P("clip", "frame", None, None),
        P("cap", None, "clip"),
        P("cap", None, "clip"),
        P("cap"),
    )
    assert mesh.shape["cap"] == mesh.shape["frame"]
    return jax.shard_map(
        functools.partial(body, mesh.shape["cap"], mesh.shape["clip"]),
        mesh=mesh,
        in_specs=placed,
        out_specs=(P(), P("cap", "clip", None), P("clip", "frame", None, "cap")),
        check_vma=False,
    )
```

```python
import functools

import jax
import jax.numpy as jnp
from jax import lax
from jax.experimental import pallas as pl
from jax.experimental.pallas import tpu as pltpu
from jax.sharding import PartitionSpec as P

MESH = pl.DeviceIdType.MESH
logit_scale = 1.0 / 0.07
norm_eps = 1e-06
f32 = jnp.float32
bf16 = jnp.bfloat16
LANES = 128
SUB = 8


def iota(shape, dim):
    return lax.broadcasted_iota(jnp.int32, shape, dim)


def two_terms(x):
    high = x.astype(bf16)
    return high, (x - high.astype(f32)).astype(bf16)


def three_terms(x):
    high = x.astype(bf16).astype(f32)
    rest = x - high
    middle = rest.astype(bf16).astype(f32)
    return high, middle, rest - middle


def dot(a, b):
    return jnp.dot(a, b, preferred_element_type=f32)


def times_exact(tile, table):
    high, middle, low = three_terms(tile)
    stacked = jnp.concatenate([high, middle, low, jnp.zeros_like(high)], axis=0).astype(bf16)
    out = dot(stacked, table)
    return out[0:SUB] + out[SUB : 2 * SUB] + out[2 * SUB : 3 * SUB]


def group_of(lane, size):
    return lane >> log2(size)


def log2(n):
    assert n & (n - 1) == 0
    return n.bit_length() - 1


def kernel(
    nc, nv, patches,
    cap_ref, clip_ref, wf_ref, wp_ref, len_ref,
    loss_ref, cap_res, clip_res,
    cap_raw, clip_raw, wf_raw, wp_raw, qn, give, trade, q_full, q_pick, unit_keys, keys, key_inv, key_cat, column,
    picked_rows, rows_in, tiles_in, scores_in, logits_in, tile_out, line_out, weights, turned, grads_in, grad_out, spread_table, caption_table, one_hot,
    len_raw,
    load_sem, trade_send, trade_recv, key_send, key_recv, pick_send, pick_recv, gather_send, gather_recv,
    spread_send, spread_recv, rows_send, rows_recv, tile_send, tile_recv, score_send, score_recv, logit_send, logit_recv, grad_send, grad_recv,
):
    nf = nc
    tok = nv
    me_c, me_v, me_f = lax.axis_index("cap"), lax.axis_index("clip"), lax.axis_index("frame")
    rows = 4 * patches
    all_rows = nf * rows
    per_block = tok * SUB
    all_tokens = nf * per_block
    tok_bits, block_bits = log2(tok), log2(per_block)

    loads = [
        pltpu.make_async_copy(clip_ref, clip_raw, load_sem.at[0]),
        pltpu.make_async_copy(cap_ref, cap_raw, load_sem.at[1]),
        pltpu.make_async_copy(wf_ref, wf_raw, load_sem.at[2]),
        pltpu.make_async_copy(wp_ref, wp_raw, load_sem.at[3]),
        pltpu.make_async_copy(len_ref, len_raw, load_sem.at[4]),
    ]
    for load in loads:
        load.start()

    barrier = pltpu.get_barrier_semaphore()

    def device(dc, dv, df):
        return {
            "cap": lax.rem(me_c + dc, nc),
            "clip": lax.rem(me_v + dv, nv),
            "frame": lax.rem(me_f + df, nf),
        }

    def signal(dc, dv, df):
        pl.semaphore_signal(barrier, inc=1, device_id=device(dc, dv, df), device_id_type=MESH)

    @pl.loop(1, nc * nf)
    def _(step):
        signal(step // nf, 0, lax.rem(step, nf))

    @pl.loop(1, nv)
    def _(step):
        signal(0, step, 0)

    lane = iota((SUB, LANES), 1)
    sub = iota((SUB, LANES), 0)
    group = lane >> tok_bits
    slot_in_group = lane & (tok - 1)
    used = group < nc
    cap_lanes = LANES // nc
    in_line = (lane & (cap_lanes - 1)) < SUB

    loads[1].wait()
    raw = [cap_raw[pl.ds(j, SUB, stride=nc), :] for j in range(nc)]
    total = raw[0] * raw[0]
    for j in range(1, nc):
        total = total + raw[j] * raw[j]
    cap_inv = lax.rsqrt(jnp.sum(total, axis=1, keepdims=True) + norm_eps)
    for j in range(nc):
        unit = raw[j] * cap_inv
        qn[j] = unit
        give[j, 0:SUB, :] = unit

    loads[0].wait()
    whole = clip_raw[...].reshape(patches, nc // 2, SUB, LANES)
    square = whole * whole
    summed = square[:, 0]
    for j in range(1, nc // 2):
        summed = summed + square[:, j]
    summed = summed + pltpu.roll(summed, 4, 1)
    inverse = lax.rsqrt(jnp.sum(summed, axis=2, keepdims=True) + norm_eps)
    low_half = iota((patches // 2, SUB, LANES), 1) < 4
    for j in range(nc // 2):
        unit = (whole[:, j] * inverse).reshape(patches // 2, 2, SUB, LANES)
        first, second = unit[:, 0], unit[:, 1]
        unit_keys[2 * j] = jnp.where(low_half, first, pltpu.roll(second, 4, 1)).reshape(rows, LANES)
        unit_keys[2 * j + 1] = jnp.where(low_half, pltpu.roll(first, 4, 1), second).reshape(rows, LANES)
    inverse = jnp.broadcast_to(inverse, (patches, SUB, LANES)).reshape(patches // 2, 2, SUB, LANES)
    key_inv[...] = jnp.where(low_half, inverse[:, 0], inverse[:, 1]).reshape(rows, LANES)

    pl.semaphore_wait(barrier, nc * nf - 1 + nv - 1)

    own_key_rows = pl.ds(pl.multiple_of(me_f * rows, SUB), rows)
    own_rows = pl.ds(pl.multiple_of(me_v * SUB, SUB), SUB)

    def key_copy(d):
        return pltpu.make_async_remote_copy(
            src_ref=unit_keys.at[lax.rem(me_f + d, nf)], dst_ref=keys.at[own_key_rows],
            send_sem=key_send.at[d], recv_sem=key_recv.at[d], device_id=device(0, 0, d), device_id_type=MESH,
        )

    key_copies = [key_copy(d) for d in range(1, nf)]
    for copy in key_copies:
        copy.start()

    @pl.loop(1, nv)
    def _(step):
        pltpu.make_async_remote_copy(
            src_ref=qn.at[me_f], dst_ref=q_pick.at[own_rows],
            send_sem=pick_send, recv_sem=pick_recv, device_id=device(0, step, 0), device_id_type=MESH,
        ).start()

    for load in loads[2:]:
        load.wait()
    diagonal = iota((SUB, SUB), 0) == iota((SUB, SUB), 1)
    lengths = jnp.sum(jnp.where(diagonal, len_raw[...].astype(f32), 0.0), axis=1, keepdims=True)
    lengths = jnp.broadcast_to(lengths, (SUB, LANES))
    give[:, SUB : 3 * SUB, :] = jnp.zeros((nc, 2 * SUB, LANES), f32)
    for j in range(nc):
        give[j, SUB : 2 * SUB, 0:tok] = wf_raw[...].astype(f32)
        give[j, 2 * SUB : 3 * SUB, 0:tok] = wp_raw[...].astype(f32)
        give[j, 3 * SUB : 4 * SUB, :] = lengths

    def trade_copy(d):
        to = lax.rem(me_c + d, nc)
        return pltpu.make_async_remote_copy(
            src_ref=give.at[to], dst_ref=trade.at[me_c], send_sem=trade_send.at[d], recv_sem=trade_recv.at[d],
            device_id=device(d, 0, 0), device_id_type=MESH,
        )

    trades = [trade_copy(d) for d in range(1, nc)]
    for copy in trades:
        copy.start()
    trade[me_c] = give[me_c]
    keys[own_key_rows, :] = unit_keys[me_f]
    q_pick[own_rows, :] = qn[me_f]

    frame_own = wf_raw[...]
    winner = (frame_own >> 2) * rows + wp_raw[...] * 4 + (frame_own & 3)
    for t in range(tok):
        column[t * SUB : (t + 1) * SUB, :] = jnp.broadcast_to(winner[:, t : t + 1], (SUB, LANES))
    wide_lane = iota((per_block, LANES), 1)
    column_value = column[...]
    padded = key_cat.shape[0]
    chosen = jnp.concatenate(
        [(column_value == wide_lane + k * LANES).astype(f32).astype(bf16) for k in range(padded // LANES)], axis=1
    )
    if padded > all_rows:
        key_cat[all_rows:padded, :] = jnp.zeros((padded - all_rows, 2 * LANES), bf16)

    from_lane = iota((LANES, all_tokens), 0)
    token = iota((LANES, all_tokens), 1)
    spread_table[...] = (
        (from_lane == ((token >> block_bits) << tok_bits) + ((token & (per_block - 1)) >> 3)).astype(f32).astype(bf16)
    )
    caption_of = iota((all_tokens, LANES), 0)
    caption_lane = (caption_of >> block_bits) * (LANES // nc) + (caption_of & 7)
    caption_table[...] = (iota((all_tokens, LANES), 1) == caption_lane).astype(f32).astype(bf16)
    same_group = ((iota((LANES, LANES), 0) >> tok_bits) == (iota((LANES, LANES), 1) >> tok_bits)).astype(f32).astype(bf16)
    mine_of = (iota((SUB, all_tokens), 1) & 7) == iota((SUB, all_tokens), 0)

    def as_row(values):
        return jnp.sum(jnp.where(mine_of, values, 0.0), axis=0, keepdims=True)

    for copy in trades:
        copy.wait()
    q_full[me_f, own_rows, :] = trade[me_f, 0:SUB, :]

    @pl.loop(1, nv)
    def _(step):
        pltpu.make_async_remote_copy(
            src_ref=trade.at[me_f, pl.ds(0, SUB)], dst_ref=q_full.at[me_f, own_rows],
            send_sem=gather_send, recv_sem=gather_recv, device_id=device(0, step, 0), device_id_type=MESH,
        ).start()

    frames = jnp.zeros((SUB, LANES), f32)
    patch_all = jnp.zeros((SUB, LANES), f32)
    length = jnp.zeros((SUB, LANES), f32)
    for j in range(nc):
        here = group == j
        frames = jnp.where(here, pltpu.roll(trade[j, SUB : 2 * SUB, :], j * tok, 1), frames)
        patch_all = jnp.where(here, pltpu.roll(trade[j, 2 * SUB : 3 * SUB, :], j * tok, 1), patch_all)
        length = jnp.where(here, trade[j, 3 * SUB : 4 * SUB, :], length)
    frames = frames.astype(jnp.int32)
    live = (slot_in_group.astype(f32) < length) & used
    safe_length = jnp.maximum(length, 1.0)
    local = jnp.where(((frames >> 2) == me_f) & used, patch_all.astype(jnp.int32) * 4 + (frames & 3), 255)
    twice = jnp.concatenate([local.astype(f32), jnp.zeros((SUB, LANES), f32)], axis=0).astype(bf16)
    local_row = as_row(dot(twice, spread_table[...])[0:SUB]).astype(jnp.int32)
    one_hot[...] = (iota((rows, all_tokens), 0) == local_row).astype(f32).astype(bf16)

    for copy in key_copies:
        copy.wait()
    high, low = two_terms(keys[...])
    key_cat[0:all_rows, 0:LANES] = high
    key_cat[0:all_rows, LANES:] = low
    both = dot(chosen, key_cat[...])
    picked = both[:, 0:LANES] + both[:, LANES:]
    picked_rows[...] = picked

    all_but_one = pl.ds(0, (nv - 1) * SUB)
    pltpu.make_async_copy(q_pick.at[all_but_one], q_pick.at[all_but_one], pick_recv).wait()
    product = (picked * q_pick[...]).reshape(tok, SUB, LANES)

    when = iota((tok, SUB, LANES), 0).astype(f32)
    score = jnp.sum(jnp.sum(jnp.where(when < lengths[None], product, 0.0), axis=0), axis=1, keepdims=True)
    score = score * logit_scale / lengths
    me_16 = me_c * nf + me_f
    own_score = pl.ds(me_16, 1)
    line_out[0:1, :] = jnp.sum(jnp.where(lane == me_c * cap_lanes + sub, score, 0.0), axis=0, keepdims=True)
    scores_in[own_score, :] = line_out[0:1, :]

    @pl.loop(1, nc * nf)
    def _(step):
        pltpu.make_async_remote_copy(
            src_ref=line_out.at[0:1], dst_ref=scores_in.at[own_score], send_sem=score_send, recv_sem=score_recv,
            device_id=device(step // nf, 0, lax.rem(step, nf)), device_id_type=MESH,
        ).start()

    tile = jnp.zeros((SUB, LANES), f32)
    for t in range(tok):
        tile = jnp.where(lane == me_c * tok + t, jnp.sum(product[t], axis=1, keepdims=True), tile)
    tile_out[...] = tile
    tiles_in[me_16] = tile

    @pl.loop(1, nc * nf)
    def _(step):
        pltpu.make_async_remote_copy(
            src_ref=tile_out, dst_ref=tiles_in.at[me_16], send_sem=tile_send, recv_sem=tile_recv,
            device_id=device(step // nf, 0, lax.rem(step, nf)), device_id_type=MESH,
        ).start()

    rows_in[me_v] = picked_rows[own_rows, :]

    @pl.loop(1, nv)
    def _(step):
        to = lax.rem(me_v + step, nv)
        pltpu.make_async_remote_copy(
            src_ref=picked_rows.at[pl.ds(pl.multiple_of(to * SUB, SUB), SUB)], dst_ref=rows_in.at[me_v],
            send_sem=rows_send, recv_sem=rows_recv, device_id=device(0, step, 0), device_id_type=MESH,
        ).start()

    other_scores = scores_in.at[pl.ds(0, nc * nf - 1)]
    pltpu.make_async_copy(other_scores, other_scores, score_recv).wait()
    own_logits = jnp.sum(scores_in[...], axis=0, keepdims=True)
    line_out[1:2, :] = own_logits
    own_line = pl.ds(me_v, 1)
    logits_in[own_line, :] = own_logits

    @pl.loop(1, nv)
    def _(step):
        pltpu.make_async_remote_copy(
            src_ref=line_out.at[1:2], dst_ref=logits_in.at[own_line], send_sem=logit_send, recv_sem=logit_recv,
            device_id=device(0, step, 0), device_id_type=MESH,
        ).start()

    gathered = q_full.at[0, all_but_one]
    pltpu.make_async_copy(gathered, gathered, gather_recv).wait()

    def spread_copy(d):
        return pltpu.make_async_remote_copy(
            src_ref=q_full.at[me_f], dst_ref=q_full.at[me_f], send_sem=spread_send.at[d], recv_sem=spread_recv.at[d],
            device_id=device(0, 0, d), device_id_type=MESH,
        )

    spreads = [spread_copy(d) for d in range(1, nf)]
    for copy in spreads:
        copy.start()

    other_tiles = tiles_in.at[pl.ds(0, nc * nf - 1)]
    other_clips = rows_in.at[pl.ds(0, nv - 1)]
    pltpu.make_async_copy(other_tiles, other_tiles, tile_recv).wait()
    live_share = jnp.where(live, jnp.sum(tiles_in[...], axis=0), 0.0)
    share_row = as_row(times_exact(live_share / safe_length, spread_table[...]))
    share_high, share_low = two_terms(one_hot[...].astype(f32) * share_row)
    inner_table = dot(share_high, caption_table[...]) + dot(share_low, caption_table[...])
    pltpu.make_async_copy(other_clips, other_clips, rows_recv).wait()

    length_line = jnp.zeros((SUB, LANES), f32)
    for j in range(nc):
        length_line = jnp.where(lane == j * cap_lanes + sub, trade[j, 3 * SUB : 4 * SUB, :], length_line)
    inverse_length = 1.0 / jnp.maximum(jnp.sum(length_line, axis=0, keepdims=True), 1.0)
    clip_id = iota((nv, LANES), 0)
    line_lane = iota((nv, LANES), 1)
    valid = (line_lane & (cap_lanes - 1)) < SUB
    positive = valid & (clip_id == group_of(line_lane, cap_lanes) * SUB + (line_lane & (cap_lanes - 1)))
    positive = positive.astype(f32)

    other_logits = logits_in.at[pl.ds(0, nv - 1)]
    pltpu.make_async_copy(other_logits, other_logits, logit_recv).wait()
    logits = logits_in[...]
    exp_logits = jnp.where(valid, jnp.exp(logits), 0.0)
    row_total = jnp.where(in_line[0:1], jnp.sum(exp_logits, axis=0, keepdims=True), 1.0)
    col_total = jnp.sum(exp_logits, axis=1, keepdims=True)
    grad = logit_scale * (exp_logits * (0.5 / row_total + 0.5 / col_total) - positive)
    weights[...] = grad
    turned[...] = jnp.transpose(grad * inverse_length)

    block_weight = turned[pl.ds(pl.multiple_of(me_c * cap_lanes, SUB), SUB), :]
    slice_grad = jnp.zeros((SUB, LANES), f32)
    for v in range(nv):
        slice_grad = slice_grad + block_weight[:, v : v + 1] * rows_in[v]
    slice_grad = jnp.where(me_v.astype(f32) < lengths, slice_grad, 0.0)
    grad_out[...] = slice_grad
    grads_in[me_f] = slice_grad

    def grad_copy(d):
        return pltpu.make_async_remote_copy(
            src_ref=grad_out, dst_ref=grads_in.at[me_f], send_sem=grad_send.at[d], recv_sem=grad_recv.at[d],
            device_id=device(0, 0, d), device_id_type=MESH,
        )

    grad_copies = [grad_copy(d) for d in range(1, nf)]
    for copy in grad_copies:
        copy.start()

    own_grad = weights[own_line, :]
    own_weight = own_grad * inverse_length
    token_weight = [
        jnp.sum(jnp.where(lane == j * cap_lanes + sub, own_weight, 0.0), axis=1, keepdims=True) for j in range(nc)
    ]
    inner = jnp.sum(inner_table * own_grad, axis=1, keepdims=True)
    for copy in spreads:
        copy.wait()
    parts = []
    for j in range(nc):
        mask = when < trade[j, 3 * SUB : 4 * SUB, :][None]
        scaled = q_full[j].reshape(tok, SUB, LANES) * jnp.where(mask, token_weight[j][None], 0.0)
        parts.append(jnp.concatenate(two_terms(scaled.reshape(per_block, LANES)), axis=1))
    both = dot(one_hot[...], jnp.concatenate(parts, axis=0))
    clip_res[...] = key_inv[...] * (both[:, 0:LANES] + both[:, LANES:] - unit_keys[me_c] * inner)

    terms = 0.5 * jnp.sum(jnp.where(in_line[0:1], jnp.log(row_total), 0.0)) + 0.5 * jnp.sum(jnp.log(col_total))
    terms = terms - jnp.sum(positive * logits)
    loss_ref[...] = jnp.broadcast_to(terms / (nc * SUB), (1, 1))

    for copy in grad_copies:
        copy.wait()
    dot_tile = jnp.zeros((SUB, LANES), f32)
    for j in range(nc):
        dot_tile = dot_tile + qn[j] * grads_in[j]
    cap_inner = jnp.sum(dot_tile, axis=1, keepdims=True)
    for j in range(nc):
        cap_res[pl.ds(j, SUB, stride=nc), :] = cap_inv * (grads_in[j] - qn[j] * cap_inner)

    pltpu.make_async_copy(gathered, gathered, pick_send).wait()
    pltpu.make_async_copy(gathered, gathered, gather_send).wait()
    pltpu.make_async_copy(other_clips, other_clips, rows_send).wait()
    pltpu.make_async_copy(other_scores, other_scores, score_send).wait()
    pltpu.make_async_copy(other_logits, other_logits, logit_send).wait()
    pltpu.make_async_copy(other_tiles, other_tiles, tile_send).wait()


def body(nc, nv, cap_tokens, clip_tokens, win_frame, win_patch, cap_lengths):
    block, _, width = cap_tokens.shape
    _, frames, patches, _ = clip_tokens.shape
    assert block == SUB and frames == 4 and width == nc * LANES and win_frame.shape == (SUB, nv, 1)
    rows = frames * patches
    per_block = nv * SUB
    padded = -(-nc * rows // LANES) * LANES
    caps = cap_tokens.reshape(SUB * nc, LANES)
    clips = clip_tokens.reshape(frames, patches, nc, LANES).transpose(1, 2, 0, 3).reshape(patches, nc * frames, LANES)
    vmem = pltpu.VMEM
    dma = pltpu.SemaphoreType.DMA
    scratch = [
        vmem((SUB * nc, LANES), f32),
        vmem((patches, nc * frames, LANES), f32),
        vmem((SUB, nv), jnp.int32),
        vmem((SUB, nv), jnp.int32),
        vmem((nc, SUB, LANES), f32),
        vmem((nc, 4 * SUB, LANES), f32),
        vmem((nc, 4 * SUB, LANES), f32),
        vmem((nc, per_block, LANES), f32),
        vmem((per_block, LANES), f32),
        vmem((nc, rows, LANES), f32),
        vmem((nc * rows, LANES), f32),
        vmem((rows, LANES), f32),
        vmem((padded, 2 * LANES), bf16),
        vmem((per_block, LANES), jnp.int32),
        vmem((per_block, LANES), f32),
        vmem((nv, SUB, LANES), f32),
        vmem((nc * nc, SUB, LANES), f32),
        vmem((nc * nc, LANES), f32),
        vmem((nv, LANES), f32),
        vmem((SUB, LANES), f32),
        vmem((SUB, LANES), f32),
        vmem((nv, LANES), f32),
        vmem((LANES, nv), f32),
        vmem((nc, SUB, LANES), f32),
        vmem((SUB, LANES), f32),
        vmem((LANES, nc * per_block), bf16),
        vmem((nc * per_block, LANES), bf16),
        vmem((rows, nc * per_block), bf16),
        vmem((1, SUB), jnp.int32),
        dma((5,)),
        dma((nc,)), dma((nc,)), dma((nc,)), dma((nc,)),
        dma, dma, dma, dma,
        dma((nc,)), dma((nc,)),
        dma, dma, dma, dma, dma, dma, dma, dma,
        dma((nc,)), dma((nc,)),
    ]
    hbm = pl.BlockSpec(memory_space=pl.ANY)
    near = pl.BlockSpec(memory_space=pltpu.VMEM)
    in_hbm = functools.partial(pltpu.with_memory_space_constraint, memory_space=pltpu.HBM)
    operands = (caps, clips, win_frame.reshape(SUB, nv), win_patch.reshape(SUB, nv), cap_lengths.reshape(1, SUB))
    shapes = ((1, 1), (SUB * nc, LANES), (rows, LANES))
    loss, cap_grad, clip_grad = pl.pallas_call(
        functools.partial(kernel, nc, nv, patches),
        out_shape=[vmem(shape, f32) for shape in shapes],
        in_specs=[hbm] * 5,
        out_specs=[near] * 3,
        scratch_shapes=scratch,
        compiler_params=pltpu.CompilerParams(
            collective_id=0, has_side_effects=True, vmem_limit_bytes=32 * 1024 * 1024
        ),
    )(*map(in_hbm, operands))
    clip_grad = clip_grad.reshape(patches, frames, LANES).transpose(1, 0, 2)[None]
    return loss.reshape(()), cap_grad.reshape(SUB, 1, width), clip_grad


def solution(mesh):
    placed = (
        P("cap", "clip", None),
        P("clip", "frame", None, None),
        P("cap", None, "clip"),
        P("cap", None, "clip"),
        P("cap"),
    )
    assert mesh.shape["cap"] == mesh.shape["frame"]
    return jax.shard_map(
        functools.partial(body, mesh.shape["cap"], mesh.shape["clip"]),
        mesh=mesh,
        in_specs=placed,
        out_specs=(P(), P("cap", "clip", None), P("clip", "frame", None, "cap")),
        check_vma=False,
    )
```

```python
import functools

import jax
import jax.numpy as jnp
from jax import lax
from jax.experimental import pallas as pl
from jax.experimental.pallas import tpu as pltpu
from jax.sharding import PartitionSpec as P

MESH = pl.DeviceIdType.MESH
logit_scale = 1.0 / 0.07
norm_eps = 1e-06
f32 = jnp.float32
bf16 = jnp.bfloat16
LANES = 128
SUB = 8


def iota(shape, dim):
    return lax.broadcasted_iota(jnp.int32, shape, dim)


def two_terms(x):
    high = x.astype(bf16)
    return high, (x - high.astype(f32)).astype(bf16)


def three_terms(x):
    high = x.astype(bf16).astype(f32)
    rest = x - high
    middle = rest.astype(bf16).astype(f32)
    return high, middle, rest - middle


def dot(a, b):
    return jnp.dot(a, b, preferred_element_type=f32)


def times_exact(tile, table):
    high, middle, low = three_terms(tile)
    stacked = jnp.concatenate([high, middle, low, jnp.zeros_like(high)], axis=0).astype(bf16)
    out = dot(stacked, table)
    return out[0:SUB] + out[SUB : 2 * SUB] + out[2 * SUB : 3 * SUB]


def group_of(lane, size):
    return lane >> log2(size)


def log2(n):
    assert n & (n - 1) == 0
    return n.bit_length() - 1


def kernel(
    nc, nv, patches,
    cap_ref, clip_ref, wf_ref, wp_ref, len_ref,
    loss_ref, cap_res, clip_res,
    cap_raw, clip_raw, wf_raw, wp_raw, qn, give, trade, q_full, q_pick, unit_keys, keys, key_inv, key_cat, column,
    picked_rows, rows_in, tiles_in, scores_in, logits_in, tile_out, line_out, lines_out, weights, turned, grads_in, grad_out, spread_table, caption_table, one_hot,
    len_raw,
    load_sem, trade_send, trade_recv, key_send, key_recv, pick_send, pick_recv, gather_send, gather_recv,
    spread_send, spread_recv, rows_send, rows_recv, tile_send, tile_recv, score_send, score_recv, logit_send, logit_recv, grad_send, grad_recv,
):
    nf = nc
    tok = nv
    me_c, me_v, me_f = lax.axis_index("cap"), lax.axis_index("clip"), lax.axis_index("frame")
    rows = 4 * patches
    all_rows = nf * rows
    per_block = tok * SUB
    all_tokens = nf * per_block
    tok_bits, block_bits = log2(tok), log2(per_block)

    half_clips, side_rows = nv // 2, nv // 4
    me_half, me_side = me_v // half_clips, lax.rem(me_v, 2)
    me_row = lax.rem(me_v, half_clips) // 2
    me_corner = me_half * 2 + me_side
    others_in_row, others_in_corner = nf * side_rows - 1, nc * 4 - 1

    loads = [
        pltpu.make_async_copy(clip_ref, clip_raw, load_sem.at[0]),
        pltpu.make_async_copy(cap_ref, cap_raw, load_sem.at[1]),
        pltpu.make_async_copy(wf_ref, wf_raw, load_sem.at[2]),
        pltpu.make_async_copy(wp_ref, wp_raw, load_sem.at[3]),
        pltpu.make_async_copy(len_ref, len_raw, load_sem.at[4]),
    ]
    for load in loads:
        load.start()

    barrier = pltpu.get_barrier_semaphore()

    def device(dc, dv, df):
        return {
            "cap": lax.rem(me_c + dc, nc),
            "clip": lax.rem(me_v + dv, nv),
            "frame": lax.rem(me_f + df, nf),
        }

    def signal(dc, dv, df):
        pl.semaphore_signal(barrier, inc=1, device_id=device(dc, dv, df), device_id_type=MESH)

    @pl.loop(1, nc * nf)
    def _(step):
        signal(step // nf, 0, lax.rem(step, nf))

    @pl.loop(1, nv)
    def _(step):
        signal(0, step, 0)

    lane = iota((SUB, LANES), 1)
    sub = iota((SUB, LANES), 0)
    group = lane >> tok_bits
    slot_in_group = lane & (tok - 1)
    used = group < nc
    cap_lanes = LANES // nc
    in_line = (lane & (cap_lanes - 1)) < SUB

    loads[1].wait()
    raw = [cap_raw[pl.ds(j, SUB, stride=nc), :] for j in range(nc)]
    total = raw[0] * raw[0]
    for j in range(1, nc):
        total = total + raw[j] * raw[j]
    cap_inv = lax.rsqrt(jnp.sum(total, axis=1, keepdims=True) + norm_eps)
    for j in range(nc):
        unit = raw[j] * cap_inv
        qn[j] = unit
        give[j, 0:SUB, :] = unit

    loads[0].wait()
    whole = clip_raw[...].reshape(patches, nc // 2, SUB, LANES)
    square = whole * whole
    summed = square[:, 0]
    for j in range(1, nc // 2):
        summed = summed + square[:, j]
    summed = summed + pltpu.roll(summed, 4, 1)
    inverse = lax.rsqrt(jnp.sum(summed, axis=2, keepdims=True) + norm_eps)
    low_half = iota((patches // 2, SUB, LANES), 1) < 4
    for j in range(nc // 2):
        unit = (whole[:, j] * inverse).reshape(patches // 2, 2, SUB, LANES)
        first, second = unit[:, 0], unit[:, 1]
        unit_keys[2 * j] = jnp.where(low_half, first, pltpu.roll(second, 4, 1)).reshape(rows, LANES)
        unit_keys[2 * j + 1] = jnp.where(low_half, pltpu.roll(first, 4, 1), second).reshape(rows, LANES)
    inverse = jnp.broadcast_to(inverse, (patches, SUB, LANES)).reshape(patches // 2, 2, SUB, LANES)
    key_inv[...] = jnp.where(low_half, inverse[:, 0], inverse[:, 1]).reshape(rows, LANES)

    pl.semaphore_wait(barrier, nc * nf - 1 + nv - 1)

    own_key_rows = pl.ds(pl.multiple_of(me_f * rows, SUB), rows)
    own_rows = pl.ds(pl.multiple_of(me_v * SUB, SUB), SUB)

    def key_copy(d):
        return pltpu.make_async_remote_copy(
            src_ref=unit_keys.at[lax.rem(me_f + d, nf)], dst_ref=keys.at[own_key_rows],
            send_sem=key_send.at[d], recv_sem=key_recv.at[d], device_id=device(0, 0, d), device_id_type=MESH,
        )

    key_copies = [key_copy(d) for d in range(1, nf)]
    for copy in key_copies:
        copy.start()

    @pl.loop(1, nv)
    def _(step):
        pltpu.make_async_remote_copy(
            src_ref=qn.at[me_f], dst_ref=q_pick.at[own_rows],
            send_sem=pick_send, recv_sem=pick_recv, device_id=device(0, step, 0), device_id_type=MESH,
        ).start()

    for load in loads[2:]:
        load.wait()
    diagonal = iota((SUB, SUB), 0) == iota((SUB, SUB), 1)
    lengths = jnp.sum(jnp.where(diagonal, len_raw[...].astype(f32), 0.0), axis=1, keepdims=True)
    lengths = jnp.broadcast_to(lengths, (SUB, LANES))
    give[:, SUB : 3 * SUB, :] = jnp.zeros((nc, 2 * SUB, LANES), f32)
    for j in range(nc):
        give[j, SUB : 2 * SUB, 0:tok] = wf_raw[...].astype(f32)
        give[j, 2 * SUB : 3 * SUB, 0:tok] = wp_raw[...].astype(f32)
        give[j, 3 * SUB : 4 * SUB, :] = lengths

    def trade_copy(d):
        to = lax.rem(me_c + d, nc)
        return pltpu.make_async_remote_copy(
            src_ref=give.at[to], dst_ref=trade.at[me_c], send_sem=trade_send.at[d], recv_sem=trade_recv.at[d],
            device_id=device(d, 0, 0), device_id_type=MESH,
        )

    trades = [trade_copy(d) for d in range(1, nc)]
    for copy in trades:
        copy.start()
    trade[me_c] = give[me_c]
    keys[own_key_rows, :] = unit_keys[me_f]
    q_pick[own_rows, :] = qn[me_f]

    frame_own = wf_raw[...]
    winner = (frame_own >> 2) * rows + wp_raw[...] * 4 + (frame_own & 3)
    for t in range(tok):
        column[t * SUB : (t + 1) * SUB, :] = jnp.broadcast_to(winner[:, t : t + 1], (SUB, LANES))
    wide_lane = iota((per_block, LANES), 1)
    column_value = column[...]
    padded = key_cat.shape[0]
    chosen = jnp.concatenate(
        [(column_value == wide_lane + k * LANES).astype(f32).astype(bf16) for k in range(padded // LANES)], axis=1
    )
    if padded > all_rows:
        key_cat[all_rows:padded, :] = jnp.zeros((padded - all_rows, 2 * LANES), bf16)

    from_lane = iota((LANES, all_tokens), 0)
    token = iota((LANES, all_tokens), 1)
    spread_table[...] = (
        (from_lane == ((token >> block_bits) << tok_bits) + ((token & (per_block - 1)) >> 3)).astype(f32).astype(bf16)
    )
    caption_of = iota((all_tokens, LANES), 0)
    caption_lane = (caption_of >> block_bits) * (LANES // nc) + (caption_of & 7)
    caption_table[...] = (iota((all_tokens, LANES), 1) == caption_lane).astype(f32).astype(bf16)
    same_group = ((iota((LANES, LANES), 0) >> tok_bits) == (iota((LANES, LANES), 1) >> tok_bits)).astype(f32).astype(bf16)
    mine_of = (iota((SUB, all_tokens), 1) & 7) == iota((SUB, all_tokens), 0)

    def as_row(values):
        return jnp.sum(jnp.where(mine_of, values, 0.0), axis=0, keepdims=True)

    for copy in trades:
        copy.wait()
    q_full[me_f, own_rows, :] = trade[me_f, 0:SUB, :]

    @pl.loop(1, nv)
    def _(step):
        pltpu.make_async_remote_copy(
            src_ref=trade.at[me_f, pl.ds(0, SUB)], dst_ref=q_full.at[me_f, own_rows],
            send_sem=gather_send, recv_sem=gather_recv, device_id=device(0, step, 0), device_id_type=MESH,
        ).start()

    frames = jnp.zeros((SUB, LANES), f32)
    patch_all = jnp.zeros((SUB, LANES), f32)
    length = jnp.zeros((SUB, LANES), f32)
    for j in range(nc):
        here = group == j
        frames = jnp.where(here, pltpu.roll(trade[j, SUB : 2 * SUB, :], j * tok, 1), frames)
        patch_all = jnp.where(here, pltpu.roll(trade[j, 2 * SUB : 3 * SUB, :], j * tok, 1), patch_all)
        length = jnp.where(here, trade[j, 3 * SUB : 4 * SUB, :], length)
    frames = frames.astype(jnp.int32)
    live = (slot_in_group.astype(f32) < length) & used
    safe_length = jnp.maximum(length, 1.0)
    local = jnp.where(((frames >> 2) == me_f) & used, patch_all.astype(jnp.int32) * 4 + (frames & 3), 255)
    twice = jnp.concatenate([local.astype(f32), jnp.zeros((SUB, LANES), f32)], axis=0).astype(bf16)
    local_row = as_row(dot(twice, spread_table[...])[0:SUB]).astype(jnp.int32)
    one_hot[...] = (iota((rows, all_tokens), 0) == local_row).astype(f32).astype(bf16)

    for copy in key_copies:
        copy.wait()
    high, low = two_terms(keys[...])
    key_cat[0:all_rows, 0:LANES] = high
    key_cat[0:all_rows, LANES:] = low
    both = dot(chosen, key_cat[...])
    picked = both[:, 0:LANES] + both[:, LANES:]
    picked_rows[...] = picked

    all_but_one = pl.ds(0, (nv - 1) * SUB)
    pltpu.make_async_copy(q_pick.at[all_but_one], q_pick.at[all_but_one], pick_recv).wait()
    product = (picked * q_pick[...]).reshape(tok, SUB, LANES)

    when = iota((tok, SUB, LANES), 0).astype(f32)
    score = jnp.sum(jnp.sum(jnp.where(when < lengths[None], product, 0.0), axis=0), axis=1, keepdims=True)
    score = score * logit_scale / lengths
    own_score = pl.ds(me_f * side_rows + me_row, 1)
    line_out[...] = jnp.sum(jnp.where(lane == me_c * cap_lanes + sub, score, 0.0), axis=0, keepdims=True)
    scores_in[own_score, :] = line_out[...]

    @pl.loop(1, nf * side_rows)
    def _(step):
        to_row = lax.rem(me_row + step // nf, side_rows)
        to = {
            "cap": me_c,
            "clip": me_half * half_clips + to_row * 2 + me_side,
            "frame": lax.rem(me_f + lax.rem(step, nf), nf),
        }
        pltpu.make_async_remote_copy(
            src_ref=line_out, dst_ref=scores_in.at[own_score], send_sem=score_send, recv_sem=score_recv,
            device_id=to, device_id_type=MESH,
        ).start()

    tile = jnp.zeros((SUB, LANES), f32)
    for t in range(tok):
        tile = jnp.where(lane == me_c * tok + t, jnp.sum(product[t], axis=1, keepdims=True), tile)
    tile_out[...] = tile
    me_16 = me_c * nf + me_f
    tiles_in[me_16] = tile

    @pl.loop(1, nc * nf)
    def _(step):
        pltpu.make_async_remote_copy(
            src_ref=tile_out, dst_ref=tiles_in.at[me_16], send_sem=tile_send, recv_sem=tile_recv,
            device_id=device(step // nf, 0, lax.rem(step, nf)), device_id_type=MESH,
        ).start()

    rows_in[me_v] = picked_rows[own_rows, :]

    @pl.loop(1, nv)
    def _(step):
        to = lax.rem(me_v + step, nv)
        pltpu.make_async_remote_copy(
            src_ref=picked_rows.at[pl.ds(pl.multiple_of(to * SUB, SUB), SUB)], dst_ref=rows_in.at[me_v],
            send_sem=rows_send, recv_sem=rows_recv, device_id=device(0, step, 0), device_id_type=MESH,
        ).start()

    other_scores = scores_in.at[pl.ds(0, others_in_row)]
    pltpu.make_async_copy(other_scores, other_scores, score_recv).wait()
    column_logits = scores_in[0:side_rows, :]
    for j in range(1, nf):
        column_logits = column_logits + scores_in[j * side_rows : (j + 1) * side_rows, :]
    lines_out[...] = column_logits
    own_slot = me_c * 4 + me_corner
    logits_in[own_slot] = column_logits

    @pl.loop(1, nc * 4)
    def _(step):
        corner = lax.rem(step, 4)
        to_half, to_side = lax.rem(me_half + corner // 2, 2), lax.rem(me_side + lax.rem(corner, 2), 2)
        to = {
            "cap": lax.rem(me_c + step // 4, nc),
            "clip": to_half * half_clips + me_row * 2 + to_side,
            "frame": me_f,
        }
        pltpu.make_async_remote_copy(
            src_ref=lines_out, dst_ref=logits_in.at[own_slot], send_sem=logit_send, recv_sem=logit_recv,
            device_id=to, device_id_type=MESH,
        ).start()

    gathered = q_full.at[0, all_but_one]
    pltpu.make_async_copy(gathered, gathered, gather_recv).wait()

    def spread_copy(d):
        return pltpu.make_async_remote_copy(
            src_ref=q_full.at[me_f], dst_ref=q_full.at[me_f], send_sem=spread_send.at[d], recv_sem=spread_recv.at[d],
            device_id=device(0, 0, d), device_id_type=MESH,
        )

    spreads = [spread_copy(d) for d in range(1, nf)]
    for copy in spreads:
        copy.start()

    other_tiles = tiles_in.at[pl.ds(0, nc * nf - 1)]
    other_clips = rows_in.at[pl.ds(0, nv - 1)]
    pltpu.make_async_copy(other_tiles, other_tiles, tile_recv).wait()
    live_share = jnp.where(live, jnp.sum(tiles_in[...], axis=0), 0.0)
    share_row = as_row(times_exact(live_share / safe_length, spread_table[...]))
    share_high, share_low = two_terms(one_hot[...].astype(f32) * share_row)
    inner_table = dot(share_high, caption_table[...]) + dot(share_low, caption_table[...])
    pltpu.make_async_copy(other_clips, other_clips, rows_recv).wait()

    length_line = jnp.zeros((SUB, LANES), f32)
    for j in range(nc):
        length_line = jnp.where(lane == j * cap_lanes + sub, trade[j, 3 * SUB : 4 * SUB, :], length_line)
    inverse_length = 1.0 / jnp.maximum(jnp.sum(length_line, axis=0, keepdims=True), 1.0)
    place = iota((nv, LANES), 0)
    corner, row = group_of(place, side_rows), place & (side_rows - 1)
    clip_id = (corner >> 1) * half_clips + row * 2 + (corner & 1)
    line_lane = iota((nv, LANES), 1)
    valid = (line_lane & (cap_lanes - 1)) < SUB
    positive = valid & (clip_id == group_of(line_lane, cap_lanes) * SUB + (line_lane & (cap_lanes - 1)))
    positive = positive.astype(f32)

    other_logits = logits_in.at[pl.ds(0, others_in_corner)]
    pltpu.make_async_copy(other_logits, other_logits, logit_recv).wait()
    logits = logits_in[0:4]
    for j in range(1, nc):
        logits = logits + logits_in[4 * j : 4 * j + 4]
    logits = logits.reshape(nv, LANES)
    exp_logits = jnp.where(valid, jnp.exp(logits), 0.0)
    row_total = jnp.where(in_line[0:1], jnp.sum(exp_logits, axis=0, keepdims=True), 1.0)
    col_total = jnp.sum(exp_logits, axis=1, keepdims=True)
    grad = logit_scale * (exp_logits * (0.5 / row_total + 0.5 / col_total) - positive)
    weights[...] = grad
    turned[...] = jnp.transpose(grad * inverse_length)

    block_weight = turned[pl.ds(pl.multiple_of(me_c * cap_lanes, SUB), SUB), :]
    slice_grad = jnp.zeros((SUB, LANES), f32)
    for v in range(nv):
        at = (v // half_clips * 2 + v % 2) * side_rows + v % half_clips // 2
        slice_grad = slice_grad + block_weight[:, at : at + 1] * rows_in[v]
    slice_grad = jnp.where(me_v.astype(f32) < lengths, slice_grad, 0.0)
    grad_out[...] = slice_grad
    grads_in[me_f] = slice_grad

    def grad_copy(d):
        return pltpu.make_async_remote_copy(
            src_ref=grad_out, dst_ref=grads_in.at[me_f], send_sem=grad_send.at[d], recv_sem=grad_recv.at[d],
            device_id=device(0, 0, d), device_id_type=MESH,
        )

    grad_copies = [grad_copy(d) for d in range(1, nf)]
    for copy in grad_copies:
        copy.start()

    own_grad = weights[pl.ds(me_corner * side_rows + me_row, 1), :]
    own_weight = own_grad * inverse_length
    token_weight = [
        jnp.sum(jnp.where(lane == j * cap_lanes + sub, own_weight, 0.0), axis=1, keepdims=True) for j in range(nc)
    ]
    inner = jnp.sum(inner_table * own_grad, axis=1, keepdims=True)
    for copy in spreads:
        copy.wait()
    parts = []
    for j in range(nc):
        mask = when < trade[j, 3 * SUB : 4 * SUB, :][None]
        scaled = q_full[j].reshape(tok, SUB, LANES) * jnp.where(mask, token_weight[j][None], 0.0)
        parts.append(jnp.concatenate(two_terms(scaled.reshape(per_block, LANES)), axis=1))
    both = dot(one_hot[...], jnp.concatenate(parts, axis=0))
    clip_res[...] = key_inv[...] * (both[:, 0:LANES] + both[:, LANES:] - unit_keys[me_c] * inner)

    terms = 0.5 * jnp.sum(jnp.where(in_line[0:1], jnp.log(row_total), 0.0)) + 0.5 * jnp.sum(jnp.log(col_total))
    terms = terms - jnp.sum(positive * logits)
    loss_ref[...] = jnp.broadcast_to(terms / (nc * SUB), (1, 1))

    for copy in grad_copies:
        copy.wait()
    dot_tile = jnp.zeros((SUB, LANES), f32)
    for j in range(nc):
        dot_tile = dot_tile + qn[j] * grads_in[j]
    cap_inner = jnp.sum(dot_tile, axis=1, keepdims=True)
    for j in range(nc):
        cap_res[pl.ds(j, SUB, stride=nc), :] = cap_inv * (grads_in[j] - qn[j] * cap_inner)

    pltpu.make_async_copy(gathered, gathered, pick_send).wait()
    pltpu.make_async_copy(gathered, gathered, gather_send).wait()
    pltpu.make_async_copy(other_clips, other_clips, rows_send).wait()
    pltpu.make_async_copy(other_scores, other_scores, score_send).wait()
    pltpu.make_async_copy(other_logits, other_logits, logit_send).wait()
    pltpu.make_async_copy(other_tiles, other_tiles, tile_send).wait()


def body(nc, nv, cap_tokens, clip_tokens, win_frame, win_patch, cap_lengths):
    block, _, width = cap_tokens.shape
    _, frames, patches, _ = clip_tokens.shape
    assert block == SUB and frames == 4 and width == nc * LANES and win_frame.shape == (SUB, nv, 1)
    rows = frames * patches
    per_block = nv * SUB
    padded = -(-nc * rows // LANES) * LANES
    caps = cap_tokens.reshape(SUB * nc, LANES)
    clips = clip_tokens.reshape(frames, patches, nc, LANES).transpose(1, 2, 0, 3).reshape(patches, nc * frames, LANES)
    vmem = pltpu.VMEM
    dma = pltpu.SemaphoreType.DMA
    scratch = [
        vmem((SUB * nc, LANES), f32),
        vmem((patches, nc * frames, LANES), f32),
        vmem((SUB, nv), jnp.int32),
        vmem((SUB, nv), jnp.int32),
        vmem((nc, SUB, LANES), f32),
        vmem((nc, 4 * SUB, LANES), f32),
        vmem((nc, 4 * SUB, LANES), f32),
        vmem((nc, per_block, LANES), f32),
        vmem((per_block, LANES), f32),
        vmem((nc, rows, LANES), f32),
        vmem((nc * rows, LANES), f32),
        vmem((rows, LANES), f32),
        vmem((padded, 2 * LANES), bf16),
        vmem((per_block, LANES), jnp.int32),
        vmem((per_block, LANES), f32),
        vmem((nv, SUB, LANES), f32),
        vmem((nc * nc, SUB, LANES), f32),
        vmem((nc * nv // 4, LANES), f32),
        vmem((nc * 4, nv // 4, LANES), f32),
        vmem((SUB, LANES), f32),
        vmem((1, LANES), f32),
        vmem((nv // 4, LANES), f32),
        vmem((nv, LANES), f32),
        vmem((LANES, nv), f32),
        vmem((nc, SUB, LANES), f32),
        vmem((SUB, LANES), f32),
        vmem((LANES, nc * per_block), bf16),
        vmem((nc * per_block, LANES), bf16),
        vmem((rows, nc * per_block), bf16),
        vmem((1, SUB), jnp.int32),
        dma((5,)),
        dma((nc,)), dma((nc,)), dma((nc,)), dma((nc,)),
        dma, dma, dma, dma,
        dma((nc,)), dma((nc,)),
        dma, dma, dma, dma, dma, dma, dma, dma,
        dma((nc,)), dma((nc,)),
    ]
    hbm = pl.BlockSpec(memory_space=pl.ANY)
    near = pl.BlockSpec(memory_space=pltpu.VMEM)
    in_hbm = functools.partial(pltpu.with_memory_space_constraint, memory_space=pltpu.HBM)
    operands = (caps, clips, win_frame.reshape(SUB, nv), win_patch.reshape(SUB, nv), cap_lengths.reshape(1, SUB))
    shapes = ((1, 1), (SUB * nc, LANES), (rows, LANES))
    loss, cap_grad, clip_grad = pl.pallas_call(
        functools.partial(kernel, nc, nv, patches),
        out_shape=[vmem(shape, f32) for shape in shapes],
        in_specs=[hbm] * 5,
        out_specs=[near] * 3,
        scratch_shapes=scratch,
        compiler_params=pltpu.CompilerParams(
            collective_id=0, has_side_effects=True, vmem_limit_bytes=32 * 1024 * 1024
        ),
    )(*map(in_hbm, operands))
    clip_grad = clip_grad.reshape(patches, frames, LANES).transpose(1, 0, 2)[None]
    return loss.reshape(()), cap_grad.reshape(SUB, 1, width), clip_grad


def solution(mesh):
    placed = (
        P("cap", "clip", None),
        P("clip", "frame", None, None),
        P("cap", None, "clip"),
        P("cap", None, "clip"),
        P("cap"),
    )
    assert mesh.shape["cap"] == mesh.shape["frame"]
    return jax.shard_map(
        functools.partial(body, mesh.shape["cap"], mesh.shape["clip"]),
        mesh=mesh,
        in_specs=placed,
        out_specs=(P(), P("cap", "clip", None), P("clip", "frame", None, "cap")),
        check_vma=False,
    )
```

```python
import functools

import jax
import jax.numpy as jnp
from jax import lax
from jax.experimental import pallas as pl
from jax.experimental.pallas import tpu as pltpu
from jax.sharding import PartitionSpec as P

MESH = pl.DeviceIdType.MESH
logit_scale = 1.0 / 0.07
norm_eps = 1e-06
f32 = jnp.float32
bf16 = jnp.bfloat16
LANES = 128
SUB = 8


def iota(shape, dim):
    return lax.broadcasted_iota(jnp.int32, shape, dim)


def two_terms(x):
    high = x.astype(bf16)
    return high, (x - high.astype(f32)).astype(bf16)


def three_terms(x):
    high = x.astype(bf16).astype(f32)
    rest = x - high
    middle = rest.astype(bf16).astype(f32)
    return high, middle, rest - middle


def dot(a, b):
    return jnp.dot(a, b, preferred_element_type=f32)


def times_exact(tile, table):
    high, middle, low = three_terms(tile)
    stacked = jnp.concatenate([high, middle, low, jnp.zeros_like(high)], axis=0).astype(bf16)
    out = dot(stacked, table)
    return out[0:SUB] + out[SUB : 2 * SUB] + out[2 * SUB : 3 * SUB]


def group_of(lane, size):
    return lane >> log2(size)


def log2(n):
    assert n & (n - 1) == 0
    return n.bit_length() - 1


def kernel(
    nc, nv, patches,
    cap_ref, clip_ref, wf_ref, wp_ref, len_ref,
    loss_ref, cap_res, clip_res,
    cap_raw, clip_raw, wf_raw, wp_raw, qn, give, trade, q_full, q_pick, unit_keys, keys, key_inv, column,
    picked_rows, rows_in, tiles_in, scores_in, logits_in, tile_out, line_out, lines_out, weights, turned, grads_in, grad_out, spread_table, caption_table, one_hot,
    len_raw,
    load_sem, trade_send, trade_recv, key_send, key_recv, pick_send, pick_recv, gather_send, gather_recv,
    spread_send, spread_recv, rows_send, rows_recv, tile_send, tile_recv, score_send, score_recv, logit_send, logit_recv, grad_send, grad_recv,
):
    nf = nc
    tok = nv
    me_c, me_v, me_f = lax.axis_index("cap"), lax.axis_index("clip"), lax.axis_index("frame")
    rows = 4 * patches
    per_block = tok * SUB
    all_tokens = nf * per_block
    tok_bits, block_bits = log2(tok), log2(per_block)

    half_clips, side_rows = nv // 2, nv // 4
    me_half, me_side = me_v // half_clips, lax.rem(me_v, 2)
    me_row = lax.rem(me_v, half_clips) // 2
    me_corner = me_half * 2 + me_side
    others_in_row, others_in_corner = nf * side_rows - 1, nc * 4 - 1

    loads = [
        pltpu.make_async_copy(clip_ref, clip_raw, load_sem.at[0]),
        pltpu.make_async_copy(cap_ref, cap_raw, load_sem.at[1]),
        pltpu.make_async_copy(wf_ref, wf_raw, load_sem.at[2]),
        pltpu.make_async_copy(wp_ref, wp_raw, load_sem.at[3]),
        pltpu.make_async_copy(len_ref, len_raw, load_sem.at[4]),
    ]
    barrier = pltpu.get_barrier_semaphore()

    def device(dc, dv, df):
        return {
            "cap": lax.rem(me_c + dc, nc),
            "clip": lax.rem(me_v + dv, nv),
            "frame": lax.rem(me_f + df, nf),
        }

    def signal(dc, dv, df):
        pl.semaphore_signal(barrier, inc=1, device_id=device(dc, dv, df), device_id_type=MESH)

    def at_clip(clip):
        return {"cap": me_c, "clip": clip, "frame": me_f}

    across = lax.rem(me_v + half_clips, nv)
    in_half = [me_half * half_clips + lax.rem(me_v + step, half_clips) for step in range(1, half_clips)]
    pl.semaphore_signal(barrier, inc=1, device_id=at_clip(across), device_id_type=MESH)
    for clip in in_half:
        pl.semaphore_signal(barrier, inc=1, device_id=at_clip(clip), device_id_type=MESH)
    for load in loads:
        load.start()
    for step in range(1, nf):
        signal(0, 0, step)
    for step in range(1, nc):
        signal(step, 0, 0)

    lane = iota((SUB, LANES), 1)
    sub = iota((SUB, LANES), 0)
    group = lane >> tok_bits
    slot_in_group = lane & (tok - 1)
    used = group < nc
    cap_lanes = LANES // nc
    in_line = (lane & (cap_lanes - 1)) < SUB

    loads[1].wait()
    raw = [cap_raw[pl.ds(j, SUB, stride=nc), :] for j in range(nc)]
    total = raw[0] * raw[0]
    for j in range(1, nc):
        total = total + raw[j] * raw[j]
    cap_inv = lax.rsqrt(jnp.sum(total, axis=1, keepdims=True) + norm_eps)
    for j in range(nc):
        unit = raw[j] * cap_inv
        qn[j] = unit
        give[j, 0:SUB, :] = unit

    for load in loads[2:]:
        load.wait()
    diagonal = iota((SUB, SUB), 0) == iota((SUB, SUB), 1)
    lengths = jnp.sum(jnp.where(diagonal, len_raw[...].astype(f32), 0.0), axis=1, keepdims=True)
    lengths = jnp.broadcast_to(lengths, (SUB, LANES))
    give[:, SUB : 3 * SUB, :] = jnp.zeros((nc, 2 * SUB, LANES), f32)
    for j in range(nc):
        give[j, SUB : 2 * SUB, 0:tok] = wf_raw[...].astype(f32)
        give[j, 2 * SUB : 3 * SUB, 0:tok] = wp_raw[...].astype(f32)
        give[j, 3 * SUB : 4 * SUB, :] = lengths

    pl.semaphore_wait(barrier, nc - 1 + nf - 1 + half_clips)

    own_rows = pl.ds(pl.multiple_of(me_v * SUB, SUB), SUB)

    def pick_copy(src, place, clip, sem):
        return pltpu.make_async_remote_copy(
            src_ref=src, dst_ref=q_pick.at[place], send_sem=pick_send.at[sem], recv_sem=pick_recv.at[sem],
            device_id=at_clip(clip), device_id_type=MESH,
        )

    across_copy = pick_copy(qn.at[me_f], own_rows, across, 0)
    across_copy.start()
    for clip in in_half:
        pick_copy(qn.at[me_f], own_rows, clip, 1).start()

    def trade_copy(d):
        to = lax.rem(me_c + d, nc)
        return pltpu.make_async_remote_copy(
            src_ref=give.at[to], dst_ref=trade.at[me_c], send_sem=trade_send.at[d], recv_sem=trade_recv.at[d],
            device_id=device(d, 0, 0), device_id_type=MESH,
        )

    trades = [trade_copy(d) for d in range(1, nc)]
    for copy in trades:
        copy.start()

    keys[:, rows:, :] = jnp.zeros((nf, keys.shape[1] - rows, LANES), f32)
    loads[0].wait()
    whole = clip_raw[...].reshape(patches, nc // 2, SUB, LANES)
    square = whole * whole
    summed = square[:, 0]
    for j in range(1, nc // 2):
        summed = summed + square[:, j]
    summed = summed + pltpu.roll(summed, 4, 1)
    inverse = lax.rsqrt(jnp.sum(summed, axis=2, keepdims=True) + norm_eps)
    low_half = iota((patches // 2, SUB, LANES), 1) < 4
    for j in range(nc // 2):
        unit = (whole[:, j] * inverse).reshape(patches // 2, 2, SUB, LANES)
        first, second = unit[:, 0], unit[:, 1]
        unit_keys[2 * j] = jnp.where(low_half, first, pltpu.roll(second, 4, 1)).reshape(rows, LANES)
        unit_keys[2 * j + 1] = jnp.where(low_half, pltpu.roll(first, 4, 1), second).reshape(rows, LANES)
    inverse = jnp.broadcast_to(inverse, (patches, SUB, LANES)).reshape(patches // 2, 2, SUB, LANES)
    key_inv[...] = jnp.where(low_half, inverse[:, 0], inverse[:, 1]).reshape(rows, LANES)


    def key_copy(d):
        return pltpu.make_async_remote_copy(
            src_ref=unit_keys.at[lax.rem(me_f + d, nf)], dst_ref=keys.at[me_f, pl.ds(0, rows)],
            send_sem=key_send.at[d], recv_sem=key_recv.at[d], device_id=device(0, 0, d), device_id_type=MESH,
        )

    key_copies = [key_copy(d) for d in range(1, nf)]
    for copy in key_copies:
        copy.start()

    trade[me_c] = give[me_c]
    keys[me_f, 0:rows, :] = unit_keys[me_f]
    q_pick[own_rows, :] = qn[me_f]

    frame_own = wf_raw[...]
    chunk = keys.shape[1]
    winner = (frame_own >> 2) * chunk + wp_raw[...] * 4 + (frame_own & 3)
    for t in range(tok):
        column[t * SUB : (t + 1) * SUB, :] = jnp.broadcast_to(winner[:, t : t + 1], (SUB, LANES))
    wide_lane = iota((per_block, chunk), 1)
    column_value = jnp.concatenate([column[...]] * (chunk // LANES), axis=1)

    def picked_from(d):
        part = lax.rem(me_f + nf - d, nf)
        chosen = (column_value == wide_lane + part * chunk).astype(f32).astype(bf16)
        both = dot(chosen, jnp.concatenate(two_terms(keys[part]), axis=1))
        return both[:, 0:LANES] + both[:, LANES:]

    picked = picked_from(0)

    from_lane = iota((LANES, all_tokens), 0)
    token = iota((LANES, all_tokens), 1)
    spread_table[...] = (
        (from_lane == ((token >> block_bits) << tok_bits) + ((token & (per_block - 1)) >> 3)).astype(f32).astype(bf16)
    )
    caption_of = iota((all_tokens, LANES), 0)
    caption_lane = (caption_of >> block_bits) * (LANES // nc) + (caption_of & 7)
    caption_table[...] = (iota((all_tokens, LANES), 1) == caption_lane).astype(f32).astype(bf16)
    same_group = ((iota((LANES, LANES), 0) >> tok_bits) == (iota((LANES, LANES), 1) >> tok_bits)).astype(f32).astype(bf16)
    mine_of = (iota((SUB, all_tokens), 1) & 7) == iota((SUB, all_tokens), 0)

    def as_row(values):
        return jnp.sum(jnp.where(mine_of, values, 0.0), axis=0, keepdims=True)

    def gather_copy(clip, to, sem):
        place = q_full.at[me_f, clip // 2, lax.rem(clip, 2)]
        return pltpu.make_async_remote_copy(
            src_ref=place, dst_ref=place, send_sem=gather_send.at[sem], recv_sem=gather_recv.at[sem],
            device_id=at_clip(to), device_id_type=MESH,
        )

    for copy in trades:
        copy.wait()
    q_full[me_f, me_v // 2, me_side] = trade[me_f, 0:SUB, :]
    across_gather = gather_copy(me_v, across, 0)
    across_gather.start()

    across_copy.wait()
    across_rows = pl.ds(pl.multiple_of(across * SUB, SUB), SUB)
    for clip in in_half:
        pick_copy(q_pick.at[across_rows], across_rows, clip, 2).start()

    frames = jnp.zeros((SUB, LANES), f32)
    patch_all = jnp.zeros((SUB, LANES), f32)
    length = jnp.zeros((SUB, LANES), f32)
    for j in range(nc):
        here = group == j
        frames = jnp.where(here, pltpu.roll(trade[j, SUB : 2 * SUB, :], j * tok, 1), frames)
        patch_all = jnp.where(here, pltpu.roll(trade[j, 2 * SUB : 3 * SUB, :], j * tok, 1), patch_all)
        length = jnp.where(here, trade[j, 3 * SUB : 4 * SUB, :], length)
    frames = frames.astype(jnp.int32)
    live = (slot_in_group.astype(f32) < length) & used
    safe_length = jnp.maximum(length, 1.0)
    local = jnp.where(((frames >> 2) == me_f) & used, patch_all.astype(jnp.int32) * 4 + (frames & 3), 255)
    twice = jnp.concatenate([local.astype(f32), jnp.zeros((SUB, LANES), f32)], axis=0).astype(bf16)
    local_row = as_row(dot(twice, spread_table[...])[0:SUB]).astype(jnp.int32)
    one_hot[...] = (iota((rows, all_tokens), 0) == local_row).astype(f32).astype(bf16)

    across_gather.wait()
    for dr in range(1, side_rows):
        to = me_half * half_clips + lax.rem(me_row + dr, side_rows) * 2 + me_side
        gather_copy(me_v, to, 1).start()
        gather_copy(across, to, 1).start()

    for d in [d for d in range(1, nf) if d != nf // 2] + [nf // 2]:
        key_copies[d - 1].wait()
        picked = picked + picked_from(d)
    picked_rows[...] = picked

    half_but_one = q_pick.at[pl.ds(0, (half_clips - 1) * SUB)]
    for sem in (1, 2):
        pltpu.make_async_copy(half_but_one, half_but_one, pick_recv.at[sem]).wait()
    product = (picked * q_pick[...]).reshape(tok, SUB, LANES)

    when = iota((tok, SUB, LANES), 0).astype(f32)
    score = jnp.sum(jnp.sum(jnp.where(when < lengths[None], product, 0.0), axis=0), axis=1, keepdims=True)
    score = score * logit_scale / lengths
    own_score = pl.ds(me_f * side_rows + me_row, 1)
    line_out[...] = jnp.sum(jnp.where(lane == me_c * cap_lanes + sub, score, 0.0), axis=0, keepdims=True)
    scores_in[own_score, :] = line_out[...]

    def apart(step, size):
        return min(step, size - step)

    row_steps = [(dr, df) for dr in range(side_rows) for df in range(nf)][1:]
    for dr, df in sorted(row_steps, key=lambda p: -apart(p[0], side_rows) - apart(p[1], nf)):
        to = {
            "cap": me_c,
            "clip": me_half * half_clips + lax.rem(me_row + dr, side_rows) * 2 + me_side,
            "frame": lax.rem(me_f + df, nf),
        }
        pltpu.make_async_remote_copy(
            src_ref=line_out, dst_ref=scores_in.at[own_score], send_sem=score_send, recv_sem=score_recv,
            device_id=to, device_id_type=MESH,
        ).start()

    tile = jnp.zeros((SUB, LANES), f32)
    for t in range(tok):
        tile = jnp.where(lane == me_c * tok + t, jnp.sum(product[t], axis=1, keepdims=True), tile)
    tile_out[...] = tile
    me_16 = me_c * nf + me_f
    tiles_in[me_16] = tile

    @pl.loop(1, nc * nf)
    def _(step):
        pltpu.make_async_remote_copy(
            src_ref=tile_out, dst_ref=tiles_in.at[me_16], send_sem=tile_send, recv_sem=tile_recv,
            device_id=device(step // nf, 0, lax.rem(step, nf)), device_id_type=MESH,
        ).start()

    rows_in[me_v] = picked_rows[own_rows, :]

    @pl.loop(1, nv)
    def _(step):
        to = lax.rem(me_v + step, nv)
        pltpu.make_async_remote_copy(
            src_ref=picked_rows.at[pl.ds(pl.multiple_of(to * SUB, SUB), SUB)], dst_ref=rows_in.at[me_v],
            send_sem=rows_send, recv_sem=rows_recv, device_id=device(0, step, 0), device_id_type=MESH,
        ).start()

    row_tiles = q_full.at[0, pl.ds(0, side_rows - 1)]
    pltpu.make_async_copy(row_tiles, row_tiles, gather_recv.at[1]).wait()
    side_tiles = q_full.at[me_f, pl.ds(0, half_clips), me_side]
    side_copy = pltpu.make_async_remote_copy(
        src_ref=side_tiles, dst_ref=side_tiles, send_sem=gather_send.at[2], recv_sem=gather_recv.at[2],
        device_id=at_clip(me_v + 1 - 2 * me_side), device_id_type=MESH,
    )
    side_copy.start()

    other_scores = scores_in.at[pl.ds(0, others_in_row)]
    pltpu.make_async_copy(other_scores, other_scores, score_recv).wait()
    column_logits = scores_in[0:side_rows, :]
    for j in range(1, nf):
        column_logits = column_logits + scores_in[j * side_rows : (j + 1) * side_rows, :]
    lines_out[...] = column_logits
    own_slot = me_c * 4 + me_corner
    logits_in[own_slot] = column_logits

    corner_steps = [(dh, ds, dc) for dh in (1, 0) for ds in (0, 1) for dc in range(nc)]
    for dh, ds, dc in corner_steps:
        if (dh, ds, dc) == (0, 0, 0):
            continue
        to_half, to_side = lax.rem(me_half + dh, 2), lax.rem(me_side + ds, 2)
        to = {
            "cap": lax.rem(me_c + dc, nc),
            "clip": to_half * half_clips + me_row * 2 + to_side,
            "frame": me_f,
        }
        pltpu.make_async_remote_copy(
            src_ref=lines_out, dst_ref=logits_in.at[own_slot], send_sem=logit_send, recv_sem=logit_recv,
            device_id=to, device_id_type=MESH,
        ).start()

    side_copy.wait()

    def spread_copy(d):
        return pltpu.make_async_remote_copy(
            src_ref=q_full.at[me_f], dst_ref=q_full.at[me_f], send_sem=spread_send.at[d], recv_sem=spread_recv.at[d],
            device_id=device(0, 0, d), device_id_type=MESH,
        )

    spreads = [spread_copy(d) for d in range(1, nf)]
    for copy in spreads:
        copy.start()

    other_tiles = tiles_in.at[pl.ds(0, nc * nf - 1)]
    other_clips = rows_in.at[pl.ds(0, nv - 1)]
    pltpu.make_async_copy(other_tiles, other_tiles, tile_recv).wait()
    live_share = jnp.where(live, jnp.sum(tiles_in[...], axis=0), 0.0)
    share_row = as_row(times_exact(live_share / safe_length, spread_table[...]))
    share_high, share_low = two_terms(one_hot[...].astype(f32) * share_row)
    inner_table = dot(share_high, caption_table[...]) + dot(share_low, caption_table[...])
    pltpu.make_async_copy(other_clips, other_clips, rows_recv).wait()

    length_line = jnp.zeros((SUB, LANES), f32)
    for j in range(nc):
        length_line = jnp.where(lane == j * cap_lanes + sub, trade[j, 3 * SUB : 4 * SUB, :], length_line)
    inverse_length = 1.0 / jnp.maximum(jnp.sum(length_line, axis=0, keepdims=True), 1.0)
    place = iota((nv, LANES), 0)
    corner, row = group_of(place, side_rows), place & (side_rows - 1)
    clip_id = (corner >> 1) * half_clips + row * 2 + (corner & 1)
    line_lane = iota((nv, LANES), 1)
    valid = (line_lane & (cap_lanes - 1)) < SUB
    positive = valid & (clip_id == group_of(line_lane, cap_lanes) * SUB + (line_lane & (cap_lanes - 1)))
    positive = positive.astype(f32)

    other_logits = logits_in.at[pl.ds(0, others_in_corner)]
    pltpu.make_async_copy(other_logits, other_logits, logit_recv).wait()
    logits = logits_in[0:4]
    for j in range(1, nc):
        logits = logits + logits_in[4 * j : 4 * j + 4]
    logits = logits.reshape(nv, LANES)
    exp_logits = jnp.where(valid, jnp.exp(logits), 0.0)
    row_total = jnp.where(in_line[0:1], jnp.sum(exp_logits, axis=0, keepdims=True), 1.0)
    col_total = jnp.sum(exp_logits, axis=1, keepdims=True)
    grad = logit_scale * (exp_logits * (0.5 / row_total + 0.5 / col_total) - positive)
    weights[...] = grad
    turned[...] = jnp.transpose(grad * inverse_length)

    block_weight = turned[pl.ds(pl.multiple_of(me_c * cap_lanes, SUB), SUB), :]
    slice_grad = jnp.zeros((SUB, LANES), f32)
    for v in range(nv):
        at = (v // half_clips * 2 + v % 2) * side_rows + v % half_clips // 2
        slice_grad = slice_grad + block_weight[:, at : at + 1] * rows_in[v]
    slice_grad = jnp.where(me_v.astype(f32) < lengths, slice_grad, 0.0)
    grad_out[...] = slice_grad
    grads_in[me_f] = slice_grad

    def grad_copy(d):
        return pltpu.make_async_remote_copy(
            src_ref=grad_out, dst_ref=grads_in.at[me_f], send_sem=grad_send.at[d], recv_sem=grad_recv.at[d],
            device_id=device(0, 0, d), device_id_type=MESH,
        )

    grad_copies = [grad_copy(d) for d in range(1, nf)]
    for copy in grad_copies:
        copy.start()

    own_grad = weights[pl.ds(me_corner * side_rows + me_row, 1), :]
    own_weight = own_grad * inverse_length
    token_weight = [
        jnp.sum(jnp.where(lane == j * cap_lanes + sub, own_weight, 0.0), axis=1, keepdims=True) for j in range(nc)
    ]
    inner = jnp.sum(inner_table * own_grad, axis=1, keepdims=True)
    for copy in spreads:
        copy.wait()
    parts = []
    for j in range(nc):
        mask = when < trade[j, 3 * SUB : 4 * SUB, :][None]
        scaled = q_full[j].reshape(tok, SUB, LANES) * jnp.where(mask, token_weight[j][None], 0.0)
        parts.append(jnp.concatenate(two_terms(scaled.reshape(per_block, LANES)), axis=1))
    both = dot(one_hot[...], jnp.concatenate(parts, axis=0))
    clip_res[...] = key_inv[...] * (both[:, 0:LANES] + both[:, LANES:] - unit_keys[me_c] * inner)

    terms = 0.5 * jnp.sum(jnp.where(in_line[0:1], jnp.log(row_total), 0.0)) + 0.5 * jnp.sum(jnp.log(col_total))
    terms = terms - jnp.sum(positive * logits)
    loss_ref[...] = jnp.broadcast_to(terms / (nc * SUB), (1, 1))

    for copy in grad_copies:
        copy.wait()
    dot_tile = jnp.zeros((SUB, LANES), f32)
    for j in range(nc):
        dot_tile = dot_tile + qn[j] * grads_in[j]
    cap_inner = jnp.sum(dot_tile, axis=1, keepdims=True)
    for j in range(nc):
        cap_res[pl.ds(j, SUB, stride=nc), :] = cap_inv * (grads_in[j] - qn[j] * cap_inner)

    for sem in (1, 2):
        pltpu.make_async_copy(half_but_one, half_but_one, pick_send.at[sem]).wait()
    pltpu.make_async_copy(row_tiles, row_tiles, gather_send.at[1]).wait()
    pltpu.make_async_copy(other_clips, other_clips, rows_send).wait()
    pltpu.make_async_copy(other_scores, other_scores, score_send).wait()
    pltpu.make_async_copy(other_logits, other_logits, logit_send).wait()
    pltpu.make_async_copy(other_tiles, other_tiles, tile_send).wait()


def body(nc, nv, cap_tokens, clip_tokens, win_frame, win_patch, cap_lengths):
    block, _, width = cap_tokens.shape
    _, frames, patches, _ = clip_tokens.shape
    assert block == SUB and frames == 4 and width == nc * LANES and win_frame.shape == (SUB, nv, 1)
    rows = frames * patches
    per_block = nv * SUB
    caps = cap_tokens.reshape(SUB * nc, LANES)
    clips = clip_tokens.reshape(frames, patches, nc, LANES).transpose(1, 2, 0, 3).reshape(patches, nc * frames, LANES)
    vmem = pltpu.VMEM
    dma = pltpu.SemaphoreType.DMA
    scratch = [
        vmem((SUB * nc, LANES), f32),
        vmem((patches, nc * frames, LANES), f32),
        vmem((SUB, nv), jnp.int32),
        vmem((SUB, nv), jnp.int32),
        vmem((nc, SUB, LANES), f32),
        vmem((nc, 4 * SUB, LANES), f32),
        vmem((nc, 4 * SUB, LANES), f32),
        vmem((nc, nv // 2, 2, SUB, LANES), f32),
        vmem((per_block, LANES), f32),
        vmem((nc, rows, LANES), f32),
        vmem((nc, -(-rows // LANES) * LANES, LANES), f32),
        vmem((rows, LANES), f32),
        vmem((per_block, LANES), jnp.int32),
        vmem((per_block, LANES), f32),
        vmem((nv, SUB, LANES), f32),
        vmem((nc * nc, SUB, LANES), f32),
        vmem((nc * nv // 4, LANES), f32),
        vmem((nc * 4, nv // 4, LANES), f32),
        vmem((SUB, LANES), f32),
        vmem((1, LANES), f32),
        vmem((nv // 4, LANES), f32),
        vmem((nv, LANES), f32),
        vmem((LANES, nv), f32),
        vmem((nc, SUB, LANES), f32),
        vmem((SUB, LANES), f32),
        vmem((LANES, nc * per_block), bf16),
        vmem((nc * per_block, LANES), bf16),
        vmem((rows, nc * per_block), bf16),
        vmem((1, SUB), jnp.int32),
        dma((5,)),
        dma((nc,)), dma((nc,)), dma((nc,)), dma((nc,)),
        dma((3,)), dma((3,)), dma((3,)), dma((3,)),
        dma((nc,)), dma((nc,)),
        dma, dma, dma, dma, dma, dma, dma, dma,
        dma((nc,)), dma((nc,)),
    ]
    hbm = pl.BlockSpec(memory_space=pl.ANY)
    near = pl.BlockSpec(memory_space=pltpu.VMEM)
    in_hbm = functools.partial(pltpu.with_memory_space_constraint, memory_space=pltpu.HBM)
    operands = (caps, clips, win_frame.reshape(SUB, nv), win_patch.reshape(SUB, nv), cap_lengths.reshape(1, SUB))
    shapes = ((1, 1), (SUB * nc, LANES), (rows, LANES))
    loss, cap_grad, clip_grad = pl.pallas_call(
        functools.partial(kernel, nc, nv, patches),
        out_shape=[vmem(shape, f32) for shape in shapes],
        in_specs=[hbm] * 5,
        out_specs=[near] * 3,
        scratch_shapes=scratch,
        compiler_params=pltpu.CompilerParams(
            collective_id=0, has_side_effects=True, vmem_limit_bytes=32 * 1024 * 1024
        ),
    )(*map(in_hbm, operands))
    clip_grad = clip_grad.reshape(patches, frames, LANES).transpose(1, 0, 2)[None]
    return loss.reshape(()), cap_grad.reshape(SUB, 1, width), clip_grad


def solution(mesh):
    placed = (
        P("cap", "clip", None),
        P("clip", "frame", None, None),
        P("cap", None, "clip"),
        P("cap", None, "clip"),
        P("cap"),
    )
    assert mesh.shape["cap"] == mesh.shape["frame"]
    return jax.shard_map(
        functools.partial(body, mesh.shape["cap"], mesh.shape["clip"]),
        mesh=mesh,
        in_specs=placed,
        out_specs=(P(), P("cap", "clip", None), P("clip", "frame", None, "cap")),
        check_vma=False,
    )
```

```python
import functools

import jax
import jax.numpy as jnp
from jax import lax
from jax.experimental import pallas as pl
from jax.experimental.pallas import tpu as pltpu
from jax.sharding import PartitionSpec as P

MESH = pl.DeviceIdType.MESH
logit_scale = 1.0 / 0.07
norm_eps = 1e-06
f32 = jnp.float32
bf16 = jnp.bfloat16
LANES = 128
SUB = 8


def iota(shape, dim):
    return lax.broadcasted_iota(jnp.int32, shape, dim)


def two_terms(x):
    high = x.astype(bf16)
    return high, (x - high.astype(f32)).astype(bf16)


def three_terms(x):
    high = x.astype(bf16).astype(f32)
    rest = x - high
    middle = rest.astype(bf16).astype(f32)
    return high, middle, rest - middle


def dot(a, b):
    return jnp.dot(a, b, preferred_element_type=f32)


def times_exact(tile, table):
    high, middle, low = three_terms(tile)
    stacked = jnp.concatenate([high, middle, low, jnp.zeros_like(high)], axis=0).astype(bf16)
    out = dot(stacked, table)
    return out[0:SUB] + out[SUB : 2 * SUB] + out[2 * SUB : 3 * SUB]


def group_of(lane, size):
    return lane >> log2(size)


def log2(n):
    assert n & (n - 1) == 0
    return n.bit_length() - 1


def kernel(
    nc, nv, patches,
    cap_ref, clip_ref, wf_ref, wp_ref, len_ref,
    loss_ref, cap_res, clip_res,
    cap_raw, clip_raw, wf_raw, wp_raw, qn, give, trade, q_full, q_pick, unit_keys, keys, key_inv, column,
    picked_rows, rows_in, tiles_in, scores_in, logits_in, tile_out, line_out, lines_out, weights, turned, grads_in, grad_out, spread_table, sums_table, caption_table, one_hot,
    len_raw,
    load_sem, trade_send, trade_recv, key_send, key_recv, pick_send, pick_recv, gather_send, gather_recv,
    spread_send, spread_recv, rows_send, rows_recv, tile_send, tile_recv, score_send, score_recv, logit_send, logit_recv, grad_send, grad_recv,
):
    nf = nc
    tok = nv
    me_c, me_v, me_f = lax.axis_index("cap"), lax.axis_index("clip"), lax.axis_index("frame")
    rows = 4 * patches
    per_block = tok * SUB
    all_tokens = nf * per_block
    tok_bits, block_bits = log2(tok), log2(per_block)

    half_clips, side_rows = nv // 2, nv // 4
    me_half, me_side = me_v // half_clips, lax.rem(me_v, 2)
    me_row = lax.rem(me_v, half_clips) // 2
    me_corner = me_half * 2 + me_side
    others_in_row, others_in_corner = nf * side_rows - 1, nc * 4 - 1

    loads = [
        pltpu.make_async_copy(clip_ref, clip_raw, load_sem.at[0]),
        pltpu.make_async_copy(cap_ref, cap_raw, load_sem.at[1]),
        pltpu.make_async_copy(wf_ref, wf_raw, load_sem.at[2]),
        pltpu.make_async_copy(wp_ref, wp_raw, load_sem.at[3]),
        pltpu.make_async_copy(len_ref, len_raw, load_sem.at[4]),
    ]
    logits_in[...] = jnp.zeros((4 * SUB, LANES), f32)

    barrier = pltpu.get_barrier_semaphore()

    def device(dc, dv, df):
        return {
            "cap": lax.rem(me_c + dc, nc),
            "clip": lax.rem(me_v + dv, nv),
            "frame": lax.rem(me_f + df, nf),
        }

    def signal(dc, dv, df):
        pl.semaphore_signal(barrier, inc=1, device_id=device(dc, dv, df), device_id_type=MESH)

    def at_clip(clip):
        return {"cap": me_c, "clip": clip, "frame": me_f}

    across = lax.rem(me_v + half_clips, nv)
    in_half = [me_half * half_clips + lax.rem(me_v + step, half_clips) for step in range(1, half_clips)]
    pl.semaphore_signal(barrier, inc=1, device_id=at_clip(across), device_id_type=MESH)
    for clip in in_half:
        pl.semaphore_signal(barrier, inc=1, device_id=at_clip(clip), device_id_type=MESH)
    for load in loads:
        load.start()
    for step in range(1, nf):
        signal(0, 0, step)
    for step in range(1, nc):
        signal(step, 0, 0)

    lane = iota((SUB, LANES), 1)
    sub = iota((SUB, LANES), 0)
    group = lane >> tok_bits
    slot_in_group = lane & (tok - 1)
    used = group < nc
    cap_lanes = LANES // nc

    loads[1].wait()
    raw = [cap_raw[pl.ds(j, SUB, stride=nc), :] for j in range(nc)]
    total = raw[0] * raw[0]
    for j in range(1, nc):
        total = total + raw[j] * raw[j]
    cap_inv = lax.rsqrt(jnp.sum(total, axis=1, keepdims=True) + norm_eps)
    for j in range(nc):
        unit = raw[j] * cap_inv
        qn[j] = unit
        give[j, 0:SUB, :] = unit

    for load in loads[2:]:
        load.wait()
    diagonal = iota((SUB, SUB), 0) == iota((SUB, SUB), 1)
    lengths = jnp.sum(jnp.where(diagonal, len_raw[...].astype(f32), 0.0), axis=1, keepdims=True)
    lengths = jnp.broadcast_to(lengths, (SUB, LANES))
    give[:, SUB : 3 * SUB, :] = jnp.zeros((nc, 2 * SUB, LANES), f32)
    for j in range(nc):
        give[j, SUB : 2 * SUB, 0:tok] = wf_raw[...].astype(f32)
        give[j, 2 * SUB : 3 * SUB, 0:tok] = wp_raw[...].astype(f32)
        give[j, 3 * SUB : 4 * SUB, :] = lengths

    pl.semaphore_wait(barrier, nc - 1 + nf - 1 + half_clips)

    own_rows = pl.ds(pl.multiple_of(me_v * SUB, SUB), SUB)

    def pick_copy(src, place, clip, sem):
        return pltpu.make_async_remote_copy(
            src_ref=src, dst_ref=q_pick.at[place], send_sem=pick_send.at[sem], recv_sem=pick_recv.at[sem],
            device_id=at_clip(clip), device_id_type=MESH,
        )

    across_copy = pick_copy(qn.at[me_f], own_rows, across, 0)
    across_copy.start()
    for clip in in_half:
        pick_copy(qn.at[me_f], own_rows, clip, 1).start()

    def trade_copy(d):
        to = lax.rem(me_c + d, nc)
        return pltpu.make_async_remote_copy(
            src_ref=give.at[to], dst_ref=trade.at[me_c], send_sem=trade_send.at[d], recv_sem=trade_recv.at[d],
            device_id=device(d, 0, 0), device_id_type=MESH,
        )

    trades = [trade_copy(d) for d in range(1, nc)]
    for copy in trades:
        copy.start()

    keys[:, rows:, :] = jnp.zeros((nf, keys.shape[1] - rows, LANES), f32)
    loads[0].wait()
    whole = clip_raw[...].reshape(patches, nc // 2, SUB, LANES)
    square = whole * whole
    summed = square[:, 0]
    for j in range(1, nc // 2):
        summed = summed + square[:, j]
    summed = summed + pltpu.roll(summed, 4, 1)
    inverse = lax.rsqrt(jnp.sum(summed, axis=2, keepdims=True) + norm_eps)
    low_half = iota((patches // 2, SUB, LANES), 1) < 4
    for j in range(nc // 2):
        unit = (whole[:, j] * inverse).reshape(patches // 2, 2, SUB, LANES)
        first, second = unit[:, 0], unit[:, 1]
        unit_keys[2 * j] = jnp.where(low_half, first, pltpu.roll(second, 4, 1)).reshape(rows, LANES)
        unit_keys[2 * j + 1] = jnp.where(low_half, pltpu.roll(first, 4, 1), second).reshape(rows, LANES)
    inverse = jnp.broadcast_to(inverse, (patches, SUB, LANES)).reshape(patches // 2, 2, SUB, LANES)
    key_inv[...] = jnp.where(low_half, inverse[:, 0], inverse[:, 1]).reshape(rows, LANES)


    def key_copy(d):
        return pltpu.make_async_remote_copy(
            src_ref=unit_keys.at[lax.rem(me_f + d, nf)], dst_ref=keys.at[me_f, pl.ds(0, rows)],
            send_sem=key_send.at[d], recv_sem=key_recv.at[d], device_id=device(0, 0, d), device_id_type=MESH,
        )

    key_copies = [key_copy(d) for d in range(1, nf)]
    for copy in key_copies:
        copy.start()

    trade[me_c] = give[me_c]
    keys[me_f, 0:rows, :] = unit_keys[me_f]
    q_pick[own_rows, :] = qn[me_f]

    frame_own = wf_raw[...]
    chunk = keys.shape[1]
    winner = (frame_own >> 2) * chunk + wp_raw[...] * 4 + (frame_own & 3)
    for t in range(tok):
        column[t * SUB : (t + 1) * SUB, :] = jnp.broadcast_to(winner[:, t : t + 1], (SUB, LANES))
    wide_lane = iota((per_block, chunk), 1)
    column_value = jnp.concatenate([column[...]] * (chunk // LANES), axis=1)

    def picked_from(d):
        part = lax.rem(me_f + nf - d, nf)
        chosen = (column_value == wide_lane + part * chunk).astype(f32).astype(bf16)
        both = dot(chosen, jnp.concatenate(two_terms(keys[part]), axis=1))
        return both[:, 0:LANES] + both[:, LANES:]

    picked = picked_from(0)

    from_row, to_row = iota((LANES, LANES), 0), iota((LANES, LANES), 1)
    of_caption, of_clip = (from_row & 7) == (to_row & 7), (from_row >> 3) == (to_row >> 3)
    sums_table[...] = jnp.concatenate([of_caption, of_clip], axis=1).astype(f32).astype(bf16)
    corner, block, at = (iota((4, SUB, LANES), d) for d in range(3))
    valid = (block < nc) & (at < side_rows * SUB)
    clip_id = (corner >> 1) * half_clips + (at >> 3) * 2 + (corner & 1)
    positive = (valid & (clip_id == block * SUB + (at & 7))).astype(f32)

    from_lane = iota((LANES, all_tokens), 0)
    token = iota((LANES, all_tokens), 1)
    spread_table[...] = (
        (from_lane == ((token >> block_bits) << tok_bits) + ((token & (per_block - 1)) >> 3)).astype(f32).astype(bf16)
    )
    caption_of = iota((all_tokens, LANES), 0)
    caption_lane = (caption_of >> block_bits) * (LANES // nc) + (caption_of & 7)
    caption_table[...] = (iota((all_tokens, LANES), 1) == caption_lane).astype(f32).astype(bf16)
    same_group = ((iota((LANES, LANES), 0) >> tok_bits) == (iota((LANES, LANES), 1) >> tok_bits)).astype(f32).astype(bf16)
    mine_of = (iota((SUB, all_tokens), 1) & 7) == iota((SUB, all_tokens), 0)

    def as_row(values):
        return jnp.sum(jnp.where(mine_of, values, 0.0), axis=0, keepdims=True)

    def gather_copy(clip, to, sem):
        place = q_full.at[me_f, clip // 2, lax.rem(clip, 2)]
        return pltpu.make_async_remote_copy(
            src_ref=place, dst_ref=place, send_sem=gather_send.at[sem], recv_sem=gather_recv.at[sem],
            device_id=at_clip(to), device_id_type=MESH,
        )

    for copy in trades:
        copy.wait()
    q_full[me_f, me_v // 2, me_side] = trade[me_f, 0:SUB, :]
    across_gather = gather_copy(me_v, across, 0)
    across_gather.start()

    across_copy.wait()
    across_rows = pl.ds(pl.multiple_of(across * SUB, SUB), SUB)
    for clip in in_half:
        pick_copy(q_pick.at[across_rows], across_rows, clip, 2).start()

    frames = jnp.zeros((SUB, LANES), f32)
    patch_all = jnp.zeros((SUB, LANES), f32)
    length = jnp.zeros((SUB, LANES), f32)
    for j in range(nc):
        here = group == j
        frames = jnp.where(here, pltpu.roll(trade[j, SUB : 2 * SUB, :], j * tok, 1), frames)
        patch_all = jnp.where(here, pltpu.roll(trade[j, 2 * SUB : 3 * SUB, :], j * tok, 1), patch_all)
        length = jnp.where(here, trade[j, 3 * SUB : 4 * SUB, :], length)
    frames = frames.astype(jnp.int32)
    live = (slot_in_group.astype(f32) < length) & used
    safe_length = jnp.maximum(length, 1.0)
    local = jnp.where(((frames >> 2) == me_f) & used, patch_all.astype(jnp.int32) * 4 + (frames & 3), 255)
    twice = jnp.concatenate([local.astype(f32), jnp.zeros((SUB, LANES), f32)], axis=0).astype(bf16)
    local_row = as_row(dot(twice, spread_table[...])[0:SUB]).astype(jnp.int32)
    one_hot[...] = (iota((rows, all_tokens), 0) == local_row).astype(f32).astype(bf16)

    across_gather.wait()
    for dr in range(1, side_rows):
        to = me_half * half_clips + lax.rem(me_row + dr, side_rows) * 2 + me_side
        gather_copy(me_v, to, 1).start()
        gather_copy(across, to, 1).start()

    for d in [d for d in range(1, nf) if d != nf // 2] + [nf // 2]:
        key_copies[d - 1].wait()
        picked = picked + picked_from(d)
    picked_rows[...] = picked

    half_but_one = q_pick.at[pl.ds(0, (half_clips - 1) * SUB)]
    for sem in (1, 2):
        pltpu.make_async_copy(half_but_one, half_but_one, pick_recv.at[sem]).wait()
    product = (picked * q_pick[...]).reshape(tok, SUB, LANES)

    when = iota((tok, SUB, LANES), 0).astype(f32)
    score = jnp.sum(jnp.sum(jnp.where(when < lengths[None], product, 0.0), axis=0), axis=1, keepdims=True)
    score = score * logit_scale / lengths
    own_score = pl.ds(me_f * side_rows + me_row, 1)
    line_out[...] = jnp.sum(jnp.where(lane == me_row * SUB + sub, score, 0.0), axis=0, keepdims=True)
    scores_in[own_score, :] = line_out[...]

    def apart(step, size):
        return min(step, size - step)

    row_steps = [(dr, df) for dr in range(side_rows) for df in range(nf)][1:]
    for dr, df in sorted(row_steps, key=lambda p: -apart(p[0], side_rows) - apart(p[1], nf)):
        to = {
            "cap": me_c,
            "clip": me_half * half_clips + lax.rem(me_row + dr, side_rows) * 2 + me_side,
            "frame": lax.rem(me_f + df, nf),
        }
        pltpu.make_async_remote_copy(
            src_ref=line_out, dst_ref=scores_in.at[own_score], send_sem=score_send, recv_sem=score_recv,
            device_id=to, device_id_type=MESH,
        ).start()

    tile = jnp.zeros((SUB, LANES), f32)
    for t in range(tok):
        tile = jnp.where(lane == me_c * tok + t, jnp.sum(product[t], axis=1, keepdims=True), tile)
    tile_out[...] = tile
    me_16 = me_c * nf + me_f
    tiles_in[me_16] = tile

    @pl.loop(1, nc * nf)
    def _(step):
        pltpu.make_async_remote_copy(
            src_ref=tile_out, dst_ref=tiles_in.at[me_16], send_sem=tile_send, recv_sem=tile_recv,
            device_id=device(step // nf, 0, lax.rem(step, nf)), device_id_type=MESH,
        ).start()

    rows_in[me_v] = picked_rows[own_rows, :]

    @pl.loop(1, nv)
    def _(step):
        to = lax.rem(me_v + step, nv)
        pltpu.make_async_remote_copy(
            src_ref=picked_rows.at[pl.ds(pl.multiple_of(to * SUB, SUB), SUB)], dst_ref=rows_in.at[me_v],
            send_sem=rows_send, recv_sem=rows_recv, device_id=device(0, step, 0), device_id_type=MESH,
        ).start()

    row_tiles = q_full.at[0, pl.ds(0, side_rows - 1)]
    pltpu.make_async_copy(row_tiles, row_tiles, gather_recv.at[1]).wait()
    side_tiles = q_full.at[me_f, pl.ds(0, half_clips), me_side]
    side_copy = pltpu.make_async_remote_copy(
        src_ref=side_tiles, dst_ref=side_tiles, send_sem=gather_send.at[2], recv_sem=gather_recv.at[2],
        device_id=at_clip(me_v + 1 - 2 * me_side), device_id_type=MESH,
    )
    side_copy.start()

    other_scores = scores_in.at[pl.ds(0, others_in_row)]
    pltpu.make_async_copy(other_scores, other_scores, score_recv).wait()
    lines_out[...] = jnp.sum(scores_in[...], axis=0, keepdims=True)
    own_slot = pl.ds(me_corner * SUB + me_c, 1)
    logits_in[own_slot, :] = lines_out[...]

    corner_steps = [(dh, ds, dc) for dh in (1, 0) for ds in (0, 1) for dc in range(nc)]
    for dh, ds, dc in corner_steps:
        if (dh, ds, dc) == (0, 0, 0):
            continue
        to_half, to_side = lax.rem(me_half + dh, 2), lax.rem(me_side + ds, 2)
        to = {
            "cap": lax.rem(me_c + dc, nc),
            "clip": to_half * half_clips + me_row * 2 + to_side,
            "frame": me_f,
        }
        pltpu.make_async_remote_copy(
            src_ref=lines_out, dst_ref=logits_in.at[own_slot], send_sem=logit_send, recv_sem=logit_recv,
            device_id=to, device_id_type=MESH,
        ).start()

    side_copy.wait()

    def spread_copy(d):
        return pltpu.make_async_remote_copy(
            src_ref=q_full.at[me_f], dst_ref=q_full.at[me_f], send_sem=spread_send.at[d], recv_sem=spread_recv.at[d],
            device_id=device(0, 0, d), device_id_type=MESH,
        )

    spreads = [spread_copy(d) for d in range(1, nf)]
    for copy in spreads:
        copy.start()

    other_tiles = tiles_in.at[pl.ds(0, nc * nf - 1)]
    other_clips = rows_in.at[pl.ds(0, nv - 1)]
    pltpu.make_async_copy(other_tiles, other_tiles, tile_recv).wait()
    live_share = jnp.where(live, jnp.sum(tiles_in[...], axis=0), 0.0)
    share_row = as_row(times_exact(live_share / safe_length, spread_table[...]))
    share_high, share_low = two_terms(one_hot[...].astype(f32) * share_row)
    inner_table = dot(share_high, caption_table[...]) + dot(share_low, caption_table[...])
    pltpu.make_async_copy(other_clips, other_clips, rows_recv).wait()

    length_lines = jnp.zeros((SUB, LANES), f32)
    for j in range(nc):
        line = jnp.sum(jnp.where((lane & 7) == sub, trade[j, 3 * SUB : 4 * SUB, :], 0.0), axis=0, keepdims=True)
        length_lines = jnp.where(sub == j, line, length_lines)
    inverse_length = 1.0 / jnp.maximum(length_lines, 1.0)

    other_logits = logits_in.at[pl.ds(0, others_in_corner)]
    pltpu.make_async_copy(other_logits, other_logits, logit_recv).wait()
    logits = logits_in[...]
    exp_logits = jnp.where(valid, jnp.exp(logits).reshape(4, SUB, LANES), 0.0)
    terms = jnp.concatenate(three_terms(exp_logits.reshape(4 * SUB, LANES)), axis=0).astype(bf16)
    sums = dot(terms, sums_table[...]).reshape(3, 4, SUB, 2 * LANES)
    sums = sums[0] + sums[1] + sums[2]
    row_total = jnp.where(valid[0], jnp.sum(sums[:, :, 0:LANES], axis=0), 1.0)
    col_total = jnp.where(at[:, 0:1] < side_rows * SUB, jnp.sum(sums[:, :, LANES:], axis=1, keepdims=True), 1.0)
    grad = logit_scale * (exp_logits * (0.5 / row_total + 0.5 / col_total) - positive)
    weights[...] = grad.reshape(4 * SUB, LANES)
    block_grad = jnp.sum(jnp.where(block == me_c, grad * inverse_length, 0.0), axis=1, keepdims=True)
    turned[...] = jnp.transpose(jnp.broadcast_to(block_grad, (4, SUB, LANES)).reshape(4 * SUB, LANES))

    slice_grad = jnp.zeros((SUB, LANES), f32)
    for v in range(nv):
        of_row, of_corner = v % half_clips // 2 * SUB, (v // half_clips * 2 + v % 2) * SUB
        slice_grad = slice_grad + turned[of_row : of_row + SUB, of_corner : of_corner + 1] * rows_in[v]
    slice_grad = jnp.where(me_v.astype(f32) < lengths, slice_grad, 0.0)
    grad_out[...] = slice_grad
    grads_in[me_f] = slice_grad

    def grad_copy(d):
        return pltpu.make_async_remote_copy(
            src_ref=grad_out, dst_ref=grads_in.at[me_f], send_sem=grad_send.at[d], recv_sem=grad_recv.at[d],
            device_id=device(0, 0, d), device_id_type=MESH,
        )

    grad_copies = [grad_copy(d) for d in range(1, nf)]
    for copy in grad_copies:
        copy.start()

    own_lines = weights[pl.ds(pl.multiple_of(me_corner * SUB, SUB), SUB), :]
    own_grad = jnp.zeros((SUB, LANES), f32)
    token_weight = []
    for j in range(nc):
        value = jnp.sum(jnp.where(lane == me_row * SUB + sub, own_lines[j : j + 1], 0.0), axis=1, keepdims=True)
        own_grad = jnp.where(lane == j * cap_lanes + sub, value, own_grad)
        token_weight.append(value / jnp.maximum(trade[j, 3 * SUB : 4 * SUB, :], 1.0))
    own_grad = jnp.sum(own_grad, axis=0, keepdims=True)
    inner = jnp.sum(inner_table * own_grad, axis=1, keepdims=True)
    for copy in spreads:
        copy.wait()
    parts = []
    for j in range(nc):
        mask = when < trade[j, 3 * SUB : 4 * SUB, :][None]
        scaled = q_full[j].reshape(tok, SUB, LANES) * jnp.where(mask, token_weight[j][None], 0.0)
        parts.append(jnp.concatenate(two_terms(scaled.reshape(per_block, LANES)), axis=1))
    both = dot(one_hot[...], jnp.concatenate(parts, axis=0))
    clip_res[...] = key_inv[...] * (both[:, 0:LANES] + both[:, LANES:] - unit_keys[me_c] * inner)

    row_terms = jnp.where((sub < nc) & (lane < SUB), jnp.log(row_total), 0.0)
    col_terms = jnp.where((at[:, 0:1] & 7) == 0, jnp.log(col_total), 0.0)
    terms = 0.5 * jnp.sum(row_terms) + 0.5 * jnp.sum(col_terms)
    terms = terms - jnp.sum(positive * logits.reshape(4, SUB, LANES))
    loss_ref[...] = jnp.broadcast_to(terms / (nc * SUB), (1, 1))

    for copy in grad_copies:
        copy.wait()
    dot_tile = jnp.zeros((SUB, LANES), f32)
    for j in range(nc):
        dot_tile = dot_tile + qn[j] * grads_in[j]
    cap_inner = jnp.sum(dot_tile, axis=1, keepdims=True)
    for j in range(nc):
        cap_res[pl.ds(j, SUB, stride=nc), :] = cap_inv * (grads_in[j] - qn[j] * cap_inner)

    for sem in (1, 2):
        pltpu.make_async_copy(half_but_one, half_but_one, pick_send.at[sem]).wait()
    pltpu.make_async_copy(row_tiles, row_tiles, gather_send.at[1]).wait()
    pltpu.make_async_copy(other_clips, other_clips, rows_send).wait()
    pltpu.make_async_copy(other_scores, other_scores, score_send).wait()
    pltpu.make_async_copy(other_logits, other_logits, logit_send).wait()
    pltpu.make_async_copy(other_tiles, other_tiles, tile_send).wait()


def body(nc, nv, cap_tokens, clip_tokens, win_frame, win_patch, cap_lengths):
    block, _, width = cap_tokens.shape
    _, frames, patches, _ = clip_tokens.shape
    assert block == SUB and frames == 4 and width == nc * LANES and win_frame.shape == (SUB, nv, 1)
    rows = frames * patches
    per_block = nv * SUB
    caps = cap_tokens.reshape(SUB * nc, LANES)
    clips = clip_tokens.reshape(frames, patches, nc, LANES).transpose(1, 2, 0, 3).reshape(patches, nc * frames, LANES)
    vmem = pltpu.VMEM
    dma = pltpu.SemaphoreType.DMA
    scratch = [
        vmem((SUB * nc, LANES), f32),
        vmem((patches, nc * frames, LANES), f32),
        vmem((SUB, nv), jnp.int32),
        vmem((SUB, nv), jnp.int32),
        vmem((nc, SUB, LANES), f32),
        vmem((nc, 4 * SUB, LANES), f32),
        vmem((nc, 4 * SUB, LANES), f32),
        vmem((nc, nv // 2, 2, SUB, LANES), f32),
        vmem((per_block, LANES), f32),
        vmem((nc, rows, LANES), f32),
        vmem((nc, -(-rows // LANES) * LANES, LANES), f32),
        vmem((rows, LANES), f32),
        vmem((per_block, LANES), jnp.int32),
        vmem((per_block, LANES), f32),
        vmem((nv, SUB, LANES), f32),
        vmem((nc * nc, SUB, LANES), f32),
        vmem((nc * nv // 4, LANES), f32),
        vmem((4 * SUB, LANES), f32),
        vmem((SUB, LANES), f32),
        vmem((1, LANES), f32),
        vmem((1, LANES), f32),
        vmem((4 * SUB, LANES), f32),
        vmem((LANES, 4 * SUB), f32),
        vmem((nc, SUB, LANES), f32),
        vmem((SUB, LANES), f32),
        vmem((LANES, nc * per_block), bf16),
        vmem((LANES, 2 * LANES), bf16),
        vmem((nc * per_block, LANES), bf16),
        vmem((rows, nc * per_block), bf16),
        vmem((1, SUB), jnp.int32),
        dma((5,)),
        dma((nc,)), dma((nc,)), dma((nc,)), dma((nc,)),
        dma((3,)), dma((3,)), dma((3,)), dma((3,)),
        dma((nc,)), dma((nc,)),
        dma, dma, dma, dma, dma, dma, dma, dma,
        dma((nc,)), dma((nc,)),
    ]
    hbm = pl.BlockSpec(memory_space=pl.ANY)
    near = pl.BlockSpec(memory_space=pltpu.VMEM)
    in_hbm = functools.partial(pltpu.with_memory_space_constraint, memory_space=pltpu.HBM)
    operands = (caps, clips, win_frame.reshape(SUB, nv), win_patch.reshape(SUB, nv), cap_lengths.reshape(1, SUB))
    shapes = ((1, 1), (SUB * nc, LANES), (rows, LANES))
    loss, cap_grad, clip_grad = pl.pallas_call(
        functools.partial(kernel, nc, nv, patches),
        out_shape=[vmem(shape, f32) for shape in shapes],
        in_specs=[hbm] * 5,
        out_specs=[near] * 3,
        scratch_shapes=scratch,
        compiler_params=pltpu.CompilerParams(
            collective_id=0, has_side_effects=True, vmem_limit_bytes=32 * 1024 * 1024
        ),
    )(*map(in_hbm, operands))
    clip_grad = clip_grad.reshape(patches, frames, LANES).transpose(1, 0, 2)[None]
    return loss.reshape(()), cap_grad.reshape(SUB, 1, width), clip_grad


def solution(mesh):
    placed = (
        P("cap", "clip", None),
        P("clip", "frame", None, None),
        P("cap", None, "clip"),
        P("cap", None, "clip"),
        P("cap"),
    )
    assert mesh.shape["cap"] == mesh.shape["frame"]
    return jax.shard_map(
        functools.partial(body, mesh.shape["cap"], mesh.shape["clip"]),
        mesh=mesh,
        in_specs=placed,
        out_specs=(P(), P("cap", "clip", None), P("clip", "frame", None, "cap")),
        check_vma=False,
    )
```

```python
import functools

import jax
import jax.numpy as jnp
from jax import lax
from jax.experimental import pallas as pl
from jax.experimental.pallas import tpu as pltpu
from jax.sharding import PartitionSpec as P

MESH = pl.DeviceIdType.MESH
logit_scale = 1.0 / 0.07
norm_eps = 1e-06
f32 = jnp.float32
bf16 = jnp.bfloat16
LANES = 128
SUB = 8


def iota(shape, dim):
    return lax.broadcasted_iota(jnp.int32, shape, dim)


def two_terms(x):
    high = x.astype(bf16)
    return high, (x - high.astype(f32)).astype(bf16)


def three_terms(x):
    high = x.astype(bf16).astype(f32)
    rest = x - high
    middle = rest.astype(bf16).astype(f32)
    return high, middle, rest - middle


def dot(a, b):
    return jnp.dot(a, b, preferred_element_type=f32)


def times_exact(tile, table):
    high, middle, low = three_terms(tile)
    stacked = jnp.concatenate([high, middle, low, jnp.zeros_like(high)], axis=0).astype(bf16)
    out = dot(stacked, table)
    return out[0:SUB] + out[SUB : 2 * SUB] + out[2 * SUB : 3 * SUB]


def group_of(lane, size):
    return lane >> log2(size)


def log2(n):
    assert n & (n - 1) == 0
    return n.bit_length() - 1


def kernel(
    nc, nv, patches,
    cap_ref, clip_ref, wf_ref, wp_ref, len_ref,
    loss_ref, cap_res, clip_res,
    cap_raw, clip_raw, wf_raw, wp_raw, qn, give, trade, q_full, q_pick, unit_keys, keys, key_inv, column,
    picked_rows, rows_in, tiles_in, scores_in, logits_in, tile_out, line_out, lines_out, weights, turned, grads_in, grad_out, spread_table, sums_table, caption_table, one_hot,
    len_raw,
    load_sem, trade_send, trade_recv, key_send, key_recv, pick_send, pick_recv, gather_send, gather_recv,
    spread_send, spread_recv, rows_send, rows_recv, tile_send, tile_recv, score_send, score_recv, logit_send, logit_recv, grad_send, grad_recv,
):
    nf = nc
    tok = nv
    me_c, me_v, me_f = lax.axis_index("cap"), lax.axis_index("clip"), lax.axis_index("frame")
    rows = 4 * patches
    per_block = tok * SUB
    all_tokens = nf * per_block
    tok_bits, block_bits = log2(tok), log2(per_block)

    half_clips, side_rows = nv // 2, nv // 4
    me_half, me_side = me_v // half_clips, lax.rem(me_v, 2)
    me_row = lax.rem(me_v, half_clips) // 2
    me_corner = me_half * 2 + me_side
    others_in_row, others_in_corner = nf * side_rows - 1, nc * 4 - 1

    loads = [
        pltpu.make_async_copy(clip_ref, clip_raw, load_sem.at[0]),
        pltpu.make_async_copy(cap_ref, cap_raw, load_sem.at[1]),
        pltpu.make_async_copy(wf_ref, wf_raw, load_sem.at[2]),
        pltpu.make_async_copy(wp_ref, wp_raw, load_sem.at[3]),
        pltpu.make_async_copy(len_ref, len_raw, load_sem.at[4]),
    ]
    logits_in[...] = jnp.zeros((4 * SUB, LANES), f32)

    barrier = pltpu.get_barrier_semaphore()

    def device(dc, dv, df):
        return {
            "cap": lax.rem(me_c + dc, nc),
            "clip": lax.rem(me_v + dv, nv),
            "frame": lax.rem(me_f + df, nf),
        }

    def signal(dc, dv, df):
        pl.semaphore_signal(barrier, inc=1, device_id=device(dc, dv, df), device_id_type=MESH)

    def at_clip(clip):
        return {"cap": me_c, "clip": clip, "frame": me_f}

    across = lax.rem(me_v + half_clips, nv)
    in_half = [me_half * half_clips + lax.rem(me_v + step, half_clips) for step in range(1, half_clips)]
    pl.semaphore_signal(barrier, inc=1, device_id=at_clip(across), device_id_type=MESH)
    for clip in in_half:
        pl.semaphore_signal(barrier, inc=1, device_id=at_clip(clip), device_id_type=MESH)
    for load in loads:
        load.start()
    for step in range(1, nf):
        signal(0, 0, step)
    for step in range(1, nc):
        signal(step, 0, 0)

    lane = iota((SUB, LANES), 1)
    sub = iota((SUB, LANES), 0)
    group = lane >> tok_bits
    slot_in_group = lane & (tok - 1)
    used = group < nc
    cap_lanes = LANES // nc

    loads[1].wait()
    raw = [cap_raw[pl.ds(j, SUB, stride=nc), :] for j in range(nc)]
    total = raw[0] * raw[0]
    for j in range(1, nc):
        total = total + raw[j] * raw[j]
    cap_inv = lax.rsqrt(jnp.sum(total, axis=1, keepdims=True) + norm_eps)
    for j in range(nc):
        unit = raw[j] * cap_inv
        qn[j] = unit
        give[j, 0:SUB, :] = unit

    for load in loads[2:]:
        load.wait()
    diagonal = iota((SUB, SUB), 0) == iota((SUB, SUB), 1)
    lengths = jnp.sum(jnp.where(diagonal, len_raw[...].astype(f32), 0.0), axis=1, keepdims=True)
    lengths = jnp.broadcast_to(lengths, (SUB, LANES))
    give[:, SUB : 3 * SUB, :] = jnp.zeros((nc, 2 * SUB, LANES), f32)
    for j in range(nc):
        give[j, SUB : 2 * SUB, 0:tok] = wf_raw[...].astype(f32)
        give[j, 2 * SUB : 3 * SUB, 0:tok] = wp_raw[...].astype(f32)
        give[j, 3 * SUB : 4 * SUB, :] = lengths

    pl.semaphore_wait(barrier, nc - 1 + nf - 1 + half_clips)

    own_rows = pl.ds(pl.multiple_of(me_v * SUB, SUB), SUB)

    def pick_copy(src, place, clip, sem):
        return pltpu.make_async_remote_copy(
            src_ref=src, dst_ref=q_pick.at[place], send_sem=pick_send.at[sem], recv_sem=pick_recv.at[sem],
            device_id=at_clip(clip), device_id_type=MESH,
        )

    across_copy = pick_copy(qn.at[me_f], own_rows, across, 0)
    across_copy.start()
    for clip in in_half:
        pick_copy(qn.at[me_f], own_rows, clip, 1).start()

    def trade_copy(d):
        to = lax.rem(me_c + d, nc)
        return pltpu.make_async_remote_copy(
            src_ref=give.at[to], dst_ref=trade.at[me_c], send_sem=trade_send.at[d], recv_sem=trade_recv.at[d],
            device_id=device(d, 0, 0), device_id_type=MESH,
        )

    trades = [trade_copy(d) for d in range(1, nc)]
    for copy in trades:
        copy.start()

    keys[:, rows:, :] = jnp.zeros((nf, keys.shape[1] - rows, LANES), f32)
    loads[0].wait()
    whole = clip_raw[...].reshape(patches, nc // 2, SUB, LANES)
    square = whole * whole
    summed = square[:, 0]
    for j in range(1, nc // 2):
        summed = summed + square[:, j]
    summed = summed + pltpu.roll(summed, 4, 1)
    inverse = lax.rsqrt(jnp.sum(summed, axis=2, keepdims=True) + norm_eps)
    low_half = iota((patches // 2, SUB, LANES), 1) < 4
    for j in range(nc // 2):
        unit = (whole[:, j] * inverse).reshape(patches // 2, 2, SUB, LANES)
        first, second = unit[:, 0], unit[:, 1]
        unit_keys[2 * j] = jnp.where(low_half, first, pltpu.roll(second, 4, 1)).reshape(rows, LANES)
        unit_keys[2 * j + 1] = jnp.where(low_half, pltpu.roll(first, 4, 1), second).reshape(rows, LANES)
    inverse = jnp.broadcast_to(inverse, (patches, SUB, LANES)).reshape(patches // 2, 2, SUB, LANES)
    key_inv[...] = jnp.where(low_half, inverse[:, 0], inverse[:, 1]).reshape(rows, LANES)


    def key_copy(d):
        return pltpu.make_async_remote_copy(
            src_ref=unit_keys.at[lax.rem(me_f + d, nf)], dst_ref=keys.at[me_f, pl.ds(0, rows)],
            send_sem=key_send.at[d], recv_sem=key_recv.at[d], device_id=device(0, 0, d), device_id_type=MESH,
        )

    key_copies = [key_copy(d) for d in range(1, nf)]
    for copy in key_copies:
        copy.start()

    trade[me_c] = give[me_c]
    keys[me_f, 0:rows, :] = unit_keys[me_f]
    q_pick[own_rows, :] = qn[me_f]

    frame_own = wf_raw[...]
    chunk = keys.shape[1]
    winner = (frame_own >> 2) * chunk + wp_raw[...] * 4 + (frame_own & 3)
    for t in range(tok):
        column[t * SUB : (t + 1) * SUB, :] = jnp.broadcast_to(winner[:, t : t + 1], (SUB, LANES))
    wide_lane = iota((per_block, chunk), 1)
    column_value = jnp.concatenate([column[...]] * (chunk // LANES), axis=1)

    def picked_from(d):
        part = lax.rem(me_f + nf - d, nf)
        chosen = (column_value == wide_lane + part * chunk).astype(f32).astype(bf16)
        both = dot(chosen, jnp.concatenate(two_terms(keys[part]), axis=1))
        return both[:, 0:LANES] + both[:, LANES:]

    picked = picked_from(0)

    from_row, to_row = iota((LANES, LANES), 0), iota((LANES, LANES), 1)
    of_caption, of_clip = (from_row & 7) == (to_row & 7), (from_row >> 3) == (to_row >> 3)
    sums_table[...] = jnp.concatenate([of_caption, of_clip], axis=1).astype(f32).astype(bf16)
    corner, block, at = (iota((4, SUB, LANES), d) for d in range(3))
    valid = (block < nc) & (at < side_rows * SUB)
    clip_id = (corner >> 1) * half_clips + (at >> 3) * 2 + (corner & 1)
    positive = (valid & (clip_id == block * SUB + (at & 7))).astype(f32)

    from_lane = iota((LANES, all_tokens), 0)
    token = iota((LANES, all_tokens), 1)
    spread_table[...] = (
        (from_lane == ((token >> block_bits) << tok_bits) + ((token & (per_block - 1)) >> 3)).astype(f32).astype(bf16)
    )
    caption_of = iota((all_tokens, LANES), 0)
    caption_lane = (caption_of >> block_bits) * (LANES // nc) + (caption_of & 7)
    caption_table[...] = (iota((all_tokens, LANES), 1) == caption_lane).astype(f32).astype(bf16)
    same_group = ((iota((LANES, LANES), 0) >> tok_bits) == (iota((LANES, LANES), 1) >> tok_bits)).astype(f32).astype(bf16)
    mine_of = (iota((SUB, all_tokens), 1) & 7) == iota((SUB, all_tokens), 0)

    def as_row(values):
        return jnp.sum(jnp.where(mine_of, values, 0.0), axis=0, keepdims=True)

    def gather_copy(clip, to, sem):
        place = q_full.at[me_f, clip // 2, lax.rem(clip, 2)]
        return pltpu.make_async_remote_copy(
            src_ref=place, dst_ref=place, send_sem=gather_send.at[sem], recv_sem=gather_recv.at[sem],
            device_id=at_clip(to), device_id_type=MESH,
        )

    for copy in trades:
        copy.wait()
    q_full[me_f, me_v // 2, me_side] = trade[me_f, 0:SUB, :]
    across_gather = gather_copy(me_v, across, 0)
    across_gather.start()

    across_copy.wait()
    across_rows = pl.ds(pl.multiple_of(across * SUB, SUB), SUB)
    for clip in in_half:
        pick_copy(q_pick.at[across_rows], across_rows, clip, 2).start()

    frames = jnp.zeros((SUB, LANES), f32)
    patch_all = jnp.zeros((SUB, LANES), f32)
    length = jnp.zeros((SUB, LANES), f32)
    for j in range(nc):
        here = group == j
        frames = jnp.where(here, pltpu.roll(trade[j, SUB : 2 * SUB, :], j * tok, 1), frames)
        patch_all = jnp.where(here, pltpu.roll(trade[j, 2 * SUB : 3 * SUB, :], j * tok, 1), patch_all)
        length = jnp.where(here, trade[j, 3 * SUB : 4 * SUB, :], length)
    frames = frames.astype(jnp.int32)
    live = (slot_in_group.astype(f32) < length) & used
    safe_length = jnp.maximum(length, 1.0)
    local = jnp.where(((frames >> 2) == me_f) & used, patch_all.astype(jnp.int32) * 4 + (frames & 3), 255)
    twice = jnp.concatenate([local.astype(f32), jnp.zeros((SUB, LANES), f32)], axis=0).astype(bf16)
    local_row = as_row(dot(twice, spread_table[...])[0:SUB]).astype(jnp.int32)
    one_hot[...] = (iota((rows, all_tokens), 0) == local_row).astype(f32).astype(bf16)

    across_gather.wait()
    for dr in range(1, side_rows):
        to = me_half * half_clips + lax.rem(me_row + dr, side_rows) * 2 + me_side
        gather_copy(me_v, to, 1).start()
        gather_copy(across, to, 1).start()

    for d in [d for d in range(1, nf) if d != nf // 2] + [nf // 2]:
        key_copies[d - 1].wait()
        picked = picked + picked_from(d)
    picked_rows[...] = picked

    half_but_one = q_pick.at[pl.ds(0, (half_clips - 1) * SUB)]
    for sem in (1, 2):
        pltpu.make_async_copy(half_but_one, half_but_one, pick_recv.at[sem]).wait()
    product = (picked * q_pick[...]).reshape(tok, SUB, LANES)

    when = iota((tok, SUB, LANES), 0).astype(f32)
    score = jnp.sum(jnp.sum(jnp.where(when < lengths[None], product, 0.0), axis=0), axis=1, keepdims=True)
    score = score * logit_scale / lengths
    own_score = pl.ds(me_f * side_rows + me_row, 1)
    line_out[...] = jnp.sum(jnp.where(lane == me_row * SUB + sub, score, 0.0), axis=0, keepdims=True)
    scores_in[own_score, :] = line_out[...]

    def apart(step, size):
        return min(step, size - step)

    row_steps = [(dr, df) for dr in range(side_rows) for df in range(nf)][1:]
    for dr, df in sorted(row_steps, key=lambda p: -apart(p[0], side_rows) - apart(p[1], nf)):
        to = {
            "cap": me_c,
            "clip": me_half * half_clips + lax.rem(me_row + dr, side_rows) * 2 + me_side,
            "frame": lax.rem(me_f + df, nf),
        }
        pltpu.make_async_remote_copy(
            src_ref=line_out, dst_ref=scores_in.at[own_score], send_sem=score_send, recv_sem=score_recv,
            device_id=to, device_id_type=MESH,
        ).start()

    rows_in[me_v] = picked_rows[own_rows, :]

    @pl.loop(1, nv)
    def _(step):
        to = lax.rem(me_v + step, nv)
        pltpu.make_async_remote_copy(
            src_ref=picked_rows.at[pl.ds(pl.multiple_of(to * SUB, SUB), SUB)], dst_ref=rows_in.at[me_v],
            send_sem=rows_send, recv_sem=rows_recv, device_id=device(0, step, 0), device_id_type=MESH,
        ).start()

    tile = jnp.zeros((SUB, LANES), f32)
    for t in range(tok):
        tile = jnp.where(lane == me_c * tok + t, jnp.sum(product[t], axis=1, keepdims=True), tile)
    tile_out[...] = tile
    me_16 = me_c * nf + me_f
    tiles_in[me_16] = tile

    @pl.loop(1, nc * nf)
    def _(step):
        pltpu.make_async_remote_copy(
            src_ref=tile_out, dst_ref=tiles_in.at[me_16], send_sem=tile_send, recv_sem=tile_recv,
            device_id=device(step // nf, 0, lax.rem(step, nf)), device_id_type=MESH,
        ).start()

    row_tiles = q_full.at[0, pl.ds(0, side_rows - 1)]
    pltpu.make_async_copy(row_tiles, row_tiles, gather_recv.at[1]).wait()
    side_tiles = q_full.at[me_f, pl.ds(0, half_clips), me_side]

    def spread_copy(d):
        return pltpu.make_async_remote_copy(
            src_ref=side_tiles, dst_ref=side_tiles, send_sem=spread_send.at[d], recv_sem=spread_recv.at[d],
            device_id=device(0, 0, d), device_id_type=MESH,
        )

    spreads = [spread_copy(d) for d in range(1, nf)]
    for copy in spreads:
        copy.start()

    other_scores = scores_in.at[pl.ds(0, others_in_row)]
    pltpu.make_async_copy(other_scores, other_scores, score_recv).wait()
    lines_out[...] = jnp.sum(scores_in[...], axis=0, keepdims=True)
    own_slot = pl.ds(me_corner * SUB + me_c, 1)
    logits_in[own_slot, :] = lines_out[...]

    corner_steps = [(dh, ds, dc) for dh in (1, 0) for ds in (0, 1) for dc in range(nc)]
    for dh, ds, dc in corner_steps:
        if (dh, ds, dc) == (0, 0, 0):
            continue
        to_half, to_side = lax.rem(me_half + dh, 2), lax.rem(me_side + ds, 2)
        to = {
            "cap": lax.rem(me_c + dc, nc),
            "clip": to_half * half_clips + me_row * 2 + to_side,
            "frame": me_f,
        }
        pltpu.make_async_remote_copy(
            src_ref=lines_out, dst_ref=logits_in.at[own_slot], send_sem=logit_send, recv_sem=logit_recv,
            device_id=to, device_id_type=MESH,
        ).start()

    other_tiles = tiles_in.at[pl.ds(0, nc * nf - 1)]
    other_clips = rows_in.at[pl.ds(0, nv - 1)]
    pltpu.make_async_copy(other_tiles, other_tiles, tile_recv).wait()
    live_share = jnp.where(live, jnp.sum(tiles_in[...], axis=0), 0.0)
    share_row = as_row(times_exact(live_share / safe_length, spread_table[...]))
    share_high, share_low = two_terms(one_hot[...].astype(f32) * share_row)
    inner_table = dot(share_high, caption_table[...]) + dot(share_low, caption_table[...])
    for copy in spreads:
        copy.wait()
    all_tiles = q_full.at[pl.ds(0, nf), pl.ds(0, half_clips), me_side]
    side_copy = pltpu.make_async_remote_copy(
        src_ref=all_tiles, dst_ref=all_tiles, send_sem=gather_send.at[2], recv_sem=gather_recv.at[2],
        device_id=at_clip(me_v + 1 - 2 * me_side), device_id_type=MESH,
    )
    side_copy.start()
    pltpu.make_async_copy(other_clips, other_clips, rows_recv).wait()

    length_lines = jnp.zeros((SUB, LANES), f32)
    for j in range(nc):
        line = jnp.sum(jnp.where((lane & 7) == sub, trade[j, 3 * SUB : 4 * SUB, :], 0.0), axis=0, keepdims=True)
        length_lines = jnp.where(sub == j, line, length_lines)
    inverse_length = 1.0 / jnp.maximum(length_lines, 1.0)

    other_logits = logits_in.at[pl.ds(0, others_in_corner)]
    pltpu.make_async_copy(other_logits, other_logits, logit_recv).wait()
    logits = logits_in[...]
    exp_logits = jnp.where(valid, jnp.exp(logits).reshape(4, SUB, LANES), 0.0)
    terms = jnp.concatenate(three_terms(exp_logits.reshape(4 * SUB, LANES)), axis=0).astype(bf16)
    sums = dot(terms, sums_table[...]).reshape(3, 4, SUB, 2 * LANES)
    sums = sums[0] + sums[1] + sums[2]
    row_total = jnp.where(valid[0], jnp.sum(sums[:, :, 0:LANES], axis=0), 1.0)
    col_total = jnp.where(at[:, 0:1] < side_rows * SUB, jnp.sum(sums[:, :, LANES:], axis=1, keepdims=True), 1.0)
    grad = logit_scale * (exp_logits * (0.5 / row_total + 0.5 / col_total) - positive)
    weights[...] = grad.reshape(4 * SUB, LANES)
    block_grad = jnp.sum(jnp.where(block == me_c, grad * inverse_length, 0.0), axis=1, keepdims=True)
    turned[...] = jnp.transpose(jnp.broadcast_to(block_grad, (4, SUB, LANES)).reshape(4 * SUB, LANES))

    slice_grad = jnp.zeros((SUB, LANES), f32)
    for v in range(nv):
        of_row, of_corner = v % half_clips // 2 * SUB, (v // half_clips * 2 + v % 2) * SUB
        slice_grad = slice_grad + turned[of_row : of_row + SUB, of_corner : of_corner + 1] * rows_in[v]
    slice_grad = jnp.where(me_v.astype(f32) < lengths, slice_grad, 0.0)
    grad_out[...] = slice_grad
    grads_in[me_f] = slice_grad

    def grad_copy(d):
        return pltpu.make_async_remote_copy(
            src_ref=grad_out, dst_ref=grads_in.at[me_f], send_sem=grad_send.at[d], recv_sem=grad_recv.at[d],
            device_id=device(0, 0, d), device_id_type=MESH,
        )

    grad_copies = [grad_copy(d) for d in range(1, nf)]
    for copy in grad_copies:
        copy.start()

    own_lines = weights[pl.ds(pl.multiple_of(me_corner * SUB, SUB), SUB), :]
    own_grad = jnp.zeros((SUB, LANES), f32)
    token_weight = []
    for j in range(nc):
        value = jnp.sum(jnp.where(lane == me_row * SUB + sub, own_lines[j : j + 1], 0.0), axis=1, keepdims=True)
        own_grad = jnp.where(lane == j * cap_lanes + sub, value, own_grad)
        token_weight.append(value / jnp.maximum(trade[j, 3 * SUB : 4 * SUB, :], 1.0))
    own_grad = jnp.sum(own_grad, axis=0, keepdims=True)
    inner = jnp.sum(inner_table * own_grad, axis=1, keepdims=True)
    side_copy.wait()
    parts = []
    for j in range(nc):
        mask = when < trade[j, 3 * SUB : 4 * SUB, :][None]
        scaled = q_full[j].reshape(tok, SUB, LANES) * jnp.where(mask, token_weight[j][None], 0.0)
        parts.append(jnp.concatenate(two_terms(scaled.reshape(per_block, LANES)), axis=1))
    both = dot(one_hot[...], jnp.concatenate(parts, axis=0))
    clip_res[...] = key_inv[...] * (both[:, 0:LANES] + both[:, LANES:] - unit_keys[me_c] * inner)

    row_terms = jnp.where((sub < nc) & (lane < SUB), jnp.log(row_total), 0.0)
    col_terms = jnp.where((at[:, 0:1] & 7) == 0, jnp.log(col_total), 0.0)
    terms = 0.5 * jnp.sum(row_terms) + 0.5 * jnp.sum(col_terms)
    terms = terms - jnp.sum(positive * logits.reshape(4, SUB, LANES))
    loss_ref[...] = jnp.broadcast_to(terms / (nc * SUB), (1, 1))

    for copy in grad_copies:
        copy.wait()
    dot_tile = jnp.zeros((SUB, LANES), f32)
    for j in range(nc):
        dot_tile = dot_tile + qn[j] * grads_in[j]
    cap_inner = jnp.sum(dot_tile, axis=1, keepdims=True)
    for j in range(nc):
        cap_res[pl.ds(j, SUB, stride=nc), :] = cap_inv * (grads_in[j] - qn[j] * cap_inner)

    for sem in (1, 2):
        pltpu.make_async_copy(half_but_one, half_but_one, pick_send.at[sem]).wait()
    pltpu.make_async_copy(row_tiles, row_tiles, gather_send.at[1]).wait()
    pltpu.make_async_copy(other_clips, other_clips, rows_send).wait()
    pltpu.make_async_copy(other_scores, other_scores, score_send).wait()
    pltpu.make_async_copy(other_logits, other_logits, logit_send).wait()
    pltpu.make_async_copy(other_tiles, other_tiles, tile_send).wait()


def body(nc, nv, cap_tokens, clip_tokens, win_frame, win_patch, cap_lengths):
    block, _, width = cap_tokens.shape
    _, frames, patches, _ = clip_tokens.shape
    assert block == SUB and frames == 4 and width == nc * LANES and win_frame.shape == (SUB, nv, 1)
    rows = frames * patches
    per_block = nv * SUB
    caps = cap_tokens.reshape(SUB * nc, LANES)
    clips = clip_tokens.reshape(frames, patches, nc, LANES).transpose(1, 2, 0, 3).reshape(patches, nc * frames, LANES)
    vmem = pltpu.VMEM
    dma = pltpu.SemaphoreType.DMA
    scratch = [
        vmem((SUB * nc, LANES), f32),
        vmem((patches, nc * frames, LANES), f32),
        vmem((SUB, nv), jnp.int32),
        vmem((SUB, nv), jnp.int32),
        vmem((nc, SUB, LANES), f32),
        vmem((nc, 4 * SUB, LANES), f32),
        vmem((nc, 4 * SUB, LANES), f32),
        vmem((nc, nv // 2, 2, SUB, LANES), f32),
        vmem((per_block, LANES), f32),
        vmem((nc, rows, LANES), f32),
        vmem((nc, -(-rows // LANES) * LANES, LANES), f32),
        vmem((rows, LANES), f32),
        vmem((per_block, LANES), jnp.int32),
        vmem((per_block, LANES), f32),
        vmem((nv, SUB, LANES), f32),
        vmem((nc * nc, SUB, LANES), f32),
        vmem((nc * nv // 4, LANES), f32),
        vmem((4 * SUB, LANES), f32),
        vmem((SUB, LANES), f32),
        vmem((1, LANES), f32),
        vmem((1, LANES), f32),
        vmem((4 * SUB, LANES), f32),
        vmem((LANES, 4 * SUB), f32),
        vmem((nc, SUB, LANES), f32),
        vmem((SUB, LANES), f32),
        vmem((LANES, nc * per_block), bf16),
        vmem((LANES, 2 * LANES), bf16),
        vmem((nc * per_block, LANES), bf16),
        vmem((rows, nc * per_block), bf16),
        vmem((1, SUB), jnp.int32),
        dma((5,)),
        dma((nc,)), dma((nc,)), dma((nc,)), dma((nc,)),
        dma((3,)), dma((3,)), dma((3,)), dma((3,)),
        dma((nc,)), dma((nc,)),
        dma, dma, dma, dma, dma, dma, dma, dma,
        dma((nc,)), dma((nc,)),
    ]
    hbm = pl.BlockSpec(memory_space=pl.ANY)
    near = pl.BlockSpec(memory_space=pltpu.VMEM)
    in_hbm = functools.partial(pltpu.with_memory_space_constraint, memory_space=pltpu.HBM)
    operands = (caps, clips, win_frame.reshape(SUB, nv), win_patch.reshape(SUB, nv), cap_lengths.reshape(1, SUB))
    shapes = ((1, 1), (SUB * nc, LANES), (rows, LANES))
    loss, cap_grad, clip_grad = pl.pallas_call(
        functools.partial(kernel, nc, nv, patches),
        out_shape=[vmem(shape, f32) for shape in shapes],
        in_specs=[hbm] * 5,
        out_specs=[near] * 3,
        scratch_shapes=scratch,
        compiler_params=pltpu.CompilerParams(
            collective_id=0, has_side_effects=True, vmem_limit_bytes=32 * 1024 * 1024
        ),
    )(*map(in_hbm, operands))
    clip_grad = clip_grad.reshape(patches, frames, LANES).transpose(1, 0, 2)[None]
    return loss.reshape(()), cap_grad.reshape(SUB, 1, width), clip_grad


def solution(mesh):
    placed = (
        P("cap", "clip", None),
        P("clip", "frame", None, None),
        P("cap", None, "clip"),
        P("cap", None, "clip"),
        P("cap"),
    )
    assert mesh.shape["cap"] == mesh.shape["frame"]
    return jax.shard_map(
        functools.partial(body, mesh.shape["cap"], mesh.shape["clip"]),
        mesh=mesh,
        in_specs=placed,
        out_specs=(P(), P("cap", "clip", None), P("clip", "frame", None, "cap")),
        check_vma=False,
    )
```

```python
import functools

import jax
import jax.numpy as jnp
from jax import lax
from jax.experimental import pallas as pl
from jax.experimental.pallas import tpu as pltpu
from jax.sharding import PartitionSpec as P

MESH = pl.DeviceIdType.MESH
logit_scale = 1.0 / 0.07
norm_eps = 1e-06
f32 = jnp.float32
bf16 = jnp.bfloat16
LANES = 128
SUB = 8


def iota(shape, dim):
    return lax.broadcasted_iota(jnp.int32, shape, dim)


def two_terms(x):
    high = x.astype(bf16)
    return high, (x - high.astype(f32)).astype(bf16)


def three_terms(x):
    high = x.astype(bf16).astype(f32)
    rest = x - high
    middle = rest.astype(bf16).astype(f32)
    return high, middle, rest - middle


def dot(a, b):
    return jnp.dot(a, b, preferred_element_type=f32)


def times_exact(tile, table):
    high, middle, low = three_terms(tile)
    stacked = jnp.concatenate([high, middle, low, jnp.zeros_like(high)], axis=0).astype(bf16)
    out = dot(stacked, table)
    return out[0:SUB] + out[SUB : 2 * SUB] + out[2 * SUB : 3 * SUB]


def group_of(lane, size):
    return lane >> log2(size)


def log2(n):
    assert n & (n - 1) == 0
    return n.bit_length() - 1


def kernel(
    nc, nv, patches,
    cap_ref, clip_ref, wf_ref, wp_ref, len_ref,
    loss_ref, cap_res, clip_res,
    cap_raw, clip_raw, wf_raw, wp_raw, qn, give, trade, q_full, q_pick, unit_keys, keys, key_inv, column,
    picked_rows, rows_in, tiles_in, scores_in, logits_in, tile_out, line_out, lines_out, weights, turned, grads_in, grad_out, spread_table, sums_table, caption_table, one_hot,
    len_raw,
    load_sem, trade_send, trade_recv, key_send, key_recv, pick_send, pick_recv, gather_send, gather_recv,
    spread_send, spread_recv, rows_send, rows_recv, tile_send, tile_recv, score_send, score_recv, logit_send, logit_recv, grad_send, grad_recv,
):
    nf = nc
    tok = nv
    me_c, me_v, me_f = lax.axis_index("cap"), lax.axis_index("clip"), lax.axis_index("frame")
    rows = 4 * patches
    per_block = tok * SUB
    all_tokens = nf * per_block
    tok_bits, block_bits = log2(tok), log2(per_block)

    half_clips, side_rows = nv // 2, nv // 4
    me_half, me_side = me_v // half_clips, lax.rem(me_v, 2)
    me_row = lax.rem(me_v, half_clips) // 2
    me_corner = me_half * 2 + me_side
    others_in_row, others_in_corner = nf * side_rows - 1, nc * 4 - 1

    loads = [
        pltpu.make_async_copy(clip_ref, clip_raw, load_sem.at[0]),
        pltpu.make_async_copy(cap_ref, cap_raw, load_sem.at[1]),
        pltpu.make_async_copy(wf_ref, wf_raw, load_sem.at[2]),
        pltpu.make_async_copy(wp_ref, wp_raw, load_sem.at[3]),
        pltpu.make_async_copy(len_ref, len_raw, load_sem.at[4]),
    ]
    logits_in[...] = jnp.zeros((4 * SUB, LANES), f32)

    barrier = pltpu.get_barrier_semaphore()

    def device(dc, dv, df):
        return {
            "cap": lax.rem(me_c + dc, nc),
            "clip": lax.rem(me_v + dv, nv),
            "frame": lax.rem(me_f + df, nf),
        }

    def signal(dc, dv, df):
        pl.semaphore_signal(barrier, inc=1, device_id=device(dc, dv, df), device_id_type=MESH)

    def at_clip(clip):
        return {"cap": me_c, "clip": clip, "frame": me_f}

    across = lax.rem(me_v + half_clips, nv)
    in_half = [me_half * half_clips + lax.rem(me_v + step, half_clips) for step in range(1, half_clips)]
    pl.semaphore_signal(barrier, inc=1, device_id=at_clip(across), device_id_type=MESH)
    for clip in in_half:
        pl.semaphore_signal(barrier, inc=1, device_id=at_clip(clip), device_id_type=MESH)
    for load in loads:
        load.start()
    for step in range(1, nf):
        signal(0, 0, step)
    for step in range(1, nc):
        signal(step, 0, 0)

    lane = iota((SUB, LANES), 1)
    sub = iota((SUB, LANES), 0)
    group = lane >> tok_bits
    slot_in_group = lane & (tok - 1)
    used = group < nc
    cap_lanes = LANES // nc

    loads[1].wait()
    raw = [cap_raw[pl.ds(j, SUB, stride=nc), :] for j in range(nc)]
    total = raw[0] * raw[0]
    for j in range(1, nc):
        total = total + raw[j] * raw[j]
    cap_inv = lax.rsqrt(jnp.sum(total, axis=1, keepdims=True) + norm_eps)
    for j in range(nc):
        unit = raw[j] * cap_inv
        qn[j] = unit
        give[j, 0:SUB, :] = unit

    for load in loads[2:]:
        load.wait()
    diagonal = iota((SUB, SUB), 0) == iota((SUB, SUB), 1)
    lengths = jnp.sum(jnp.where(diagonal, len_raw[...].astype(f32), 0.0), axis=1, keepdims=True)
    lengths = jnp.broadcast_to(lengths, (SUB, LANES))
    give[:, SUB : 3 * SUB, :] = jnp.zeros((nc, 2 * SUB, LANES), f32)
    for j in range(nc):
        give[j, SUB : 2 * SUB, 0:tok] = wf_raw[...].astype(f32)
        give[j, 2 * SUB : 3 * SUB, 0:tok] = wp_raw[...].astype(f32)
        give[j, 3 * SUB : 4 * SUB, :] = lengths

    pl.semaphore_wait(barrier, nc - 1 + nf - 1 + half_clips)

    own_rows = pl.ds(pl.multiple_of(me_v * SUB, SUB), SUB)

    def pick_copy(src, place, clip, sem):
        return pltpu.make_async_remote_copy(
            src_ref=src, dst_ref=q_pick.at[place], send_sem=pick_send.at[sem], recv_sem=pick_recv.at[sem],
            device_id=at_clip(clip), device_id_type=MESH,
        )

    across_copy = pick_copy(qn.at[me_f], own_rows, across, 0)
    across_copy.start()
    for clip in in_half:
        pick_copy(qn.at[me_f], own_rows, clip, 1).start()

    def trade_copy(d):
        to = lax.rem(me_c + d, nc)
        return pltpu.make_async_remote_copy(
            src_ref=give.at[to], dst_ref=trade.at[me_c], send_sem=trade_send.at[d], recv_sem=trade_recv.at[d],
            device_id=device(d, 0, 0), device_id_type=MESH,
        )

    trades = [trade_copy(d) for d in range(1, nc)]
    for copy in trades:
        copy.start()

    keys[:, rows:, :] = jnp.zeros((nf, keys.shape[1] - rows, LANES), f32)
    loads[0].wait()
    whole = clip_raw[...].reshape(patches, nc // 2, SUB, LANES)
    square = whole * whole
    summed = square[:, 0]
    for j in range(1, nc // 2):
        summed = summed + square[:, j]
    summed = summed + pltpu.roll(summed, 4, 1)
    inverse = lax.rsqrt(jnp.sum(summed, axis=2, keepdims=True) + norm_eps)
    low_half = iota((patches // 2, SUB, LANES), 1) < 4
    for j in range(nc // 2):
        unit = (whole[:, j] * inverse).reshape(patches // 2, 2, SUB, LANES)
        first, second = unit[:, 0], unit[:, 1]
        unit_keys[2 * j] = jnp.where(low_half, first, pltpu.roll(second, 4, 1)).reshape(rows, LANES)
        unit_keys[2 * j + 1] = jnp.where(low_half, pltpu.roll(first, 4, 1), second).reshape(rows, LANES)
    inverse = jnp.broadcast_to(inverse, (patches, SUB, LANES)).reshape(patches // 2, 2, SUB, LANES)
    key_inv[...] = jnp.where(low_half, inverse[:, 0], inverse[:, 1]).reshape(rows, LANES)


    def key_copy(d):
        return pltpu.make_async_remote_copy(
            src_ref=unit_keys.at[lax.rem(me_f + d, nf)], dst_ref=keys.at[me_f, pl.ds(0, rows)],
            send_sem=key_send.at[d], recv_sem=key_recv.at[d], device_id=device(0, 0, d), device_id_type=MESH,
        )

    key_copies = [key_copy(d) for d in range(1, nf)]
    for copy in key_copies:
        copy.start()

    trade[me_c] = give[me_c]
    keys[me_f, 0:rows, :] = unit_keys[me_f]
    q_pick[own_rows, :] = qn[me_f]

    frame_own = wf_raw[...]
    chunk = keys.shape[1]
    winner = (frame_own >> 2) * chunk + wp_raw[...] * 4 + (frame_own & 3)
    for t in range(tok):
        column[t * SUB : (t + 1) * SUB, :] = jnp.broadcast_to(winner[:, t : t + 1], (SUB, LANES))
    wide_lane = iota((per_block, chunk), 1)
    column_value = jnp.concatenate([column[...]] * (chunk // LANES), axis=1)

    def picked_from(d):
        part = lax.rem(me_f + nf - d, nf)
        chosen = (column_value == wide_lane + part * chunk).astype(f32).astype(bf16)
        both = dot(chosen, jnp.concatenate(two_terms(keys[part]), axis=1))
        return both[:, 0:LANES] + both[:, LANES:]

    picked = picked_from(0)

    from_row, to_row = iota((LANES, LANES), 0), iota((LANES, LANES), 1)
    of_caption, of_clip = (from_row & 7) == (to_row & 7), (from_row >> 3) == (to_row >> 3)
    sums_table[...] = jnp.concatenate([of_caption, of_clip], axis=1).astype(f32).astype(bf16)
    corner, block, at = (iota((4, SUB, LANES), d) for d in range(3))
    valid = (block < nc) & (at < side_rows * SUB)
    clip_id = (corner >> 1) * half_clips + (at >> 3) * 2 + (corner & 1)
    positive = (valid & (clip_id == block * SUB + (at & 7))).astype(f32)

    from_lane = iota((LANES, all_tokens), 0)
    token = iota((LANES, all_tokens), 1)
    spread_table[...] = (
        (from_lane == ((token >> block_bits) << tok_bits) + ((token & (per_block - 1)) >> 3)).astype(f32).astype(bf16)
    )
    caption_of = iota((all_tokens, LANES), 0)
    caption_lane = (caption_of >> block_bits) * (LANES // nc) + (caption_of & 7)
    caption_table[...] = (iota((all_tokens, LANES), 1) == caption_lane).astype(f32).astype(bf16)
    same_group = ((iota((LANES, LANES), 0) >> tok_bits) == (iota((LANES, LANES), 1) >> tok_bits)).astype(f32).astype(bf16)
    mine_of = (iota((SUB, all_tokens), 1) & 7) == iota((SUB, all_tokens), 0)

    def as_row(values):
        return jnp.sum(jnp.where(mine_of, values, 0.0), axis=0, keepdims=True)

    def gather_copy(clip, to, sem):
        place = q_full.at[me_f, clip // 2, lax.rem(clip, 2)]
        return pltpu.make_async_remote_copy(
            src_ref=place, dst_ref=place, send_sem=gather_send.at[sem], recv_sem=gather_recv.at[sem],
            device_id=at_clip(to), device_id_type=MESH,
        )

    for copy in trades:
        copy.wait()
    q_full[me_f, me_v // 2, me_side] = trade[me_f, 0:SUB, :]
    across_gather = gather_copy(me_v, across, 0)
    across_gather.start()

    across_copy.wait()
    across_rows = pl.ds(pl.multiple_of(across * SUB, SUB), SUB)
    for clip in in_half:
        pick_copy(q_pick.at[across_rows], across_rows, clip, 2).start()

    frames = jnp.zeros((SUB, LANES), f32)
    patch_all = jnp.zeros((SUB, LANES), f32)
    length = jnp.zeros((SUB, LANES), f32)
    for j in range(nc):
        here = group == j
        frames = jnp.where(here, pltpu.roll(trade[j, SUB : 2 * SUB, :], j * tok, 1), frames)
        patch_all = jnp.where(here, pltpu.roll(trade[j, 2 * SUB : 3 * SUB, :], j * tok, 1), patch_all)
        length = jnp.where(here, trade[j, 3 * SUB : 4 * SUB, :], length)
    frames = frames.astype(jnp.int32)
    live = (slot_in_group.astype(f32) < length) & used
    safe_length = jnp.maximum(length, 1.0)
    local = jnp.where(((frames >> 2) == me_f) & used, patch_all.astype(jnp.int32) * 4 + (frames & 3), 255)
    twice = jnp.concatenate([local.astype(f32), jnp.zeros((SUB, LANES), f32)], axis=0).astype(bf16)
    local_row = as_row(dot(twice, spread_table[...])[0:SUB]).astype(jnp.int32)
    one_hot[...] = (iota((rows, all_tokens), 0) == local_row).astype(f32).astype(bf16)

    across_gather.wait()
    for dr in range(1, side_rows):
        to = me_half * half_clips + lax.rem(me_row + dr, side_rows) * 2 + me_side
        gather_copy(me_v, to, 1).start()
        gather_copy(across, to, 1).start()

    for d in [d for d in range(1, nf) if d != nf // 2] + [nf // 2]:
        key_copies[d - 1].wait()
        picked = picked + picked_from(d)
    picked_rows[...] = picked

    half_but_one = q_pick.at[pl.ds(0, (half_clips - 1) * SUB)]
    for sem in (1, 2):
        pltpu.make_async_copy(half_but_one, half_but_one, pick_recv.at[sem]).wait()
    product = (picked * q_pick[...]).reshape(tok, SUB, LANES)

    when = iota((tok, SUB, LANES), 0).astype(f32)
    score = jnp.sum(jnp.sum(jnp.where(when < lengths[None], product, 0.0), axis=0), axis=1, keepdims=True)
    score = score * logit_scale / lengths
    own_score = pl.ds(me_f * side_rows + me_row, 1)
    line_out[...] = jnp.sum(jnp.where(lane == me_row * SUB + sub, score, 0.0), axis=0, keepdims=True)
    scores_in[own_score, :] = line_out[...]

    def apart(step, size):
        return min(step, size - step)

    row_steps = [(dr, df) for dr in range(side_rows) for df in range(nf)][1:]
    for dr, df in sorted(row_steps, key=lambda p: -apart(p[0], side_rows) - apart(p[1], nf)):
        to = {
            "cap": me_c,
            "clip": me_half * half_clips + lax.rem(me_row + dr, side_rows) * 2 + me_side,
            "frame": lax.rem(me_f + df, nf),
        }
        pltpu.make_async_remote_copy(
            src_ref=line_out, dst_ref=scores_in.at[own_score], send_sem=score_send, recv_sem=score_recv,
            device_id=to, device_id_type=MESH,
        ).start()

    rows_in[me_v] = picked_rows[own_rows, :]

    @pl.loop(1, nv)
    def _(step):
        to = lax.rem(me_v + step, nv)
        pltpu.make_async_remote_copy(
            src_ref=picked_rows.at[pl.ds(pl.multiple_of(to * SUB, SUB), SUB)], dst_ref=rows_in.at[me_v],
            send_sem=rows_send, recv_sem=rows_recv, device_id=device(0, step, 0), device_id_type=MESH,
        ).start()

    tile = jnp.zeros((SUB, LANES), f32)
    for t in range(tok):
        tile = jnp.where(lane == me_c * tok + t, jnp.sum(product[t], axis=1, keepdims=True), tile)
    tile_out[...] = tile
    me_16 = me_c * nf + me_f
    tiles_in[me_16] = tile

    @pl.loop(1, nc * nf)
    def _(step):
        pltpu.make_async_remote_copy(
            src_ref=tile_out, dst_ref=tiles_in.at[me_16], send_sem=tile_send, recv_sem=tile_recv,
            device_id=device(step // nf, 0, lax.rem(step, nf)), device_id_type=MESH,
        ).start()

    row_tiles = q_full.at[0, pl.ds(0, side_rows - 1)]
    pltpu.make_async_copy(row_tiles, row_tiles, gather_recv.at[1]).wait()
    side_tiles = q_full.at[me_f, pl.ds(0, half_clips), me_side]

    def spread_copy(d):
        return pltpu.make_async_remote_copy(
            src_ref=side_tiles, dst_ref=side_tiles, send_sem=spread_send.at[d], recv_sem=spread_recv.at[d],
            device_id=device(0, 0, d), device_id_type=MESH,
        )

    spreads = [spread_copy(d) for d in range(1, nf)]
    for copy in spreads:
        copy.start()

    other_scores = scores_in.at[pl.ds(0, others_in_row)]
    pltpu.make_async_copy(other_scores, other_scores, score_recv).wait()
    lines_out[...] = jnp.sum(scores_in[...], axis=0, keepdims=True)
    own_slot = pl.ds(me_corner * SUB + me_c, 1)
    logits_in[own_slot, :] = lines_out[...]

    corner_steps = [(dh, ds, dc) for dh in (1, 0) for ds in (0, 1) for dc in range(nc)]
    for dh, ds, dc in corner_steps:
        if (dh, ds, dc) == (0, 0, 0):
            continue
        to_half, to_side = lax.rem(me_half + dh, 2), lax.rem(me_side + ds, 2)
        to = {
            "cap": lax.rem(me_c + dc, nc),
            "clip": to_half * half_clips + me_row * 2 + to_side,
            "frame": me_f,
        }
        pltpu.make_async_remote_copy(
            src_ref=lines_out, dst_ref=logits_in.at[own_slot], send_sem=logit_send, recv_sem=logit_recv,
            device_id=to, device_id_type=MESH,
        ).start()

    other_tiles = tiles_in.at[pl.ds(0, nc * nf - 1)]
    other_clips = rows_in.at[pl.ds(0, nv - 1)]
    pltpu.make_async_copy(other_tiles, other_tiles, tile_recv).wait()
    live_share = jnp.where(live, jnp.sum(tiles_in[...], axis=0), 0.0)
    share_row = as_row(times_exact(live_share / safe_length, spread_table[...]))
    share_high, share_low = two_terms(one_hot[...].astype(f32) * share_row)
    inner_table = dot(share_high, caption_table[...]) + dot(share_low, caption_table[...])
    for copy in spreads:
        copy.wait()
    all_tiles = q_full.at[pl.ds(0, nf), pl.ds(0, half_clips), me_side]
    side_copy = pltpu.make_async_remote_copy(
        src_ref=all_tiles, dst_ref=all_tiles, send_sem=gather_send.at[2], recv_sem=gather_recv.at[2],
        device_id=at_clip(me_v + 1 - 2 * me_side), device_id_type=MESH,
    )
    side_copy.start()
    pltpu.make_async_copy(other_clips, other_clips, rows_recv).wait()

    length_lines = jnp.zeros((SUB, LANES), f32)
    for j in range(nc):
        line = jnp.sum(jnp.where((lane & 7) == sub, trade[j, 3 * SUB : 4 * SUB, :], 0.0), axis=0, keepdims=True)
        length_lines = jnp.where(sub == j, line, length_lines)
    inverse_length = 1.0 / jnp.maximum(length_lines, 1.0)

    other_logits = logits_in.at[pl.ds(0, others_in_corner)]
    pltpu.make_async_copy(other_logits, other_logits, logit_recv).wait()
    logits = logits_in[...]
    exp_logits = jnp.where(valid, jnp.exp(logits).reshape(4, SUB, LANES), 0.0)
    terms = jnp.concatenate(three_terms(exp_logits.reshape(4 * SUB, LANES)), axis=0).astype(bf16)
    sums = dot(terms, sums_table[...]).reshape(3, 4, SUB, 2 * LANES)
    sums = sums[0] + sums[1] + sums[2]
    row_total = jnp.where(valid[0], jnp.sum(sums[:, :, 0:LANES], axis=0), 1.0)
    col_total = jnp.where(at[:, 0:1] < side_rows * SUB, jnp.sum(sums[:, :, LANES:], axis=1, keepdims=True), 1.0)
    grad = logit_scale * (exp_logits * (0.5 / row_total + 0.5 / col_total) - positive)
    weights[...] = grad.reshape(4 * SUB, LANES)
    block_grad = jnp.sum(jnp.where(block == me_c, grad * inverse_length, 0.0), axis=1, keepdims=True)
    turned[...] = jnp.transpose(jnp.broadcast_to(block_grad, (4, SUB, LANES)).reshape(4 * SUB, LANES))

    shares = [jnp.zeros((SUB, LANES), f32)] * 4
    for v in range(nv):
        of_row, of_corner = v % half_clips // 2 * SUB, (v // half_clips * 2 + v % 2) * SUB
        shares[v % 4] = shares[v % 4] + turned[of_row : of_row + SUB, of_corner : of_corner + 1] * rows_in[v]
    slice_grad = (shares[0] + shares[1]) + (shares[2] + shares[3])
    slice_grad = jnp.where(me_v.astype(f32) < lengths, slice_grad, 0.0)
    grad_out[...] = slice_grad
    grads_in[me_f] = slice_grad

    def grad_copy(d):
        return pltpu.make_async_remote_copy(
            src_ref=grad_out, dst_ref=grads_in.at[me_f], send_sem=grad_send.at[d], recv_sem=grad_recv.at[d],
            device_id=device(0, 0, d), device_id_type=MESH,
        )

    grad_copies = [grad_copy(d) for d in range(1, nf)]
    for copy in grad_copies:
        copy.start()

    own_lines = weights[pl.ds(pl.multiple_of(me_corner * SUB, SUB), SUB), :]
    own_grad = jnp.zeros((SUB, LANES), f32)
    token_weight = []
    for j in range(nc):
        value = jnp.sum(jnp.where(lane == me_row * SUB + sub, own_lines[j : j + 1], 0.0), axis=1, keepdims=True)
        own_grad = jnp.where(lane == j * cap_lanes + sub, value, own_grad)
        token_weight.append(value / jnp.maximum(trade[j, 3 * SUB : 4 * SUB, :], 1.0))
    own_grad = jnp.sum(own_grad, axis=0, keepdims=True)
    inner = jnp.sum(inner_table * own_grad, axis=1, keepdims=True)
    side_copy.wait()
    parts = []
    for j in range(nc):
        mask = when < trade[j, 3 * SUB : 4 * SUB, :][None]
        scaled = q_full[j].reshape(tok, SUB, LANES) * jnp.where(mask, token_weight[j][None], 0.0)
        parts.append(jnp.concatenate(two_terms(scaled.reshape(per_block, LANES)), axis=1))
    both = dot(one_hot[...], jnp.concatenate(parts, axis=0))
    clip_res[...] = key_inv[...] * (both[:, 0:LANES] + both[:, LANES:] - unit_keys[me_c] * inner)

    row_terms = jnp.where((sub < nc) & (lane < SUB), jnp.log(row_total), 0.0)
    col_terms = jnp.where((at[:, 0:1] & 7) == 0, jnp.log(col_total), 0.0)
    terms = 0.5 * jnp.sum(row_terms) + 0.5 * jnp.sum(col_terms)
    terms = terms - jnp.sum(positive * logits.reshape(4, SUB, LANES))
    loss_ref[...] = jnp.broadcast_to(terms / (nc * SUB), (1, 1))

    for copy in grad_copies:
        copy.wait()
    dot_tile = jnp.zeros((SUB, LANES), f32)
    for j in range(nc):
        dot_tile = dot_tile + qn[j] * grads_in[j]
    cap_inner = jnp.sum(dot_tile, axis=1, keepdims=True)
    for j in range(nc):
        cap_res[pl.ds(j, SUB, stride=nc), :] = cap_inv * (grads_in[j] - qn[j] * cap_inner)

    for sem in (1, 2):
        pltpu.make_async_copy(half_but_one, half_but_one, pick_send.at[sem]).wait()
    pltpu.make_async_copy(row_tiles, row_tiles, gather_send.at[1]).wait()
    pltpu.make_async_copy(other_clips, other_clips, rows_send).wait()
    pltpu.make_async_copy(other_scores, other_scores, score_send).wait()
    pltpu.make_async_copy(other_logits, other_logits, logit_send).wait()
    pltpu.make_async_copy(other_tiles, other_tiles, tile_send).wait()


def body(nc, nv, cap_tokens, clip_tokens, win_frame, win_patch, cap_lengths):
    block, _, width = cap_tokens.shape
    _, frames, patches, _ = clip_tokens.shape
    assert block == SUB and frames == 4 and width == nc * LANES and win_frame.shape == (SUB, nv, 1)
    rows = frames * patches
    per_block = nv * SUB
    caps = cap_tokens.reshape(SUB * nc, LANES)
    clips = clip_tokens.reshape(frames, patches, nc, LANES).transpose(1, 2, 0, 3).reshape(patches, nc * frames, LANES)
    vmem = pltpu.VMEM
    dma = pltpu.SemaphoreType.DMA
    scratch = [
        vmem((SUB * nc, LANES), f32),
        vmem((patches, nc * frames, LANES), f32),
        vmem((SUB, nv), jnp.int32),
        vmem((SUB, nv), jnp.int32),
        vmem((nc, SUB, LANES), f32),
        vmem((nc, 4 * SUB, LANES), f32),
        vmem((nc, 4 * SUB, LANES), f32),
        vmem((nc, nv // 2, 2, SUB, LANES), f32),
        vmem((per_block, LANES), f32),
        vmem((nc, rows, LANES), f32),
        vmem((nc, -(-rows // LANES) * LANES, LANES), f32),
        vmem((rows, LANES), f32),
        vmem((per_block, LANES), jnp.int32),
        vmem((per_block, LANES), f32),
        vmem((nv, SUB, LANES), f32),
        vmem((nc * nc, SUB, LANES), f32),
        vmem((nc * nv // 4, LANES), f32),
        vmem((4 * SUB, LANES), f32),
        vmem((SUB, LANES), f32),
        vmem((1, LANES), f32),
        vmem((1, LANES), f32),
        vmem((4 * SUB, LANES), f32),
        vmem((LANES, 4 * SUB), f32),
        vmem((nc, SUB, LANES), f32),
        vmem((SUB, LANES), f32),
        vmem((LANES, nc * per_block), bf16),
        vmem((LANES, 2 * LANES), bf16),
        vmem((nc * per_block, LANES), bf16),
        vmem((rows, nc * per_block), bf16),
        vmem((1, SUB), jnp.int32),
        dma((5,)),
        dma((nc,)), dma((nc,)), dma((nc,)), dma((nc,)),
        dma((3,)), dma((3,)), dma((3,)), dma((3,)),
        dma((nc,)), dma((nc,)),
        dma, dma, dma, dma, dma, dma, dma, dma,
        dma((nc,)), dma((nc,)),
    ]
    hbm = pl.BlockSpec(memory_space=pl.ANY)
    near = pl.BlockSpec(memory_space=pltpu.VMEM)
    in_hbm = functools.partial(pltpu.with_memory_space_constraint, memory_space=pltpu.HBM)
    operands = (caps, clips, win_frame.reshape(SUB, nv), win_patch.reshape(SUB, nv), cap_lengths.reshape(1, SUB))
    shapes = ((1, 1), (SUB * nc, LANES), (rows, LANES))
    loss, cap_grad, clip_grad = pl.pallas_call(
        functools.partial(kernel, nc, nv, patches),
        out_shape=[vmem(shape, f32) for shape in shapes],
        in_specs=[hbm] * 5,
        out_specs=[near] * 3,
        scratch_shapes=scratch,
        compiler_params=pltpu.CompilerParams(
            collective_id=0, has_side_effects=True, vmem_limit_bytes=32 * 1024 * 1024
        ),
    )(*map(in_hbm, operands))
    clip_grad = clip_grad.reshape(patches, frames, LANES).transpose(1, 0, 2)[None]
    return loss.reshape(()), cap_grad.reshape(SUB, 1, width), clip_grad


def solution(mesh):
    placed = (
        P("cap", "clip", None),
        P("clip", "frame", None, None),
        P("cap", None, "clip"),
        P("cap", None, "clip"),
        P("cap"),
    )
    assert mesh.shape["cap"] == mesh.shape["frame"]
    return jax.shard_map(
        functools.partial(body, mesh.shape["cap"], mesh.shape["clip"]),
        mesh=mesh,
        in_specs=placed,
        out_specs=(P(), P("cap", "clip", None), P("clip", "frame", None, "cap")),
        check_vma=False,
    )
```
